128 devices in a mesh: pipe: 2 (over y_lo), shard: 4 (over y_hi, core), rep: 16 (over z, x).
Axes of the slice: x: 4, y: 4 (y_hi: 2, y_lo: 2; y = y_hi * 2 + y_lo), z: 4, core: 2. Of those that a mesh axis runs over, the one named last changes fastest.
Arguments:
- images: bfloat16 [256, 196, 512], P(('shard', 'rep')), may hold values from -6 to 6
- cotangent: bfloat16 [256, 196, 512], P(('shard', 'rep')), may hold values from -6 to 6
- micro_order: int32 [64, 4], P(('shard', 'rep')), may hold values from 0 to 3, each once within a row
- region_ids: int32 [196], replicated, may hold values from 0 to 3
- rel_index: int32 [49, 49], replicated, may hold values from 0 to 168
- qkv_weight: bfloat16 [2, 512, 1536], P('pipe', 'shard'), may hold values from -0.25 to 0.25
- proj_weight: bfloat16 [2, 512, 512], P('pipe', 'shard'), may hold values from -0.5 to 0.5
- up_weight: bfloat16 [2, 512, 2048], P('pipe', 'shard'), may hold values from -0.25 to 0.25
- down_weight: bfloat16 [2, 2048, 512], P('pipe', 'shard'), may hold values from -0.125 to 0.125
- bias_table: bfloat16 [2, 169, 16], P('pipe', None, 'shard'), may hold values from -4 to 4
- norm_gains: bfloat16 [2, 2, 512], P('pipe', None, 'shard'), may hold values from 0.5 to 1.5
- offsets: bfloat16 [2, 6, 512], P('pipe', None, 'shard'), may hold values from -2 to 2
- hidden_bias: bfloat16 [2, 2048], P('pipe', 'shard'), may hold values from -2 to 2
Outputs:
- layer_outputs: bfloat16 [2, 256, 196, 512], P('pipe', ('shard', 'rep'))
- input_grads: float32 [2, 256, 196, 512], P('pipe', ('shard', 'rep'))
- qkv_grad: float32 [2, 512, 1536], P('pipe', 'shard')
- proj_grad: float32 [2, 512, 512], P('pipe', 'shard')
- up_grad: float32 [2, 512, 2048], P('pipe', 'shard')
- down_grad: float32 [2, 2048, 512], P('pipe', 'shard')
- table_grad: float32 [2, 169, 16], P('pipe', None, 'shard')
- gains_grad: float32 [2, 2, 512], P('pipe', None, 'shard')
- offsets_grad: float32 [2, 6, 512], P('pipe', None, 'shard')
- hidden_grad: float32 [2, 2048], P('pipe', 'shard')
The draws below stay inside these ranges and needn't reach their ends.
Inputs may be any that keep to these rules, and one draw needn't show every extreme that they name: `micro_order`: each row names every one of its group's 4 images once.
All inputs are finite; a program needn't handle non-finite values.
Results may differ from the reference program's by a relative error of at most 0.024.
Values may be sent and summed in bfloat16 or wider, within the bound.
A program may use at most 192 MiB of HBM per device.

```python
import jax
import jax.numpy as jnp
from jax import lax

D = 512
HEADS = 16
HEAD = 32
FF = 2048
SIDE = 14
WIN = 7
SHIFT = 3
TOK_IMG = 196
WTOK = 49
NWIN = 4
RELS = 169
POOL = 4
GROUPS = 64
IMAGES = 256


def touch_ends(entries, own_key, low, largest):
    longest = entries.shape.index(max(entries.shape))
    spots = []
    for shift in (0, 1):
        where = [jax.random.randint(jax.random.fold_in(own_key, axis), (), 0, length) for axis, length in enumerate(entries.shape)]
        where[longest] = (where[longest] + shift) % entries.shape[longest]
        spots.append(tuple(where))
    return entries.at[spots[0]].set(low).at[spots[1]].set(largest)


def level_of(rng, shape, pieces, low, largest):
    level = 1.0
    for dim, shards_of in pieces:
        heights = jax.random.uniform(jax.random.fold_in(jax.random.fold_in(rng, 6), dim), (shards_of,), jnp.float32, low / len(pieces), largest / len(pieces))
        level = level * jnp.repeat(jnp.exp(heights), shape[dim] // shards_of).reshape((-1,) + (1,) * (len(shape) - 1 - dim))
    return level


def noise(rng, dims, width, reach, pieces=(), kind=jnp.bfloat16):
    values = jax.random.normal(rng, dims, jnp.float32) * width
    if len(pieces) > 0:
        values = level_of(rng, dims, pieces, -0.22, 0.18) * values
    return jnp.clip(values, min=-reach, max=reach).astype(kind)


def setup_inputs(seed: int = 0) -> dict:
    seeds = jax.random.split(jax.random.key(seed), 14)
    return {
        "images": noise(seeds[0], (IMAGES, TOK_IMG, D), 1.0, 6.0, ((0, 64),)),
        "cotangent": noise(seeds[1], (IMAGES, TOK_IMG, D), 1.0, 6.0, ((0, 64),)),
        "micro_order": jax.vmap(lambda own: jax.random.permutation(own, POOL))(jax.random.split(seeds[2], GROUPS)).reshape((GROUPS, POOL)).astype(jnp.int32),
        "region_ids": touch_ends(jax.random.randint(seeds[3], (TOK_IMG,), 0, 4), jax.random.fold_in(seeds[3], 1), 0, 3).astype(jnp.int32),
        "rel_index": touch_ends(jax.random.randint(seeds[4], (WTOK, WTOK), 0, RELS), jax.random.fold_in(seeds[4], 1), 0, RELS - 1).astype(jnp.int32),
        "qkv_weight": noise(seeds[5], (2, D, 3 * D), D ** -0.5, 0.25, ((0, 2), (1, 4))),
        "proj_weight": noise(seeds[6], (2, D, D), (D // 4) ** -0.5, 0.5, ((0, 2), (1, 4))),
        "up_weight": noise(seeds[7], (2, D, FF), D ** -0.5, 0.25, ((0, 2), (1, 4))),
        "down_weight": noise(seeds[8], (2, FF, D), FF ** -0.5, 0.125, ((0, 2), (1, 4))),
        "bias_table": noise(seeds[9], (2, RELS, HEADS), 1.0, 4.0, ((0, 2), (2, 4))),
        "norm_gains": jnp.clip(1.0 + 0.1 * jax.random.normal(seeds[10], (2, 2, D), jnp.float32), 0.5, 1.5).astype(jnp.bfloat16),
        "offsets": noise(seeds[11], (2, 6, D), 0.3, 2.0, ((0, 2), (2, 4))),
        "hidden_bias": noise(seeds[12], (2, FF), 0.3, 2.0, ((0, 2), (1, 4))),
    }


exact_precision = lax.Precision.HIGHEST

@jax.custom_vjp
def reduced_precision(v):
    return lax.optimization_barrier(v.astype(jnp.bfloat16)).astype(jnp.float32)

@jax.custom_vjp
def reduced_backward(v):
    return v

def low_keep(v):
    return (reduced_precision(v), None)

def low_pass(kept, grad):
    return (grad,)

def back_keep(v):
    return (v, None)

def back_low(kept, grad):
    return (reduced_precision(grad),)
reduced_precision.defvjp(low_keep, low_pass)
reduced_backward.defvjp(back_keep, back_low)

def layer_norm(tensor, gain_scale, offset):
    average = lax.optimization_barrier(jnp.mean(tensor, -1, keepdims=True))
    centred = tensor - average
    variance = lax.optimization_barrier(jnp.mean(centred * centred, -1, keepdims=True))
    return centred * lax.rsqrt(variance + 1e-05) * gain_scale + offset

def roll_grid(tensor, amount):
    batch_size, model_width = (tensor.shape[0], tensor.shape[2])
    grid = tensor.reshape(batch_size, SIDE, SIDE, model_width)
    grid = jnp.roll(grid, (amount, amount), (1, 2))
    return grid.reshape(batch_size, SIDE * SIDE, model_width)

def to_windows(tensor):
    batch_size, model_width = (tensor.shape[0], tensor.shape[2])
    grid = tensor.reshape(batch_size, SIDE // WIN, WIN, SIDE // WIN, WIN, model_width)
    grid = grid.transpose(0, 1, 3, 2, 4, 5)
    return grid.reshape(-1, WIN * WIN, model_width)

def from_windows(window_blocks, batch_size):
    model_width = window_blocks.shape[2]
    grid = window_blocks.reshape(batch_size, SIDE // WIN, SIDE // WIN, WIN, WIN, model_width)
    grid = grid.transpose(0, 1, 3, 2, 4, 5)
    return grid.reshape(batch_size, SIDE * SIDE, model_width)

def swin_layer(inputs, params, shift_by, mask_add, relative):
    query_key_value_weight, output_projection_weight, w_up, w_down, table, gains, offset_numbers, hidden_bias = params
    batch_size, model_width = (inputs.shape[0], inputs.shape[2])
    normed = reduced_precision(layer_norm(inputs, gains[0], offset_numbers[0]))
    window_blocks = to_windows(roll_grid(normed, -shift_by))
    bias_entries = jnp.concatenate([offset_numbers[2], jnp.zeros((model_width,), jnp.float32), offset_numbers[3]])
    projected_output = reduced_precision(reduced_backward(jnp.einsum('ngs,sa->nga', window_blocks, query_key_value_weight, precision=exact_precision) + bias_entries))
    split_heads = projected_output.reshape(-1, WTOK, 3, HEADS, HEAD)
    queries, key_heads, values = (split_heads[:, :, 0], split_heads[:, :, 1], split_heads[:, :, 2])
    scores = jnp.einsum('bqhe,bkhe->bhqk', queries, key_heads, precision=exact_precision) * HEAD ** (-0.5)
    rel_bias = jnp.take(table, relative, axis=0).reshape(WTOK, WTOK, HEADS).transpose(2, 0, 1)
    scores = scores.reshape(batch_size, NWIN, HEADS, WTOK, WTOK) + mask_add[None, :, None] + rel_bias[None, None]
    scores = reduced_backward(scores.reshape(-1, HEADS, WTOK, WTOK))
    highest = lax.optimization_barrier(jnp.max(scores, -1, keepdims=True))
    exponent = jnp.exp(scores - highest)
    attn_prob = reduced_precision(exponent / lax.optimization_barrier(jnp.sum(exponent, -1, keepdims=True)))
    attended_values = jnp.einsum('bhqk,bkhe->bqhe', attn_prob, values, precision=exact_precision)
    attended_values = reduced_precision(reduced_backward(attended_values.reshape(-1, WTOK, model_width)))
    branch_output = reduced_backward(jnp.einsum('ngs,sa->nga', attended_values, output_projection_weight, precision=exact_precision) + offset_numbers[4])
    mixed_sum = inputs + roll_grid(from_windows(branch_output, batch_size), shift_by)
    second_norm = reduced_precision(layer_norm(mixed_sum, gains[1], offset_numbers[1]))
    hidden = reduced_backward(jnp.einsum('btd,df->btf', second_norm, w_up, precision=exact_precision) + hidden_bias)
    active = reduced_precision(jax.nn.gelu(hidden, approximate=False))
    mlp_out = reduced_backward(jnp.einsum('btf,fd->btd', active, w_down, precision=exact_precision) + offset_numbers[5])
    return reduced_backward(reduced_precision(mixed_sum + mlp_out))

def reference(images, cotangent, micro_order, region_ids, rel_index, qkv_weight, proj_weight, up_weight, down_weight, bias_table, norm_gains, offsets, hidden_bias):
    params = tuple((w.astype(jnp.float32) for w in (qkv_weight, proj_weight, up_weight, down_weight, bias_table, norm_gains, offsets, hidden_bias)))
    regions = to_windows(region_ids.reshape(1, TOK_IMG, 1))[:, :, 0]
    masked = jnp.where(regions[:, :, None] == regions[:, None, :], 0.0, -1000000000.0).astype(jnp.float32)
    no_mask = jnp.zeros_like(masked)
    relative = rel_index.reshape(-1)
    pictures = images.astype(jnp.float32).reshape(GROUPS, POOL, TOK_IMG, D)
    cotangents = cotangent.astype(jnp.float32).reshape(GROUPS, POOL, TOK_IMG, D)

    def group_step(totals, group_item):
        picture, target, slot_order = group_item

        def forward(picture, weights, probe_zero):
            first_layer = tuple((w[0] for w in weights))
            second_layer = tuple((w[1] for w in weights))
            inner_out = swin_layer(jnp.take(picture, slot_order, axis=0), first_layer, 0, no_mask, relative) + probe_zero
            outer_out = swin_layer(inner_out, second_layer, SHIFT, masked, relative)
            return (outer_out, inner_out)
        probe_zero = jnp.zeros((POOL, TOK_IMG, D), jnp.float32)
        outer_out, pull_back, inner_out = jax.vjp(forward, picture, params, probe_zero, has_aux=True)
        d_picture, d_weights, d_probe = pull_back(target)
        totals = jax.tree.map(lambda summed, addend: summed + addend, totals, d_weights)
        return (totals, (inner_out, outer_out, d_picture, d_probe))
    zero_init = jax.tree.map(jnp.zeros_like, params)
    totals, (inner_all, outer_all, d_pictures, d_probes) = lax.scan(group_step, zero_init, (pictures, cotangents, micro_order))
    layer_outputs = jnp.stack([inner_all.reshape(IMAGES, TOK_IMG, D), outer_all.reshape(IMAGES, TOK_IMG, D)]).astype(jnp.bfloat16)
    input_grads = jnp.stack([d_pictures.reshape(IMAGES, TOK_IMG, D), d_probes.reshape(IMAGES, TOK_IMG, D)])
    return (layer_outputs, input_grads, totals[0], totals[1], totals[2], totals[3], totals[4], totals[5], totals[6], totals[7])
```

```python
import functools
import math

import jax
import jax.numpy as jnp
import numpy as np
from jax import lax
from jax.experimental import pallas as pl
from jax.experimental.pallas import tpu as pltpu
from jax.sharding import PartitionSpec as P

SIDE = 14
WIN = 7
SHIFT = 3
D = 512
FF = 2048
HEAD = 32
TOK = SIDE * SIDE
WTOK = WIN * WIN
WPAD = 56
PAIR = 2 * WPAD
IMG_ROWS = 4 * WPAD
IMGS = 2
ROWS = IMGS * IMG_ROWS
PAIRS = ROWS // PAIR
KEYS = 128
KROWS = ROWS + KEYS - PAIR
OUT_ROWS = 208
RELS_PAD = 256
QKV0, PROJ0, UP0, DOWN0, PACKED = 0, 1536, 2048, 4096, 6144
CHUNK = 256
SCALE = HEAD ** (-0.5)
BLOCKED = -1e30
VMEM_LIMIT = 60 * 1024 * 1024
BF16 = jnp.bfloat16
F32 = jnp.float32


def window_places(shift):
    place = np.zeros((TOK,), np.int64)
    for wr in range(2):
        for wc in range(2):
            for i in range(WIN):
                for j in range(WIN):
                    a = (wr * WIN + i + shift) % SIDE
                    b = (wc * WIN + j + shift) % SIDE
                    place[a * SIDE + b] = (wr * 2 + wc) * WPAD + i * WIN + j
    return place


def order_matrix(shift):
    matrix = np.zeros((IMG_ROWS, TOK), np.float32)
    matrix[window_places(shift), np.arange(TOK)] = 1.0
    return matrix


def back_matrix(shift):
    matrix = np.zeros((OUT_ROWS, IMG_ROWS), np.float32)
    matrix[:TOK] = order_matrix(shift).T
    return matrix


def turn_matrix(from_shift, to_shift):
    return order_matrix(to_shift) @ order_matrix(from_shift).T


def dot(a, b, dims=((1,), (0,))):
    return lax.dot_general(a, b, (dims, ((), ())), preferred_element_type=F32)


def normalised(x):
    mean = jnp.mean(x, -1, keepdims=True)
    centred = x - mean
    rstd = lax.rsqrt(jnp.mean(centred * centred, -1, keepdims=True) + 1e-5)
    return centred * rstd, rstd


def head_masks(rows):
    lane = lax.broadcasted_iota(jnp.int32, (rows, 128), 1) // HEAD
    return [lane == h for h in range(4)]


def spread_heads(block, masks):
    zero = jnp.zeros_like(block)
    return jnp.concatenate([jnp.where(m, block, zero) for m in masks], axis=0)


def join_heads(stacked, masks):
    total = None
    for h, m in enumerate(masks):
        part = jnp.where(m, stacked[h * PAIR : (h + 1) * PAIR], 0.0)
        total = part if total is None else total + part
    return total


def probabilities(q4, k, rel_ref, mask_ref, i, g):
    s = dot(q4, k, ((1,), (1,))) * SCALE
    bias = rel_ref[pl.ds(g * 4, 4)].astype(F32) + mask_ref[lax.rem(i, 2)][None]
    s = s + bias.reshape(4 * PAIR, KEYS)
    e = jnp.exp(s - jnp.max(s, -1, keepdims=True))
    return e / jnp.sum(e, -1, keepdims=True)


def down_chunk(w_ref, c):
    row = pl.multiple_of((c // 2) * 128, 128)
    col = pl.multiple_of(DOWN0 + (c % 2) * 1024, 128)
    first = w_ref[pl.ds(row, 128), pl.ds(col, D)]
    second = w_ref[pl.ds(row, 128), pl.ds(col + D, D)]
    return jnp.concatenate([first, second], axis=0)


def forward_kernel(
    turned, x_ref, w_ref, small_ref, qbias_ref, hbias_ref, rel_ref, mask_ref, back_ref, turn_ref,
    qkv_ref, o_ref, r_ref, act_ref, slope_ref, out_ref, *rest
):
    if turned:
        next_ref, low_ref, acc_ref = rest
    else:
        low_ref, acc_ref = rest
    x = x_ref[...].astype(F32)
    n1, _ = normalised(x)
    low_ref[...] = (n1 * small_ref[0:1] + small_ref[2:3]).astype(BF16)
    qkv_ref[ROWS:, :] = jnp.zeros((KROWS - ROWS, 3 * D), BF16)

    def qkv_step(n, _):
        cols = pl.ds(pl.multiple_of(n * CHUNK, CHUNK), CHUNK)
        part = dot(low_ref[...], w_ref[:, cols]) + qbias_ref[:, cols]
        qkv_ref[0:ROWS, cols] = part.astype(BF16)
        return 0

    lax.fori_loop(0, 3 * D // CHUNK, qkv_step, 0)
    masks = head_masks(PAIR)

    def attend(i, _):
        rows = pl.ds(pl.multiple_of(i * PAIR, 16), PAIR)
        keys = pl.ds(pl.multiple_of(i * PAIR, 16), KEYS)
        for g in range(4):
            q = qkv_ref[rows, g * 128 : (g + 1) * 128]
            k = qkv_ref[keys, D + g * 128 : D + (g + 1) * 128]
            v = qkv_ref[keys, 2 * D + g * 128 : 2 * D + (g + 1) * 128]
            p = probabilities(spread_heads(q, masks), k, rel_ref, mask_ref, i, g)
            o4 = dot(p.astype(BF16), v)
            o_ref[rows, g * 128 : (g + 1) * 128] = join_heads(o4, masks).astype(BF16)
        return 0

    lax.fori_loop(0, PAIRS, attend, 0)
    for n in range(D // CHUNK):
        cols = slice(n * CHUNK, (n + 1) * CHUNK)
        part = dot(o_ref[...], w_ref[:, PROJ0 + n * CHUNK : PROJ0 + (n + 1) * CHUNK])
        r_ref[:, cols] = x_ref[:, cols].astype(F32) + part + small_ref[6:7, cols]
    r = r_ref[...]
    n2, _ = normalised(r)
    low_ref[...] = (n2 * small_ref[1:2] + small_ref[3:4]).astype(BF16)
    acc_ref[...] = r + small_ref[7:8]

    def mlp(c, _):
        cols = pl.ds(pl.multiple_of(c * CHUNK, CHUNK), CHUNK)
        up = w_ref[:, pl.ds(pl.multiple_of(UP0 + c * CHUNK, CHUNK), CHUNK)]
        hid = dot(low_ref[...], up) + hbias_ref[:, cols]
        cdf = 0.5 * (1.0 + lax.erf(hid * math.sqrt(0.5)))
        act = (hid * cdf).astype(BF16)
        act_ref[:, cols] = act
        density = jnp.exp(-0.5 * hid * hid) * (1.0 / math.sqrt(2.0 * math.pi))
        slope_ref[:, cols] = (cdf + hid * density).astype(BF16)
        acc_ref[...] += dot(act, down_chunk(w_ref, c))
        return 0

    lax.fori_loop(0, FF // CHUNK, mlp, 0)
    y = acc_ref[...].astype(BF16)
    for b in range(IMGS):
        own = y[b * IMG_ROWS : (b + 1) * IMG_ROWS]
        out_ref[b] = dot(back_ref[...], own).astype(BF16)
        if turned:
            next_ref[b * IMG_ROWS : (b + 1) * IMG_ROWS] = dot(turn_ref[...], own).astype(BF16)


def backward_kernel(
    turned, dy_ref, x_ref, qkv_ref, o_ref, r_ref, act_ref, slope_ref, w_ref, small_ref, rel_ref,
    mask_ref, back_ref, turn_ref, g_ref, gsmall_ref, ghidden_ref, gbias_ref, out_ref, *rest
):
    if turned:
        next_ref, low_ref, turned_ref, dhid_ref, du_ref, dqkv_ref, do_ref = rest
    else:
        low_ref, turned_ref, dhid_ref, du_ref, dqkv_ref, do_ref = rest
    n2, rstd2 = normalised(r_ref[...])
    turned_ref[...] = (n2 * small_ref[1:2] + small_ref[3:4]).T.astype(BF16)
    du_ref[...] = jnp.zeros_like(du_ref)

    def mlp(c, _):
        cols = pl.ds(pl.multiple_of(c * CHUNK, CHUNK), CHUNK)
        up_cols = pl.ds(pl.multiple_of(UP0 + c * CHUNK, CHUNK), CHUNK)
        dy = dy_ref[...]
        dact = dot(dy, down_chunk(w_ref, c), ((1,), (1,)))
        dhid = (dact * slope_ref[:, cols].astype(F32)).astype(BF16)
        ghidden_ref[:, cols] = jnp.sum(dhid.astype(F32), 0, keepdims=True)
        down = dot(act_ref[:, cols], dy, ((0,), (0,))).astype(BF16)
        row = pl.multiple_of((c // 2) * 128, 128)
        col = pl.multiple_of(DOWN0 + (c % 2) * 1024, 128)
        g_ref[pl.ds(row, 128), pl.ds(col, D)] = down[:128]
        g_ref[pl.ds(row, 128), pl.ds(col + D, D)] = down[128:]
        g_ref[:, up_cols] = dot(turned_ref[...], dhid).astype(BF16)
        du_ref[...] += dot(dhid, w_ref[:, up_cols], ((1,), (1,)))
        return 0

    lax.fori_loop(0, FF // CHUNK, mlp, 0)
    dy = dy_ref[...].astype(F32)
    du2 = du_ref[...]
    n2, rstd2 = normalised(r_ref[...])
    z = du2 * small_ref[1:2]
    zm = jnp.mean(z, -1, keepdims=True)
    zn = jnp.mean(z * n2, -1, keepdims=True)
    dr = dy + rstd2 * (z - zm - n2 * zn)
    db = dr.astype(BF16)
    low_ref[...] = db
    gsmall_ref[1:2] = jnp.sum(du2 * n2, 0, keepdims=True)
    gsmall_ref[3:4] = jnp.sum(du2, 0, keepdims=True)
    gsmall_ref[6:7] = jnp.sum(db.astype(F32), 0, keepdims=True)
    gsmall_ref[7:8] = jnp.sum(dy, 0, keepdims=True)
    du_ref[...] = dr
    turned_ref[...] = o_ref[...].astype(F32).T.astype(BF16)
    for n in range(D // CHUNK):
        cols = slice(n * CHUNK, (n + 1) * CHUNK)
        g_ref[:, PROJ0 + n * CHUNK : PROJ0 + (n + 1) * CHUNK] = dot(
            turned_ref[...], low_ref[:, cols]
        ).astype(BF16)
        rows_of = w_ref[n * CHUNK : (n + 1) * CHUNK, PROJ0 : PROJ0 + D]
        do_ref[:, cols] = dot(low_ref[...], rows_of, ((1,), (1,))).astype(BF16)
    gbias_ref[...] = jnp.zeros_like(gbias_ref)
    masks = head_masks(PAIR)

    def attend(i, _):
        rows = pl.ds(pl.multiple_of(i * PAIR, 16), PAIR)
        keys = pl.ds(pl.multiple_of(i * PAIR, 16), KEYS)
        for g in range(4):
            here = slice(g * 128, (g + 1) * 128)
            k = qkv_ref[keys, D + g * 128 : D + (g + 1) * 128]
            v = qkv_ref[keys, 2 * D + g * 128 : 2 * D + (g + 1) * 128]
            q4 = spread_heads(qkv_ref[rows, here], masks)
            do4 = spread_heads(do_ref[rows, here], masks)
            p = probabilities(q4, k, rel_ref, mask_ref, i, g)
            dp = dot(do4, v, ((1,), (1,)))
            ds = (p * (dp - jnp.sum(dp * p, -1, keepdims=True))).astype(BF16)
            gbias_ref[g * 4 : (g + 1) * 4] += ds.astype(F32).reshape(4, PAIR, KEYS)
            dq = join_heads(dot(ds, k), masks) * SCALE
            dk = dot(ds, q4, ((0,), (0,))) * SCALE
            dv = dot(p.astype(BF16), do4, ((0,), (0,)))
            dqkv_ref[rows, here] = dq.astype(BF16)
            dqkv_ref[rows, D + g * 128 : D + (g + 1) * 128] = dk[:PAIR].astype(BF16)
            dqkv_ref[rows, 2 * D + g * 128 : 2 * D + (g + 1) * 128] = dv[:PAIR].astype(BF16)
        return 0

    lax.fori_loop(0, PAIRS, attend, 0)
    n1, rstd1 = normalised(x_ref[...].astype(F32))
    turned_ref[...] = (n1 * small_ref[0:1] + small_ref[2:3]).T.astype(BF16)

    def qkv_step(n, _):
        cols = pl.ds(pl.multiple_of(n * CHUNK, CHUNK), CHUNK)
        g_ref[:, cols] = dot(turned_ref[...], dqkv_ref[:, cols]).astype(BF16)
        return 0

    lax.fori_loop(0, 3 * D // CHUNK, qkv_step, 0)
    gsmall_ref[4:5] = jnp.sum(dqkv_ref[:, 0:D].astype(F32), 0, keepdims=True)
    gsmall_ref[5:6] = jnp.sum(dqkv_ref[:, 2 * D : 3 * D].astype(F32), 0, keepdims=True)
    du = dot(dqkv_ref[...], w_ref[:, QKV0 : QKV0 + 3 * D], ((1,), (1,)))
    n1, rstd1 = normalised(x_ref[...].astype(F32))
    gsmall_ref[0:1] = jnp.sum(du * n1, 0, keepdims=True)
    gsmall_ref[2:3] = jnp.sum(du, 0, keepdims=True)
    z = du * small_ref[0:1]
    zm = jnp.mean(z, -1, keepdims=True)
    zn = jnp.mean(z * n1, -1, keepdims=True)
    dx = (du_ref[...] + rstd1 * (z - zm - n1 * zn)).astype(BF16)
    for b in range(IMGS):
        own = dx[b * IMG_ROWS : (b + 1) * IMG_ROWS]
        out_ref[b] = dot(back_ref[...], own).astype(BF16)
        if turned:
            next_ref[b * IMG_ROWS : (b + 1) * IMG_ROWS] = dot(turn_ref[...], own).astype(BF16)


def shaped(shape, dtype):
    return jax.ShapeDtypeStruct(shape, dtype)


def whole(shape):
    return pl.BlockSpec(shape, lambda *_: (0,) * len(shape))


def packed_block(layer):
    return pl.BlockSpec((D, PACKED), lambda *_: (layer, 0))


def run_forward(layer, turned, x, packed, small, qbias, hbias, rel, mask, back, turn):
    saved = [
        shaped((KROWS, 3 * D), BF16),
        shaped((ROWS, D), BF16),
        shaped((ROWS, D), F32),
        shaped((ROWS, FF), BF16),
        shaped((ROWS, FF), BF16),
        shaped((IMGS, OUT_ROWS, D), BF16),
    ]
    if turned:
        saved.append(shaped((ROWS, D), BF16))
    operands = (x, packed, small, qbias, hbias, rel, mask, back, turn)
    specs = [whole(a.shape) for a in operands]
    specs[1] = packed_block(layer)
    return pl.pallas_call(
        functools.partial(forward_kernel, turned),
        grid=(1,),
        out_shape=saved,
        in_specs=specs,
        out_specs=[whole(a.shape) for a in saved],
        scratch_shapes=[pltpu.VMEM((ROWS, D), BF16), pltpu.VMEM((ROWS, D), F32)],
        compiler_params=pltpu.CompilerParams(vmem_limit_bytes=VMEM_LIMIT),
        cost_estimate=pl.CostEstimate(
            flops=2 * ROWS * D * PACKED, bytes_accessed=16 << 20, transcendentals=2 * ROWS * FF
        ),
        name="forward_layer",
    )(*operands)


def run_backward(layer, turned, dy, x, saved, packed, small, rel, mask, back, turn):
    results = [
        shaped((D, PACKED), BF16),
        shaped((8, D), F32),
        shaped((1, FF), F32),
        shaped((16, PAIR, KEYS), F32),
        shaped((IMGS, OUT_ROWS, D), BF16),
    ]
    if turned:
        results.append(shaped((ROWS, D), BF16))
    operands = (dy, x, *saved, packed, small, rel, mask, back, turn)
    specs = [whole(a.shape) for a in operands]
    specs[7] = packed_block(layer)
    return pl.pallas_call(
        functools.partial(backward_kernel, turned),
        grid=(1,),
        out_shape=results,
        in_specs=specs,
        out_specs=[whole(a.shape) for a in results],
        scratch_shapes=[
            pltpu.VMEM((ROWS, D), BF16),
            pltpu.VMEM((D, ROWS), BF16),
            pltpu.VMEM((ROWS, CHUNK), BF16),
            pltpu.VMEM((ROWS, D), F32),
            pltpu.VMEM((ROWS, 3 * D), BF16),
            pltpu.VMEM((ROWS, D), BF16),
        ],
        compiler_params=pltpu.CompilerParams(vmem_limit_bytes=VMEM_LIMIT),
        cost_estimate=pl.CostEstimate(
            flops=4 * ROWS * D * PACKED, bytes_accessed=24 << 20, transcendentals=ROWS * FF
        ),
        name="backward_layer",
    )(*operands)


def block_pair(blocks, fill):
    lead = blocks.shape[:-3]
    none = [(0, 0)] * len(lead)
    pad_rows = [(0, WPAD - WTOK)]
    first = jnp.pad(blocks[..., 0, :, :], none + pad_rows + [(0, KEYS - WTOK)], constant_values=fill)
    second = jnp.pad(
        blocks[..., 1, :, :], none + pad_rows + [(WPAD, KEYS - WTOK - WPAD)], constant_values=fill
    )
    return jnp.concatenate([first, second], axis=-2)


def on_device(
    images, cotangent, micro_order, region_ids, rel_index, qkv_weight, proj_weight, up_weight,
    down_weight, bias_table, norm_gains, offsets, hidden_bias,
):
    section = lax.axis_index("pipe")
    first_section = section == 0
    both = ("pipe", "shard")
    shards = lax.axis_size("shard")

    mine = jnp.concatenate(
        [qkv_weight[0], proj_weight[0], up_weight[0]]
        + [down_weight[0, k * 128 : (k + 1) * 128] for k in range(4)],
        axis=1,
    )
    packed = lax.all_gather(mine, both, axis=0, tiled=True)
    table_rows = bias_table.shape[1]
    table = jnp.pad(bias_table[0].T, ((0, 0), (0, RELS_PAD - table_rows))).reshape(8, 128)
    tiny = jnp.concatenate(
        [norm_gains[0], offsets[0], hidden_bias[0].reshape(4, 128), table, jnp.zeros((12, 128), BF16)]
    )
    tiny = lax.all_gather(tiny, both, axis=0).reshape(2, shards, 32, 128)
    small = tiny[:, :, :8].transpose(0, 2, 1, 3).reshape(2, 8, D).astype(F32)
    hbias = tiny[:, :, 8:12].reshape(2, 1, FF).astype(F32)
    tables = tiny[:, :, 12:20].reshape(2 * 16, RELS_PAD)
    qbias = jnp.concatenate([small[:, 4:5], jnp.zeros((2, 1, D), F32), small[:, 5:6]], axis=2)

    inside = np.zeros((2, WTOK, WTOK), np.int32)
    rel_pair = block_pair(jnp.broadcast_to(rel_index, inside.shape), -1)
    one_hot = (
        lax.broadcasted_iota(jnp.int32, (RELS_PAD, PAIR * KEYS), 0) == rel_pair.reshape(1, -1)
    ).astype(BF16)
    rel = jnp.dot(tables, one_hot, preferred_element_type=F32).astype(BF16)
    rel = rel.reshape(2, 16, PAIR, KEYS)
    places = window_places(0)
    win_tokens = np.zeros((4, WTOK), np.int64)
    win_tokens[places // WPAD, places % WPAD] = np.arange(TOK)
    regions = region_ids.reshape(2, WIN, 2, WIN).transpose(0, 2, 1, 3).reshape(2, 2, WTOK)
    apart = jnp.where(regions[..., :, None] == regions[..., None, :], 0.0, -1e9).astype(F32)
    mask1 = block_pair(apart, BLOCKED)
    mask0 = block_pair(jnp.zeros((2, 2, WTOK, WTOK), F32), BLOCKED)

    slot_order = micro_order[0]
    first_slot = section * IMGS
    own_slots = lax.dynamic_slice(slot_order, (first_slot,), (IMGS,))
    order0 = jnp.asarray(order_matrix(0), BF16)
    order1 = jnp.asarray(order_matrix(SHIFT), BF16)
    back0 = jnp.asarray(back_matrix(0), BF16)
    back1 = jnp.asarray(back_matrix(SHIFT), BF16)
    turn01 = jnp.asarray(turn_matrix(0, SHIFT), BF16)
    turn10 = jnp.asarray(turn_matrix(SHIFT, 0), BF16)
    pictures = jnp.take(images, own_slots, axis=0)
    x0 = jnp.einsum("rt,btd->brd", order0, pictures, preferred_element_type=F32).astype(BF16)
    x0 = x0.reshape(ROWS, D)
    target = lax.dynamic_slice(cotangent, (first_slot, 0, 0), (IMGS, TOK, D))
    dy1 = jnp.einsum("rt,btd->brd", order1, target, preferred_element_type=F32).astype(BF16)
    dy1 = dy1.reshape(ROWS, D)

    *saved0, y0, x1 = run_forward(
        0, True, x0, packed, small[0], qbias[0], hbias[0], rel[0], mask0, back0, turn01
    )
    *saved1, y1 = run_forward(
        1, False, x1, packed, small[1], qbias[1], hbias[1], rel[1], mask1, back1, turn10
    )
    swap = [(0, 1), (1, 0)]
    y_keep = jnp.where(first_section, y0, y1)
    y_come = lax.ppermute(jnp.where(first_section, y1, y0), "pipe", swap)

    g1, gsmall1, ghidden1, gbias1, dx1, dy0 = run_backward(
        1, True, dy1, x1, saved1, packed, small[1], rel[1], mask1, back1, turn10
    )
    g0, gsmall0, ghidden0, gbias0, dx0 = run_backward(
        0, False, dy0, x0, saved0, packed, small[0], rel[0], mask0, back0, turn01
    )
    dx_keep = jnp.where(first_section, dx0, dx1)
    dx_come = lax.ppermute(jnp.where(first_section, dx1, dx0), "pipe", swap)

    def in_slots(keep, come):
        low = jnp.where(first_section, keep, come)
        high = jnp.where(first_section, come, keep)
        return jnp.concatenate([low, high], axis=0)[:, :TOK]

    layer_out = in_slots(y_keep, y_come)
    dx_slots = in_slots(dx_keep, dx_come)
    slots = jnp.arange(2 * IMGS, dtype=jnp.int32)
    inverse = jnp.sum(jnp.where(slot_order[:, None] == slots[None, :], slots[:, None], 0), axis=0)
    picks = jnp.where(first_section, inverse, slots)
    input_grad = jnp.take(dx_slots, picks, axis=0).astype(F32)

    everyone = ("pipe", "shard", "rep")
    big = jnp.concatenate([g0, g1], axis=0)
    share = reduce_big(big)
    gsmall = jnp.stack([gsmall0, gsmall1])
    ghidden = jnp.stack([ghidden0, ghidden1]).reshape(2, FF)
    gbias = jnp.stack([gbias0, gbias1])
    gbias = gbias[:, :, :WTOK, :WTOK] + gbias[:, :, WPAD : WPAD + WTOK, WPAD : WPAD + WTOK]
    rel_hot = (
        rel_index.reshape(1, -1) == jnp.arange(table_rows, dtype=jnp.int32)[:, None]
    ).astype(F32)
    gtable = jnp.einsum(
        "nr,hr->nh", rel_hot, gbias.reshape(32, WTOK * WTOK), precision=lax.Precision.HIGHEST
    )
    flat = jnp.concatenate([gsmall.reshape(-1), ghidden.reshape(-1), gtable.reshape(-1)])
    flat = lax.psum(flat, everyone)
    shard = lax.axis_index("shard")
    cut_small, cut_hidden = 2 * 8 * D, 2 * 8 * D + 2 * FF
    gsmall = lax.dynamic_slice(
        flat[:cut_small].reshape(2, 8, D), (section, 0, shard * 128), (1, 8, 128)
    )
    ghidden = lax.dynamic_slice(flat[cut_small:cut_hidden].reshape(2, FF), (section, shard * D), (1, D))
    gtable = lax.dynamic_slice(
        flat[cut_hidden:].reshape(table_rows, 32), (0, section * 16 + shard * 4), (table_rows, 4)
    )[None]
    down = jnp.concatenate(
        [share[:, DOWN0 + k * D : DOWN0 + (k + 1) * D] for k in range(4)], axis=0
    )
    return (
        layer_out[None],
        input_grad[None],
        share[None, :, QKV0:PROJ0].astype(F32),
        share[None, :, PROJ0:UP0].astype(F32),
        share[None, :, UP0:DOWN0].astype(F32),
        down[None].astype(F32),
        gtable,
        gsmall[:, 0:2],
        gsmall[:, 2:8],
        ghidden,
    )


def reduce_big(big):
    share = lax.psum_scatter(big, ("pipe", "shard"), scatter_dimension=0, tiled=True)
    return lax.psum(share, "rep")


def solution(mesh):
    rows = P(("shard", "rep"), None, None)
    split = P("pipe", "shard", None)
    lanes = P("pipe", None, "shard")
    return jax.shard_map(
        on_device,
        mesh=mesh,
        in_specs=(
            rows, rows, P(("shard", "rep"), None), P(), P(),
            split, split, split, split, lanes, lanes, lanes, P("pipe", "shard"),
        ),
        out_specs=(
            P("pipe", ("shard", "rep"), None, None), P("pipe", ("shard", "rep"), None, None),
            split, split, split, split, lanes, lanes, lanes, P("pipe", "shard"),
        ),
        check_vma=False,
    )
```

```python
import functools
import math

import jax
import jax.numpy as jnp
import numpy as np
from jax import lax
from jax.experimental import pallas as pl
from jax.experimental.pallas import tpu as pltpu
from jax.sharding import PartitionSpec as P

SIDE = 14
WIN = 7
SHIFT = 3
D = 512
FF = 2048
HEAD = 32
TOK = SIDE * SIDE
WTOK = WIN * WIN
WPAD = 56
PAIR = 2 * WPAD
IMG_ROWS = 4 * WPAD
IMGS = 2
ROWS = IMGS * IMG_ROWS
PAIRS = ROWS // PAIR
KEYS = 128
KROWS = ROWS + KEYS - PAIR
OUT_ROWS = 208
RELS_PAD = 256
QKV0, PROJ0, UP0, DOWN0, PACKED = 0, 1536, 2048, 4096, 6144
CHUNK = 256
SCALE = HEAD ** (-0.5)
BLOCKED = -1e30
VMEM_LIMIT = 64 * 1024 * 1024 - 1024
BF16 = jnp.bfloat16
F32 = jnp.float32


def window_places(shift):
    place = np.zeros((TOK,), np.int64)
    for wr in range(2):
        for wc in range(2):
            for i in range(WIN):
                for j in range(WIN):
                    a = (wr * WIN + i + shift) % SIDE
                    b = (wc * WIN + j + shift) % SIDE
                    place[a * SIDE + b] = (wr * 2 + wc) * WPAD + i * WIN + j
    return place


def order_matrix(shift):
    matrix = np.zeros((IMG_ROWS, TOK), np.float32)
    matrix[window_places(shift), np.arange(TOK)] = 1.0
    return matrix


def back_matrix(shift):
    matrix = np.zeros((OUT_ROWS, IMG_ROWS), np.float32)
    matrix[:TOK] = order_matrix(shift).T
    return matrix


def turn_matrix(from_shift, to_shift):
    return order_matrix(to_shift) @ order_matrix(from_shift).T


def dot(a, b, dims=((1,), (0,))):
    return lax.dot_general(a, b, (dims, ((), ())), preferred_element_type=F32)


def normalised(x):
    mean = jnp.mean(x, -1, keepdims=True)
    centred = x - mean
    rstd = lax.rsqrt(jnp.mean(centred * centred, -1, keepdims=True) + 1e-5)
    return centred * rstd, rstd


def head_masks(rows):
    lane = lax.broadcasted_iota(jnp.int32, (rows, 128), 1) // HEAD
    return [lane == h for h in range(4)]


def spread_heads(block, masks):
    zero = jnp.zeros_like(block)
    return jnp.concatenate([jnp.where(m, block, zero) for m in masks], axis=0)


def join_heads(stacked, masks):
    total = None
    for h, m in enumerate(masks):
        part = jnp.where(m, stacked[h * PAIR : (h + 1) * PAIR], 0.0)
        total = part if total is None else total + part
    return total


def probabilities(q4, k, rel_ref, mask_ref, i, g):
    s = dot(q4, k, ((1,), (1,))) * SCALE
    bias = rel_ref[pl.ds(g * 4, 4)].astype(F32) + mask_ref[lax.rem(i, 2)][None]
    s = s + bias.reshape(4 * PAIR, KEYS)
    e = jnp.exp(s - jnp.max(s, -1, keepdims=True))
    return e / jnp.sum(e, -1, keepdims=True)


def down_chunk(w_ref, c):
    row = pl.multiple_of((c // 2) * 128, 128)
    col = pl.multiple_of(DOWN0 + (c % 2) * 1024, 128)
    first = w_ref[pl.ds(row, 128), pl.ds(col, D)]
    second = w_ref[pl.ds(row, 128), pl.ds(col + D, D)]
    return jnp.concatenate([first, second], axis=0)


MESH = pl.DeviceIdType.MESH
STREAMS = ((2048, 4096, "xz"), (4096, 6144, "zx"), (0, 1024, "xz"), (1024, 2048, "zx"))
LATE = (2, 3)
TINY_ROWS = 24
SMALL_ROWS = 24


def here():
    pipe, shard, rep = lax.axis_index("pipe"), lax.axis_index("shard"), lax.axis_index("rep")
    return {"y": (shard // 2) * 2 + pipe, "core": shard % 2, "z": rep // 4, "x": rep % 4}


def device_at(place):
    return {
        "pipe": place["y"] % 2,
        "shard": (place["y"] // 2) * 2 + place["core"],
        "rep": place["z"] * 4 + place["x"],
    }


def moved(place, axis, steps):
    size = 2 if axis == "core" else 4
    return {**place, axis: (place[axis] + steps) % size}


def block_index(y, core):
    return (y % 2) * 4 + (y // 2) * 2 + core


class Copies:
    def __init__(self, send_sem, recv_sem):
        self.send_sem, self.recv_sem, self.count, self.started = send_sem, recv_sem, 0, []

    def start(self, src, dst, place):
        copy = pltpu.make_async_remote_copy(
            src_ref=src, dst_ref=dst, send_sem=self.send_sem.at[self.count],
            recv_sem=self.recv_sem.at[self.count], device_id=device_at(place), device_id_type=MESH,
        )
        copy.start()
        self.count += 1
        self.started.append(copy)
        return copy

    def finish(self):
        for copy in self.started:
            copy.wait_send()


def greet(places):
    barrier = pltpu.get_barrier_semaphore()
    for place in places:
        pl.semaphore_signal(barrier, inc=1, device_id=device_at(place), device_id_type=MESH)
    pl.semaphore_wait(barrier, len(places))


def nothing():
    pass


def forward_body(params, saved, x_ref, low_ref, acc_ref, after_attend=nothing):
    w_ref, small_ref, qbias_ref, hbias_ref, rel_ref, mask_ref = params
    qkv_ref, o_ref, r_ref, act_ref, slope_ref = saved
    n1, _ = normalised(x_ref[...].astype(F32))
    low_ref[...] = (n1 * small_ref[0:1] + small_ref[2:3]).astype(BF16)
    qkv_ref[ROWS:, :] = jnp.zeros((KROWS - ROWS, 3 * D), BF16)

    def qkv_step(n, _):
        cols = pl.ds(pl.multiple_of(n * CHUNK, CHUNK), CHUNK)
        part = dot(low_ref[...], w_ref[:, cols]) + qbias_ref[:, cols]
        qkv_ref[0:ROWS, cols] = part.astype(BF16)
        return 0

    lax.fori_loop(0, 3 * D // CHUNK, qkv_step, 0)
    masks = head_masks(PAIR)

    def attend(i, _):
        rows = pl.ds(pl.multiple_of(i * PAIR, 16), PAIR)
        keys = pl.ds(pl.multiple_of(i * PAIR, 16), KEYS)
        for g in range(4):
            q = qkv_ref[rows, g * 128 : (g + 1) * 128]
            k = qkv_ref[keys, D + g * 128 : D + (g + 1) * 128]
            v = qkv_ref[keys, 2 * D + g * 128 : 2 * D + (g + 1) * 128]
            p = probabilities(spread_heads(q, masks), k, rel_ref, mask_ref, i, g)
            o4 = dot(p.astype(BF16), v)
            o_ref[rows, g * 128 : (g + 1) * 128] = join_heads(o4, masks).astype(BF16)
        return 0

    lax.fori_loop(0, PAIRS, attend, 0)
    after_attend()
    for n in range(D // CHUNK):
        cols = slice(n * CHUNK, (n + 1) * CHUNK)
        part = dot(o_ref[...], w_ref[:, PROJ0 + n * CHUNK : PROJ0 + (n + 1) * CHUNK])
        r_ref[:, cols] = x_ref[:, cols].astype(F32) + part + small_ref[6:7, cols]
    r = r_ref[...]
    n2, _ = normalised(r)
    low_ref[...] = (n2 * small_ref[1:2] + small_ref[3:4]).astype(BF16)
    acc_ref[...] = r + small_ref[7:8]

    def mlp(c, _):
        cols = pl.ds(pl.multiple_of(c * CHUNK, CHUNK), CHUNK)
        up = w_ref[:, pl.ds(pl.multiple_of(UP0 + c * CHUNK, CHUNK), CHUNK)]
        hid = dot(low_ref[...], up) + hbias_ref[:, cols]
        cdf = 0.5 * (1.0 + lax.erf(hid * math.sqrt(0.5)))
        act = (hid * cdf).astype(BF16)
        act_ref[:, cols] = act
        density = jnp.exp(-0.5 * hid * hid) * (1.0 / math.sqrt(2.0 * math.pi))
        slope_ref[:, cols] = (cdf + hid * density).astype(BF16)
        acc_ref[...] += dot(act, down_chunk(w_ref, c))
        return 0

    lax.fori_loop(0, FF // CHUNK, mlp, 0)
    return acc_ref[...].astype(BF16)


def backward_body(
    params, saved, x_ref, dy_ref, results, scratch,
    in_mlp=nothing, after_mlp=nothing, before_attend=nothing, after_attend=nothing, after_weights=nothing,
):
    w_ref, small_ref, _, _, rel_ref, mask_ref = params
    qkv_ref, o_ref, r_ref, act_ref, slope_ref = saved
    g_ref, gsmall_ref, ghidden_ref, gbias_ref = results
    low_ref, turned_ref, du_ref, dqkv_ref, do_ref = scratch

    def put(cols, value):
        for b in range(4):
            g_ref[b // 2, b % 2, :, cols] = value[b * 128 : (b + 1) * 128]

    n2, rstd2 = normalised(r_ref[...])
    turned_ref[...] = (n2 * small_ref[1:2] + small_ref[3:4]).T.astype(BF16)
    du_ref[...] = jnp.zeros_like(du_ref)

    def mlp(c, _):
        cols = pl.ds(pl.multiple_of(c * CHUNK, CHUNK), CHUNK)
        up_cols = pl.ds(pl.multiple_of(UP0 + c * CHUNK, CHUNK), CHUNK)
        dy = dy_ref[...]
        dact = dot(dy, down_chunk(w_ref, c), ((1,), (1,)))
        dhid = (dact * slope_ref[:, cols].astype(F32)).astype(BF16)
        ghidden_ref[:, cols] = jnp.sum(dhid.astype(F32), 0, keepdims=True)
        down = dot(act_ref[:, cols], dy, ((0,), (0,))).astype(BF16)
        block = c // 2
        col = pl.multiple_of(DOWN0 + (c % 2) * 1024, 128)
        g_ref[block // 2, block % 2, :, pl.ds(col, D)] = down[:128]
        g_ref[block // 2, block % 2, :, pl.ds(col + D, D)] = down[128:]
        put(up_cols, dot(turned_ref[...], dhid).astype(BF16))
        du_ref[...] += dot(dhid, w_ref[:, up_cols], ((1,), (1,)))
        return 0

    lax.fori_loop(0, FF // CHUNK // 2, mlp, 0)
    in_mlp()
    lax.fori_loop(FF // CHUNK // 2, FF // CHUNK, mlp, 0)
    after_mlp()
    dy = dy_ref[...].astype(F32)
    du2 = du_ref[...]
    n2, rstd2 = normalised(r_ref[...])
    z = du2 * small_ref[1:2]
    zm = jnp.mean(z, -1, keepdims=True)
    zn = jnp.mean(z * n2, -1, keepdims=True)
    dr = dy + rstd2 * (z - zm - n2 * zn)
    db = dr.astype(BF16)
    low_ref[...] = db
    gsmall_ref[1:2] = jnp.sum(du2 * n2, 0, keepdims=True)
    gsmall_ref[3:4] = jnp.sum(du2, 0, keepdims=True)
    gsmall_ref[6:7] = jnp.sum(db.astype(F32), 0, keepdims=True)
    gsmall_ref[7:8] = jnp.sum(dy, 0, keepdims=True)
    du_ref[...] = dr
    turned_ref[...] = o_ref[...].astype(F32).T.astype(BF16)
    for n in range(D // CHUNK):
        cols = slice(n * CHUNK, (n + 1) * CHUNK)
        put(
            slice(PROJ0 + n * CHUNK, PROJ0 + (n + 1) * CHUNK),
            dot(turned_ref[...], low_ref[:, cols]).astype(BF16),
        )
        rows_of = w_ref[n * CHUNK : (n + 1) * CHUNK, PROJ0 : PROJ0 + D]
        do_ref[:, cols] = dot(low_ref[...], rows_of, ((1,), (1,))).astype(BF16)
    before_attend()
    gbias_ref[...] = jnp.zeros_like(gbias_ref)
    masks = head_masks(PAIR)

    def attend(i, _):
        rows = pl.ds(pl.multiple_of(i * PAIR, 16), PAIR)
        keys = pl.ds(pl.multiple_of(i * PAIR, 16), KEYS)
        for g in range(4):
            here = slice(g * 128, (g + 1) * 128)
            k = qkv_ref[keys, D + g * 128 : D + (g + 1) * 128]
            v = qkv_ref[keys, 2 * D + g * 128 : 2 * D + (g + 1) * 128]
            q4 = spread_heads(qkv_ref[rows, here], masks)
            do4 = spread_heads(do_ref[rows, here], masks)
            p = probabilities(q4, k, rel_ref, mask_ref, i, g)
            dp = dot(do4, v, ((1,), (1,)))
            ds = (p * (dp - jnp.sum(dp * p, -1, keepdims=True))).astype(BF16)
            gbias_ref[g * 4 : (g + 1) * 4] += ds.astype(F32).reshape(4, PAIR, KEYS)
            dq = join_heads(dot(ds, k), masks) * SCALE
            dk = dot(ds, q4, ((0,), (0,))) * SCALE
            dv = dot(p.astype(BF16), do4, ((0,), (0,)))
            dqkv_ref[rows, here] = dq.astype(BF16)
            dqkv_ref[rows, D + g * 128 : D + (g + 1) * 128] = dk[:PAIR].astype(BF16)
            dqkv_ref[rows, 2 * D + g * 128 : 2 * D + (g + 1) * 128] = dv[:PAIR].astype(BF16)
        return 0

    lax.fori_loop(0, PAIRS, attend, 0)
    after_attend()
    n1, rstd1 = normalised(x_ref[...].astype(F32))
    turned_ref[...] = (n1 * small_ref[0:1] + small_ref[2:3]).T.astype(BF16)

    def qkv_step(n, _):
        cols = pl.ds(pl.multiple_of(n * CHUNK, CHUNK), CHUNK)
        put(cols, dot(turned_ref[...], dqkv_ref[:, cols]).astype(BF16))
        return 0

    lax.fori_loop(0, 3 * D // CHUNK, qkv_step, 0)
    after_weights()
    gsmall_ref[4:5] = jnp.sum(dqkv_ref[:, 0:D].astype(F32), 0, keepdims=True)
    gsmall_ref[5:6] = jnp.sum(dqkv_ref[:, 2 * D : 3 * D].astype(F32), 0, keepdims=True)
    du = dot(dqkv_ref[...], w_ref[:, QKV0 : QKV0 + 3 * D], ((1,), (1,)))
    n1, rstd1 = normalised(x_ref[...].astype(F32))
    gsmall_ref[0:1] = jnp.sum(du * n1, 0, keepdims=True)
    gsmall_ref[2:3] = jnp.sum(du, 0, keepdims=True)
    z = du * small_ref[0:1]
    zm = jnp.mean(z, -1, keepdims=True)
    zn = jnp.mean(z * n1, -1, keepdims=True)
    return (du_ref[...] + rstd1 * (z - zm - n1 * zn)).astype(BF16)


def table_rows_of(tables_ref, places_ref, rel_ref):
    rel_ref[...] = jnp.zeros_like(rel_ref)
    entry = lax.broadcasted_iota(jnp.int32, (RELS_PAD, KEYS), 0)
    tables = tables_ref[...].astype(BF16)

    def rows(n, _):
        for step in range(WIN):
            i = n * WIN + step
            hot = jnp.where(entry == places_ref[pl.ds(i, 1), :], 1.0, 0.0).astype(BF16)
            values = dot(tables, hot)
            rel_ref[:, i, :] = values
            rel_ref[:, i + WPAD, :] = pltpu.roll(values, WPAD, 1)
        return 0

    lax.fori_loop(0, WIN, rows, 0)


def table_sums(gbias_ref, places_ref):
    second = gbias_ref[:, WPAD:PAIR].reshape(16 * WPAD, KEYS)
    gbias_ref[:, 0:WPAD] += pltpu.roll(second, KEYS - WPAD, 1).reshape(16, WPAD, KEYS)
    entry = lax.broadcasted_iota(jnp.int32, (RELS_PAD, KEYS), 0)

    def rows(n, total):
        parts = []
        for step in range(WIN):
            i = n * WIN + step
            values = gbias_ref[:, i, :]
            high = values.astype(BF16)
            low = (values - high.astype(F32)).astype(BF16)
            hot = jnp.where(entry == places_ref[pl.ds(i, 1), :], 1.0, 0.0).astype(BF16)
            parts.append(dot(jnp.concatenate([high, low], axis=0), hot, ((1,), (1,))))
        return total + sum(parts)

    total = lax.fori_loop(0, WIN, rows, jnp.zeros((32, RELS_PAD), F32))
    return total[0:16] + total[16:32]


COPIES = 192


def piece_of(region):
    rows, cols = region
    return (pl.ds(rows[0], rows[1]), pl.ds(cols[0], cols[1]))


def cut(region, axis, index):
    rows, cols = region
    if axis == "z":
        return ((pl.multiple_of(index * 32, 32), 32), cols)
    width = cols[1] // 4
    return (rows, (pl.multiple_of(cols[0] + index * width, 128), width))


def train_kernel(
    slots_ref, images_ref, cot_hbm, qkv_hbm, proj_hbm, up_hbm, down_hbm, tiny_ref, places_ref, mask_ref,
    order_ref, back_ref, turn_ref,
    y_hbm, dx_hbm, grad_hbm, sums_ref,
    w_ref, x_ref, qkv_ref, o_ref, r_ref, act_ref, slope_ref, g_ref, core_ref, land_a, land_b, land_y, fin_ref,
    rel_ref, gbias_ref, low_ref, turned_ref, du_ref, dqkv_ref, do_ref, dy_ref, cot_ref,
    y_ref, y_land, dx_ref, dx_land, tiny_land, tables_ref, small_ref, qbias_ref, hbias_ref,
    gsmall_ref, ghidden_ref, sums_in, sums_core, sums_own, sums_land,
    send_sem, recv_sem, local_sem, free_sem,
):
    me = here()
    pipe = me["y"] % 2
    copies = Copies(send_sem, recv_sem)
    partner = moved(me, "core", 1)
    peers = {axis: [moved(me, axis, k) for k in (1, 2, 3)] for axis in "yxz"}
    across = [moved(partner, "y", k) for k in (1, 2, 3)]

    def block_at(y):
        return pl.ds(pl.multiple_of(block_index(y, me["core"]) * 128, 128), 128)

    own = block_index(me["y"], me["core"])
    own_rows = block_at(me["y"])
    parts = [
        (qkv_hbm.at[0], QKV0, 3 * D), (proj_hbm.at[0], PROJ0, D), (up_hbm.at[0], UP0, FF),
    ] + [(down_hbm.at[0, k * 128 : (k + 1) * 128], DOWN0 + k * D, D) for k in range(4)]
    locals_in = []
    for n, (src, lo, width) in enumerate(parts):
        local = pltpu.make_async_copy(src, w_ref.at[own_rows, lo : lo + width], local_sem.at[n])
        local.start()
        locals_in.append(local)
    cot_copy = pltpu.make_async_copy(cot_hbm.at[pl.ds(pipe * IMGS, IMGS)], cot_ref, local_sem.at[7])
    cot_copy.start()
    greet([partner] + across + [place for axis in "yxz" for place in peers[axis]])
    for local in locals_in:
        local.wait()

    width = PACKED // 8

    def quarter(half, part, index):
        return (half * 64, 64), (pl.multiple_of(part * (PACKED // 2) + index * width, 128), width)

    def weight_piece(y, region):
        (r0, nr), cols = region
        start = pl.multiple_of(block_index(y, me["core"]) * 128 + r0, 64)
        return w_ref.at[pl.ds(start, nr), pl.ds(*cols)]

    first_base = copies.count
    for half in range(2):
        for k in (1, 2, 3):
            for part, axis in enumerate("xz"):
                piece = weight_piece(me["y"], quarter(half, part, me[axis]))
                copies.start(piece, piece, moved(me, "y", k))
    own_block = w_ref.at[own_rows]
    to_partner = {"own": copies.start(own_block, own_block, partner)}
    tiny_copies = [
        copies.start(tiny_ref, tiny_land.at[own], place) for place in [partner] + peers["y"] + across
    ]
    tiny_land[own] = tiny_ref[...]

    for b in range(IMGS):
        picture = images_ref[slots_ref[pipe * IMGS + b]]
        x_ref[0, b * IMG_ROWS : (b + 1) * IMG_ROWS] = dot(order_ref[0], picture).astype(BF16)
    cot_copy.wait()
    for b in range(IMGS):
        dy_ref[b * IMG_ROWS : (b + 1) * IMG_ROWS] = dot(order_ref[1], cot_ref[b]).astype(BF16)
    for copy in tiny_copies:
        copy.wait_recv()
    qbias_ref[...] = jnp.zeros_like(qbias_ref)
    for layer in range(2):
        for shard in range(4):
            rows = tiny_land[layer * 4 + shard]
            small_ref[layer, :, shard * 128 : (shard + 1) * 128] = rows[0:8, 0:128]
            for j in range(4):
                at = shard * 512 + j * 128
                hbias_ref[layer, :, at : at + 128] = rows[8 + j : 9 + j, 0:128]
                head = layer * 16 + shard * 4 + j
                tables_ref[head : head + 1] = rows[16 + j : 17 + j]
        qbias_ref[layer, :, 0:D] = small_ref[layer, 4:5]
        qbias_ref[layer, :, 2 * D : 3 * D] = small_ref[layer, 5:6]

    steps = [2 - pipe, 1 + 2 * pipe, 3 - pipe]
    seconds = {}

    def pass_on(slot):
        y = (me["y"] - steps[slot] + 4) % 4
        for half in range(2):
            for part, axis in enumerate("xz"):
                piece = weight_piece(y, quarter(half, part, me[axis]))
                index = first_base + half * 6 + (steps[slot] - 1) * 2 + part
                pltpu.make_async_remote_copy(
                    src_ref=piece, dst_ref=piece, send_sem=send_sem.at[index],
                    recv_sem=recv_sem.at[index], device_id=device_at(partner), device_id_type=MESH,
                ).wait_recv()
                for j in (1, 3, 2):
                    seconds[slot, half, part, j] = copies.start(piece, piece, moved(me, axis, j))

    def hand_over(slot):
        y = (me["y"] - steps[slot] + 4) % 4
        for half in range(2):
            for part in range(2):
                for j in (1, 3, 2):
                    seconds[slot, half, part, j].wait_recv()
            piece = weight_piece(y, ((half * 64, 64), (0, PACKED)))
            to_partner[slot, half] = copies.start(piece, piece, partner)

    pass_on(0)
    pass_on(1)
    table_rows_of(tables_ref, places_ref, rel_ref)
    hand_over(0)
    hand_over(1)
    pass_on(2)
    to_partner["own"].wait_recv()
    for slot in range(2):
        for half in range(2):
            to_partner[slot, half].wait_recv()

    def params(layer):
        return (
            w_ref.at[pl.ds(layer * D, D)], small_ref.at[layer], qbias_ref.at[layer], hbias_ref.at[layer],
            rel_ref.at[pl.ds(layer * 16, 16)], mask_ref.at[layer],
        )

    def saved(layer):
        return tuple(ref.at[layer] for ref in (qkv_ref, o_ref, r_ref, act_ref, slope_ref))

    def in_token_order(layer, value, out, turned):
        for b in range(IMGS):
            own_rows = value[b * IMG_ROWS : (b + 1) * IMG_ROWS]
            out[b] = dot(back_ref[layer], own_rows).astype(BF16)
            if turned is not None:
                turned[b * IMG_ROWS : (b + 1) * IMG_ROWS] = dot(turn_ref[layer], own_rows).astype(BF16)

    y0 = forward_body(params(0), saved(0), x_ref.at[0], low_ref, du_ref, lambda: hand_over(2))
    in_token_order(0, y0, y_ref.at[0], x_ref.at[1])
    for half in range(2):
        to_partner[2, half].wait_recv()
    y1 = forward_body(params(1), saved(1), x_ref.at[1], low_ref, du_ref)
    in_token_order(1, y1, y_ref.at[1], None)
    neighbour = {**me, "y": me["y"] + 1 - 2 * pipe}
    y_copy = copies.start(y_ref.at[1 - pipe], y_land, neighbour)
    keep_out = pltpu.make_async_copy(y_ref.at[pipe], y_hbm.at[pl.ds(pipe * IMGS, IMGS)], local_sem.at[0])
    keep_out.start()

    core_copies, sent, regions = {}, {}, {}

    def send_core(layer, streams):
        for t in streams:
            lo, hi, _ = STREAMS[t]
            core_copies[layer, t] = copies.start(
                g_ref.at[layer, :, 1 - me["core"], :, lo:hi], core_ref.at[:, :, lo:hi], partner
            )

    def add_core(layer, streams):
        for t in streams:
            lo, hi, _ = STREAMS[t]
            core_copies[layer, t].wait_recv()

            def one(n, _, lo=lo, hi=hi):
                half, rows = n // 4, pl.ds(pl.multiple_of((n % 4) * 32, 32), 32)
                mine = (layer, half, me["core"], rows, slice(lo, hi))
                total = g_ref[mine].astype(F32) + core_ref[half, rows, lo:hi].astype(F32)
                g_ref[mine] = total.astype(BF16)
                return 0

            lax.fori_loop(0, 8, one, 0)
            regions[layer, t] = ((0, 128), (lo, hi - lo))

    def send(layer, streams, stage):
        for t in streams:
            axis = STREAMS[t][2][stage]
            land = (land_a, land_b)[stage][t]
            region = regions[layer, t]
            sent[layer, t] = [
                copies.start(
                    g_ref.at[(layer, slice(None), me["core"]) + piece_of(cut(region, axis, (me[axis] + k) % 4))],
                    land.at[layer, k - 1], moved(me, axis, k),
                )
                for k in (1, 3, 2)
            ]
            regions[layer, t] = cut(region, axis, me[axis])

    def add(layer, streams, stage):
        for t in streams:
            for copy in sent[layer, t]:
                copy.wait_recv()
            land = (land_a, land_b)[stage][t]
            (r0, nr), cols = regions[layer, t]
            steps_of = nr // 32

            def one(n, _, land=land, r0=r0, cols=cols, steps_of=steps_of):
                half, row = n // steps_of, pl.multiple_of((n % steps_of) * 32, 32)
                at = (layer, half, me["core"], pl.ds(pl.multiple_of(r0 + row, 32), 32), pl.ds(*cols))
                total = g_ref[at].astype(F32)
                for k in range(3):
                    total = total + land[layer, k, half, pl.ds(row, 32), :].astype(F32)
                g_ref[at] = total.astype(BF16)
                return 0

            lax.fori_loop(0, 2 * steps_of, one, 0)

    def send_y(streams):
        for t in streams:
            piece = piece_of(regions[0, t])
            sent["y", t] = []
            for k in (1, 3, 2):
                to = (me["y"] + k) % 4
                sent["y", t].append(
                    copies.start(
                        g_ref.at[(to % 2, to // 2, me["core"]) + piece], land_y[t].at[k - 1], moved(me, "y", k)
                    )
                )

    def add_y(streams):
        for t in streams:
            for copy in sent["y", t]:
                copy.wait_recv()
            piece = piece_of(regions[0, t])
            total = g_ref[(pipe, me["y"] // 2, me["core"]) + piece].astype(F32)
            for k in range(3):
                total = total + land_y[t][k].astype(F32)
            fin_ref[piece] = total.astype(BF16)

    def spread(streams, level):
        for t in streams:
            if level == 1:
                for copy in sent["fin", t]:
                    copy.wait_recv()
            lo, hi, order = STREAMS[t]
            part = (hi - lo) // 4
            rows = pl.ds(pl.multiple_of(me["z"] * 32, 32), 32)
            cols = pl.ds(pl.multiple_of(lo + me["x"] * part, 128), part)
            if level == 1:
                if order[0] == "x":
                    cols = pl.ds(lo, hi - lo)
                else:
                    rows = pl.ds(0, 128)
            piece = fin_ref.at[rows, cols]
            sent["fin", t] = [copies.start(piece, piece, moved(me, order[level], k)) for k in (1, 3, 2)]

    late = LATE
    early = tuple(t for t in range(len(STREAMS)) if t not in late)

    def results(layer):
        return (g_ref.at[layer], gsmall_ref.at[layer], ghidden_ref.at[layer], gbias_ref.at[layer])

    scratch = (low_ref, turned_ref, du_ref, dqkv_ref, do_ref)

    def before_attend1():
        add_core(1, early)
        send(1, early, 0)

    dx1 = backward_body(
        params(1), saved(1), x_ref.at[1], dy_ref, results(1), scratch,
        after_mlp=lambda: send_core(1, early), before_attend=before_attend1,
        after_weights=lambda: send_core(1, late),
    )
    in_token_order(1, dx1, dx_ref.at[1], dy_ref)
    add_core(1, late)
    pl.semaphore_signal(free_sem, inc=1, device_id=device_at(partner), device_id_type=MESH)
    send(1, late, 0)

    def in_mlp0():
        add(1, early, 0)
        send(1, early, 1)

    def after_mlp0():
        pl.semaphore_wait(free_sem, 1)
        send_core(0, early)
        add(1, late, 0)
        send(1, late, 1)

    def before_attend0():
        add_core(0, early)
        send(0, early, 0)

    def after_weights0():
        send_core(0, late)
        add(1, early, 1)
        add(1, late, 1)

    dx0 = backward_body(
        params(0), saved(0), x_ref.at[0], dy_ref, results(0), scratch,
        in_mlp=in_mlp0, after_mlp=after_mlp0, before_attend=before_attend0, after_weights=after_weights0,
    )
    add_core(0, late)
    send(0, late, 0)
    in_token_order(0, dx0, dx_ref.at[0], None)
    dx_copy = copies.start(dx_ref.at[1 - pipe], dx_land, neighbour)
    dx_keep = pltpu.make_async_copy(dx_ref.at[pipe], dx_hbm.at[pl.ds(pipe * IMGS, IMGS)], local_sem.at[1])
    dx_keep.start()
    add(0, early, 0)
    send(0, early, 1)

    for layer in range(2):
        gtable = table_sums(gbias_ref.at[layer], places_ref)
        for shard in range(4):
            half, core = shard // 2, shard % 2
            y = half * 2 + layer
            sums_in[core, y] = jnp.zeros((SMALL_ROWS, RELS_PAD), F32)
            sums_in[core, y, 0:8, 0:128] = gsmall_ref[layer, :, shard * 128 : (shard + 1) * 128]
            for j in range(4):
                at = shard * 512 + j * 128
                sums_in[core, y, 8 + j : 9 + j, 0:128] = ghidden_ref[layer, :, at : at + 128]
            sums_in[core, y, 16:20] = gtable[shard * 4 : shard * 4 + 4]
    small_copy = copies.start(sums_in.at[1 - me["core"]], sums_core, partner)
    add(0, early, 1)
    send_y(early)
    add(0, late, 0)
    send(0, late, 1)
    small_copy.wait_recv()
    sums_own[0] = sums_in[me["core"]] + sums_core[...]
    small_sent = [
        copies.start(sums_own.at[0, (me["y"] + k) % 4], sums_land.at[0, k - 1], moved(me, "y", k))
        for k in (1, 3, 2)
    ]

    def add_small(stage):
        for copy in small_sent:
            copy.wait_recv()
        start = sums_own[0, me["y"]] if stage == 0 else sums_own[stage, 0]
        return start + sums_land[stage, 0] + sums_land[stage, 1] + sums_land[stage, 2]

    add_y(early)
    spread(early, 0)
    add(0, late, 1)
    send_y(late)
    for stage, axis in enumerate("xz", 1):
        sums_own[stage, 0] = add_small(stage - 1)
        small_sent = [
            copies.start(sums_own.at[stage, 0], sums_land.at[stage, k - 1], moved(me, axis, k))
            for k in (1, 3, 2)
        ]
        if stage == 1:
            spread(early, 1)
            add_y(late)
            spread(late, 0)
    spread(late, 1)
    sums_ref[...] = add_small(2)
    outs = []
    y_copy.wait_recv()
    dx_copy.wait_recv()
    for n, (src, dst) in enumerate(((y_land, y_hbm), (dx_land, dx_hbm)), 2):
        out = pltpu.make_async_copy(src, dst.at[pl.ds((1 - pipe) * IMGS, IMGS)], local_sem.at[n])
        out.start()
        outs.append(out)
    for t in early + late:
        for copy in sent["fin", t]:
            copy.wait_recv()
    grad_out = pltpu.make_async_copy(fin_ref, grad_hbm, local_sem.at[4])
    grad_out.start()
    for copy in [keep_out, dx_keep, grad_out] + outs:
        copy.wait()
    copies.finish()


def land_shapes(stage):
    shapes = []
    for lo, hi, order in STREAMS:
        done = order[: stage + 1]
        shape = (2, 3, 2, 32 if "z" in done else 128, (hi - lo) // (4 if "x" in done else 1))
        shapes.append(pltpu.VMEM(shape, BF16))
    return tuple(shapes)


def train(slots, images, cotangent, qkv, proj, up, down, tiny, places, mask, order, back, turn):
    anywhere = pl.BlockSpec(memory_space=pl.ANY)
    vmem = pl.BlockSpec(memory_space=pltpu.VMEM)
    tokens = (2 * IMGS, OUT_ROWS, D)
    half = (IMGS, OUT_ROWS, D)
    piece = (SMALL_ROWS, RELS_PAD)
    low = pltpu.VMEM((ROWS, D), BF16)
    return pl.pallas_call(
        train_kernel,
        out_shape=[
            jax.ShapeDtypeStruct(tokens, BF16), jax.ShapeDtypeStruct(tokens, BF16),
            jax.ShapeDtypeStruct((128, PACKED), BF16), jax.ShapeDtypeStruct(piece, F32),
        ],
        in_specs=[pl.BlockSpec(memory_space=pltpu.SMEM), vmem] + [anywhere] * 5 + [vmem] * 6,
        out_specs=[anywhere] * 3 + [vmem],
        scratch_shapes=[
            pltpu.VMEM((2 * D, PACKED), BF16),
            pltpu.VMEM((2, ROWS, D), BF16),
            pltpu.VMEM((2, KROWS, 3 * D), BF16),
            pltpu.VMEM((2, ROWS, D), BF16),
            pltpu.VMEM((2, ROWS, D), F32),
            pltpu.VMEM((2, ROWS, FF), BF16),
            pltpu.VMEM((2, ROWS, FF), BF16),
            pltpu.VMEM((2, 2, 2, 128, PACKED), BF16),
            pltpu.VMEM((2, 128, PACKED), BF16),
            land_shapes(0), land_shapes(1),
            tuple(pltpu.VMEM((3, 32, (hi - lo) // 4), BF16) for lo, hi, _ in STREAMS),
            pltpu.VMEM((128, PACKED), BF16),
            pltpu.VMEM((32, PAIR, KEYS), F32),
            pltpu.VMEM((2, 16, PAIR, KEYS), F32),
            low,
            pltpu.VMEM((D, ROWS), BF16),
            pltpu.VMEM((ROWS, D), F32),
            pltpu.VMEM((ROWS, 3 * D), BF16),
            low,
            low,
            pltpu.VMEM((IMGS, TOK, D), BF16),
            pltpu.VMEM((2,) + half, BF16),
            pltpu.VMEM(half, BF16),
            pltpu.VMEM((2,) + half, BF16),
            pltpu.VMEM(half, BF16),
            pltpu.VMEM((8, TINY_ROWS, RELS_PAD), F32),
            pltpu.VMEM((32, RELS_PAD), F32),
            pltpu.VMEM((2, 8, D), F32),
            pltpu.VMEM((2, 1, 3 * D), F32),
            pltpu.VMEM((2, 1, FF), F32),
            pltpu.VMEM((2, 8, D), F32),
            pltpu.VMEM((2, 1, FF), F32),
            pltpu.VMEM((2, 4) + piece, F32),
            pltpu.VMEM((4,) + piece, F32),
            pltpu.VMEM((3, 4) + piece, F32),
            pltpu.VMEM((3, 3) + piece, F32),
            pltpu.SemaphoreType.DMA((COPIES,)),
            pltpu.SemaphoreType.DMA((COPIES,)),
            pltpu.SemaphoreType.DMA((8,)),
            pltpu.SemaphoreType.REGULAR,
        ],
        compiler_params=pltpu.CompilerParams(
            collective_id=1, has_side_effects=True, vmem_limit_bytes=VMEM_LIMIT
        ),
        cost_estimate=pl.CostEstimate(
            flops=12 * ROWS * D * PACKED, bytes_accessed=16 << 20, transcendentals=6 * ROWS * FF
        ),
        name="train_layers",
    )(slots, images, cotangent, qkv, proj, up, down, tiny, places, mask, order, back, turn)


def block_pair(blocks, fill):
    lead = blocks.shape[:-3]
    none = [(0, 0)] * len(lead)
    pad_rows = [(0, WPAD - WTOK)]
    first = jnp.pad(blocks[..., 0, :, :], none + pad_rows + [(0, KEYS - WTOK)], constant_values=fill)
    second = jnp.pad(
        blocks[..., 1, :, :], none + pad_rows + [(WPAD, KEYS - WTOK - WPAD)], constant_values=fill
    )
    return jnp.concatenate([first, second], axis=-2)


def inside_blocks():
    rows, cols = np.arange(PAIR)[:, None] // WPAD, np.arange(KEYS)[None, :]
    return (cols // WPAD == rows) & (cols % WPAD < WTOK) & (cols < PAIR)


def on_device(
    images, cotangent, micro_order, region_ids, rel_index, qkv_weight, proj_weight, up_weight,
    down_weight, bias_table, norm_gains, offsets, hidden_bias,
):
    first_section = lax.axis_index("pipe") == 0
    table_rows = bias_table.shape[1]

    def lanes(block, rows):
        return jnp.pad(
            block.astype(F32), ((0, rows - block.shape[0]), (0, RELS_PAD - block.shape[1]))
        )

    tiny = jnp.concatenate(
        [
            lanes(jnp.concatenate([norm_gains[0], offsets[0]]), 8),
            lanes(hidden_bias[0].reshape(4, 128), 8),
            lanes(bias_table[0].T, 8),
        ]
    )
    places = jnp.pad(rel_index, ((0, WPAD - WTOK), (0, KEYS - WTOK)), constant_values=-1)
    regions = region_ids.reshape(2, WIN, 2, WIN).transpose(0, 2, 1, 3).reshape(2, 2, WTOK)
    regions = jnp.pad(regions, ((0, 0), (0, 0), (0, WPAD - WTOK))).reshape(2, PAIR)
    queries = regions[:, :, None]
    keys = jnp.pad(regions, ((0, 0), (0, KEYS - PAIR)))[:, None, :]
    inside = inside_blocks()
    mask0 = np.broadcast_to(np.where(inside, 0.0, BLOCKED), (2, PAIR, KEYS)).astype(np.float32)
    mask1 = jnp.where(inside[None], jnp.where(queries == keys, 0.0, -1e9), BLOCKED).astype(F32)
    mask = jnp.stack([jnp.asarray(mask0), mask1])
    order = jnp.asarray(np.stack([order_matrix(0), order_matrix(SHIFT)]), BF16)
    back = jnp.asarray(np.stack([back_matrix(0), back_matrix(SHIFT)]), BF16)
    turn = jnp.asarray(np.stack([turn_matrix(0, SHIFT), turn_matrix(SHIFT, 0)]), BF16)
    slot_order = micro_order[0]

    layer_out, dx_slots, share, sums = train(
        slot_order, images, cotangent, qkv_weight, proj_weight, up_weight, down_weight, tiny, places,
        mask, order, back, turn,
    )
    slots = jnp.arange(2 * IMGS, dtype=jnp.int32)
    inverse = jnp.sum(jnp.where(slot_order[:, None] == slots[None, :], slots[:, None], 0), axis=0)
    picks = jnp.where(first_section, inverse, slots)
    input_grad = jnp.take(dx_slots[:, :TOK], picks, axis=0).astype(F32)
    down = jnp.concatenate(
        [share[:, DOWN0 + k * D : DOWN0 + (k + 1) * D] for k in range(4)], axis=0
    )
    return (
        layer_out[None, :, :TOK],
        input_grad[None],
        share[None, :, QKV0:PROJ0].astype(F32),
        share[None, :, PROJ0:UP0].astype(F32),
        share[None, :, UP0:DOWN0].astype(F32),
        down[None].astype(F32),
        sums[16:20, :table_rows].T[None],
        sums[None, 0:2, 0:128],
        sums[None, 2:8, 0:128],
        sums[8:12, 0:128].reshape(1, D),
    )


def solution(mesh):
    rows = P(("shard", "rep"), None, None)
    split = P("pipe", "shard", None)
    lanes = P("pipe", None, "shard")
    return jax.shard_map(
        on_device,
        mesh=mesh,
        in_specs=(
            rows, rows, P(("shard", "rep"), None), P(), P(),
            split, split, split, split, lanes, lanes, lanes, P("pipe", "shard"),
        ),
        out_specs=(
            P("pipe", ("shard", "rep"), None, None), P("pipe", ("shard", "rep"), None, None),
            split, split, split, split, lanes, lanes, lanes, P("pipe", "shard"),
        ),
        check_vma=False,
    )
```

```python
import functools
import math

import jax
import jax.numpy as jnp
import numpy as np
from jax import lax
from jax.experimental import pallas as pl
from jax.experimental.pallas import tpu as pltpu
from jax.sharding import PartitionSpec as P

SIDE = 14
WIN = 7
SHIFT = 3
D = 512
FF = 2048
HEAD = 32
TOK = SIDE * SIDE
WTOK = WIN * WIN
WPAD = 56
PAIR = 2 * WPAD
IMG_ROWS = 4 * WPAD
IMGS = 2
ROWS = IMGS * IMG_ROWS
PAIRS = ROWS // PAIR
KEYS = 128
KROWS = ROWS + KEYS - PAIR
OUT_ROWS = 208
RELS_PAD = 256
QKV0, PROJ0, UP0, DOWN0, PACKED = 0, 1536, 2048, 4096, 6144
CHUNK = 256
SCALE = HEAD ** (-0.5)
BLOCKED = -1e30
VMEM_LIMIT = 64 * 1024 * 1024 - 1024
BF16 = jnp.bfloat16
F32 = jnp.float32


def window_places(shift):
    place = np.zeros((TOK,), np.int64)
    for wr in range(2):
        for wc in range(2):
            for i in range(WIN):
                for j in range(WIN):
                    a = (wr * WIN + i + shift) % SIDE
                    b = (wc * WIN + j + shift) % SIDE
                    place[a * SIDE + b] = (wr * 2 + wc) * WPAD + i * WIN + j
    return place


def order_matrix(shift):
    matrix = np.zeros((IMG_ROWS, TOK), np.float32)
    matrix[window_places(shift), np.arange(TOK)] = 1.0
    return matrix


def back_matrix(shift):
    matrix = np.zeros((OUT_ROWS, IMG_ROWS), np.float32)
    matrix[:TOK] = order_matrix(shift).T
    return matrix


def turn_matrix(from_shift, to_shift):
    return order_matrix(to_shift) @ order_matrix(from_shift).T


def dot(a, b, dims=((1,), (0,))):
    return lax.dot_general(a, b, (dims, ((), ())), preferred_element_type=F32)


def normalised(x):
    mean = jnp.mean(x, -1, keepdims=True)
    centred = x - mean
    rstd = lax.rsqrt(jnp.mean(centred * centred, -1, keepdims=True) + 1e-5)
    return centred * rstd, rstd


def head_masks(rows):
    lane = lax.broadcasted_iota(jnp.int32, (rows, 128), 1) // HEAD
    return [lane == h for h in range(4)]


def spread_heads(block, masks):
    zero = jnp.zeros_like(block)
    return jnp.concatenate([jnp.where(m, block, zero) for m in masks], axis=0)


def join_heads(stacked, masks):
    total = None
    for h, m in enumerate(masks):
        part = jnp.where(m, stacked[h * PAIR : (h + 1) * PAIR], 0.0)
        total = part if total is None else total + part
    return total


def probabilities(q4, k, rel_ref, mask_ref, i, g):
    s = dot(q4, k, ((1,), (1,))) * SCALE
    bias = rel_ref[pl.ds(g * 4, 4)].astype(F32) + mask_ref[lax.rem(i, 2)][None]
    s = s + bias.reshape(4 * PAIR, KEYS)
    e = jnp.exp(s - jnp.max(s, -1, keepdims=True))
    return e / jnp.sum(e, -1, keepdims=True)


def down_chunk(w_ref, c):
    row = pl.multiple_of((c // 2) * 128, 128)
    col = pl.multiple_of(DOWN0 + (c % 2) * 1024, 128)
    first = w_ref[pl.ds(row, 128), pl.ds(col, D)]
    second = w_ref[pl.ds(row, 128), pl.ds(col + D, D)]
    return jnp.concatenate([first, second], axis=0)


MESH = pl.DeviceIdType.MESH
STREAMS = ((1536, 4096, "xz"), (4096, 6144, "zx"), (0, 512, "xz"), (512, 1536, "zx"))
LATE = (2, 3)
TINY_ROWS = 24
SMALL_ROWS = 24


def here():
    pipe, shard, rep = lax.axis_index("pipe"), lax.axis_index("shard"), lax.axis_index("rep")
    return {"y": (shard // 2) * 2 + pipe, "core": shard % 2, "z": rep // 4, "x": rep % 4}


def device_at(place):
    return {
        "pipe": place["y"] % 2,
        "shard": (place["y"] // 2) * 2 + place["core"],
        "rep": place["z"] * 4 + place["x"],
    }


def moved(place, axis, steps):
    size = 2 if axis == "core" else 4
    return {**place, axis: (place[axis] + steps) % size}


def block_index(y, core):
    return (y % 2) * 4 + (y // 2) * 2 + core


class Copies:
    def __init__(self, send_sem, recv_sem):
        self.send_sem, self.recv_sem, self.count, self.started = send_sem, recv_sem, 0, []

    def start(self, src, dst, place):
        copy = pltpu.make_async_remote_copy(
            src_ref=src, dst_ref=dst, send_sem=self.send_sem.at[self.count],
            recv_sem=self.recv_sem.at[self.count], device_id=device_at(place), device_id_type=MESH,
        )
        copy.start()
        self.count += 1
        self.started.append(copy)
        return copy

    def finish(self):
        for copy in self.started:
            copy.wait_send()


def greet(places):
    barrier = pltpu.get_barrier_semaphore()
    for place in places:
        pl.semaphore_signal(barrier, inc=1, device_id=device_at(place), device_id_type=MESH)
    pl.semaphore_wait(barrier, len(places))


def nothing():
    pass


def forward_body(
    params, saved, x_ref, low_ref, acc_ref, after_qkv=nothing, after_attend=nothing, before_mlp=nothing
):
    w_ref, small_ref, qbias_ref, hbias_ref, rel_ref, mask_ref = params
    qkv_ref, o_ref, r_ref, act_ref, slope_ref = saved
    n1, _ = normalised(x_ref[...].astype(F32))
    low_ref[...] = (n1 * small_ref[0:1] + small_ref[2:3]).astype(BF16)
    qkv_ref[ROWS:, :] = jnp.zeros((KROWS - ROWS, 3 * D), BF16)

    def qkv_step(n, _):
        cols = pl.ds(pl.multiple_of(n * CHUNK, CHUNK), CHUNK)
        part = dot(low_ref[...], w_ref[:, cols]) + qbias_ref[:, cols]
        qkv_ref[0:ROWS, cols] = part.astype(BF16)
        return 0

    lax.fori_loop(0, 3 * D // CHUNK, qkv_step, 0)
    after_qkv()
    masks = head_masks(PAIR)

    def attend(i, _):
        rows = pl.ds(pl.multiple_of(i * PAIR, 16), PAIR)
        keys = pl.ds(pl.multiple_of(i * PAIR, 16), KEYS)
        for g in range(4):
            q = qkv_ref[rows, g * 128 : (g + 1) * 128]
            k = qkv_ref[keys, D + g * 128 : D + (g + 1) * 128]
            v = qkv_ref[keys, 2 * D + g * 128 : 2 * D + (g + 1) * 128]
            p = probabilities(spread_heads(q, masks), k, rel_ref, mask_ref, i, g)
            o4 = dot(p.astype(BF16), v)
            o_ref[rows, g * 128 : (g + 1) * 128] = join_heads(o4, masks).astype(BF16)
        return 0

    lax.fori_loop(0, PAIRS, attend, 0)
    after_attend()
    for n in range(D // CHUNK):
        cols = slice(n * CHUNK, (n + 1) * CHUNK)
        part = dot(o_ref[...], w_ref[:, PROJ0 + n * CHUNK : PROJ0 + (n + 1) * CHUNK])
        r_ref[:, cols] = x_ref[:, cols].astype(F32) + part + small_ref[6:7, cols]
    r = r_ref[...]
    n2, _ = normalised(r)
    low_ref[...] = (n2 * small_ref[1:2] + small_ref[3:4]).astype(BF16)
    acc_ref[...] = r + small_ref[7:8]
    before_mlp()

    def mlp(c, _):
        cols = pl.ds(pl.multiple_of(c * CHUNK, CHUNK), CHUNK)
        up = w_ref[:, pl.ds(pl.multiple_of(UP0 + c * CHUNK, CHUNK), CHUNK)]
        hid = dot(low_ref[...], up) + hbias_ref[:, cols]
        cdf = 0.5 * (1.0 + lax.erf(hid * math.sqrt(0.5)))
        act = (hid * cdf).astype(BF16)
        act_ref[:, cols] = act
        density = jnp.exp(-0.5 * hid * hid) * (1.0 / math.sqrt(2.0 * math.pi))
        slope_ref[:, cols] = (cdf + hid * density).astype(BF16)
        acc_ref[...] += dot(act, down_chunk(w_ref, c))
        return 0

    lax.fori_loop(0, FF // CHUNK, mlp, 0)
    return acc_ref[...].astype(BF16)


def backward_body(
    params, saved, x_ref, dy_ref, results, scratch,
    in_mlp=nothing, after_mlp=nothing, after_proj=nothing, before_attend=nothing, after_attend=nothing,
    after_weights=nothing,
):
    w_ref, small_ref, _, _, rel_ref, mask_ref = params
    qkv_ref, o_ref, r_ref, act_ref, slope_ref = saved
    g_ref, gsmall_ref, ghidden_ref, gbias_ref = results
    low_ref, turned_ref, du_ref, dqkv_ref, do_ref = scratch

    def put(cols, value):
        for b in range(4):
            g_ref[b // 2, b % 2, :, cols] = value[b * 128 : (b + 1) * 128]

    n2, rstd2 = normalised(r_ref[...])
    turned_ref[...] = (n2 * small_ref[1:2] + small_ref[3:4]).T.astype(BF16)
    du_ref[...] = jnp.zeros_like(du_ref)

    def mlp(c, _):
        cols = pl.ds(pl.multiple_of(c * CHUNK, CHUNK), CHUNK)
        up_cols = pl.ds(pl.multiple_of(UP0 + c * CHUNK, CHUNK), CHUNK)
        dy = dy_ref[...]
        dact = dot(dy, down_chunk(w_ref, c), ((1,), (1,)))
        dhid = (dact * slope_ref[:, cols].astype(F32)).astype(BF16)
        ghidden_ref[:, cols] = jnp.sum(dhid.astype(F32), 0, keepdims=True)
        down = dot(act_ref[:, cols], dy, ((0,), (0,))).astype(BF16)
        block = c // 2
        col = pl.multiple_of(DOWN0 + (c % 2) * 1024, 128)
        g_ref[block // 2, block % 2, :, pl.ds(col, D)] = down[:128]
        g_ref[block // 2, block % 2, :, pl.ds(col + D, D)] = down[128:]
        put(up_cols, dot(turned_ref[...], dhid).astype(BF16))
        du_ref[...] += dot(dhid, w_ref[:, up_cols], ((1,), (1,)))
        return 0

    lax.fori_loop(0, FF // CHUNK // 2, mlp, 0)
    in_mlp()
    lax.fori_loop(FF // CHUNK // 2, FF // CHUNK, mlp, 0)
    after_mlp()
    dy = dy_ref[...].astype(F32)
    du2 = du_ref[...]
    n2, rstd2 = normalised(r_ref[...])
    z = du2 * small_ref[1:2]
    zm = jnp.mean(z, -1, keepdims=True)
    zn = jnp.mean(z * n2, -1, keepdims=True)
    dr = dy + rstd2 * (z - zm - n2 * zn)
    db = dr.astype(BF16)
    low_ref[...] = db
    gsmall_ref[1:2] = jnp.sum(du2 * n2, 0, keepdims=True)
    gsmall_ref[3:4] = jnp.sum(du2, 0, keepdims=True)
    gsmall_ref[6:7] = jnp.sum(db.astype(F32), 0, keepdims=True)
    gsmall_ref[7:8] = jnp.sum(dy, 0, keepdims=True)
    du_ref[...] = dr
    turned_ref[...] = o_ref[...].astype(F32).T.astype(BF16)
    for n in range(D // CHUNK):
        cols = slice(n * CHUNK, (n + 1) * CHUNK)
        put(
            slice(PROJ0 + n * CHUNK, PROJ0 + (n + 1) * CHUNK),
            dot(turned_ref[...], low_ref[:, cols]).astype(BF16),
        )
    after_proj()
    for n in range(D // CHUNK):
        cols = slice(n * CHUNK, (n + 1) * CHUNK)
        rows_of = w_ref[n * CHUNK : (n + 1) * CHUNK, PROJ0 : PROJ0 + D]
        do_ref[:, cols] = dot(low_ref[...], rows_of, ((1,), (1,))).astype(BF16)
    before_attend()
    gbias_ref[...] = jnp.zeros_like(gbias_ref)
    masks = head_masks(PAIR)

    def attend(i, _):
        rows = pl.ds(pl.multiple_of(i * PAIR, 16), PAIR)
        keys = pl.ds(pl.multiple_of(i * PAIR, 16), KEYS)
        for g in range(4):
            here = slice(g * 128, (g + 1) * 128)
            k = qkv_ref[keys, D + g * 128 : D + (g + 1) * 128]
            v = qkv_ref[keys, 2 * D + g * 128 : 2 * D + (g + 1) * 128]
            q4 = spread_heads(qkv_ref[rows, here], masks)
            do4 = spread_heads(do_ref[rows, here], masks)
            p = probabilities(q4, k, rel_ref, mask_ref, i, g)
            dp = dot(do4, v, ((1,), (1,)))
            ds = (p * (dp - jnp.sum(dp * p, -1, keepdims=True))).astype(BF16)
            gbias_ref[g * 4 : (g + 1) * 4] += ds.astype(F32).reshape(4, PAIR, KEYS)
            dq = join_heads(dot(ds, k), masks) * SCALE
            dk = dot(ds, q4, ((0,), (0,))) * SCALE
            dv = dot(p.astype(BF16), do4, ((0,), (0,)))
            dqkv_ref[rows, here] = dq.astype(BF16)
            dqkv_ref[rows, D + g * 128 : D + (g + 1) * 128] = dk[:PAIR].astype(BF16)
            dqkv_ref[rows, 2 * D + g * 128 : 2 * D + (g + 1) * 128] = dv[:PAIR].astype(BF16)
        return 0

    lax.fori_loop(0, PAIRS, attend, 0)
    after_attend()
    n1, rstd1 = normalised(x_ref[...].astype(F32))
    turned_ref[...] = (n1 * small_ref[0:1] + small_ref[2:3]).T.astype(BF16)

    def qkv_step(n, _):
        cols = pl.ds(pl.multiple_of(n * CHUNK, CHUNK), CHUNK)
        put(cols, dot(turned_ref[...], dqkv_ref[:, cols]).astype(BF16))
        return 0

    lax.fori_loop(0, 3 * D // CHUNK, qkv_step, 0)
    after_weights()
    gsmall_ref[4:5] = jnp.sum(dqkv_ref[:, 0:D].astype(F32), 0, keepdims=True)
    gsmall_ref[5:6] = jnp.sum(dqkv_ref[:, 2 * D : 3 * D].astype(F32), 0, keepdims=True)
    du = dot(dqkv_ref[...], w_ref[:, QKV0 : QKV0 + 3 * D], ((1,), (1,)))
    n1, rstd1 = normalised(x_ref[...].astype(F32))
    gsmall_ref[0:1] = jnp.sum(du * n1, 0, keepdims=True)
    gsmall_ref[2:3] = jnp.sum(du, 0, keepdims=True)
    z = du * small_ref[0:1]
    zm = jnp.mean(z, -1, keepdims=True)
    zn = jnp.mean(z * n1, -1, keepdims=True)
    return (du_ref[...] + rstd1 * (z - zm - n1 * zn)).astype(BF16)


def table_rows_of(tables_ref, places_ref, rel_ref):
    rel_ref[...] = jnp.zeros_like(rel_ref)
    entry = lax.broadcasted_iota(jnp.int32, (RELS_PAD, KEYS), 0)
    tables = tables_ref[...].astype(BF16)

    def rows(n, _):
        for step in range(WIN):
            i = n * WIN + step
            hot = jnp.where(entry == places_ref[pl.ds(i, 1), :], 1.0, 0.0).astype(BF16)
            values = dot(tables, hot)
            rel_ref[:, i, :] = values
            rel_ref[:, i + WPAD, :] = pltpu.roll(values, WPAD, 1)
        return 0

    lax.fori_loop(0, WIN, rows, 0)


def table_sums(gbias_ref, places_ref):
    second = gbias_ref[:, WPAD:PAIR].reshape(16 * WPAD, KEYS)
    gbias_ref[:, 0:WPAD] += pltpu.roll(second, KEYS - WPAD, 1).reshape(16, WPAD, KEYS)
    entry = lax.broadcasted_iota(jnp.int32, (RELS_PAD, KEYS), 0)

    def rows(n, total):
        parts = []
        for step in range(WIN):
            i = n * WIN + step
            values = gbias_ref[:, i, :]
            high = values.astype(BF16)
            low = (values - high.astype(F32)).astype(BF16)
            hot = jnp.where(entry == places_ref[pl.ds(i, 1), :], 1.0, 0.0).astype(BF16)
            parts.append(dot(jnp.concatenate([high, low], axis=0), hot, ((1,), (1,))))
        return total + sum(parts)

    total = lax.fori_loop(0, WIN, rows, jnp.zeros((32, RELS_PAD), F32))
    return total[0:16] + total[16:32]


COPIES = 224


def piece_of(region):
    rows, cols = region
    return (pl.ds(rows[0], rows[1]), pl.ds(cols[0], cols[1]))


def cut(region, axis, index):
    rows, cols = region
    if axis == "z":
        return ((pl.multiple_of(index * 32, 32), 32), cols)
    width = cols[1] // 4
    return (rows, (pl.multiple_of(cols[0] + index * width, 128), width))


def train_kernel(
    slots_ref, images_ref, cot_hbm, qkv_hbm, proj_hbm, up_hbm, down_hbm, tiny_ref, places_ref, mask_ref,
    order_ref, back_ref, turn_ref,
    y_hbm, dx_hbm, grad_hbm, sums_ref,
    w_ref, x_ref, qkv_ref, o_ref, r_ref, act_ref, slope_ref, g_ref, core_ref, land_a, land_b, land_y, fin_ref,
    rel_ref, gbias_ref, low_ref, turned_ref, du_ref, dqkv_ref, do_ref, dy_ref, cot_ref,
    y_ref, y_land, dx_ref, dx_land, tiny_land, tables_ref, small_ref, qbias_ref, hbias_ref,
    gsmall_ref, ghidden_ref, sums_in, sums_core, sums_own, sums_land,
    send_sem, recv_sem, local_sem, free_sem,
):
    me = here()
    pipe = me["y"] % 2
    copies = Copies(send_sem, recv_sem)
    partner = moved(me, "core", 1)
    peers = {axis: [moved(me, axis, k) for k in (1, 2, 3)] for axis in "yxz"}
    across = [moved(partner, "y", k) for k in (1, 2, 3)]

    def block_at(y):
        return pl.ds(pl.multiple_of(block_index(y, me["core"]) * 128, 128), 128)

    own = block_index(me["y"], me["core"])
    own_rows = block_at(me["y"])
    parts = [
        (qkv_hbm.at[0], QKV0, 3 * D), (proj_hbm.at[0], PROJ0, D), (up_hbm.at[0], UP0, FF),
    ] + [(down_hbm.at[0, k * 128 : (k + 1) * 128], DOWN0 + k * D, D) for k in range(4)]
    locals_in = []
    for n, (src, lo, width) in enumerate(parts):
        local = pltpu.make_async_copy(src, w_ref.at[own_rows, lo : lo + width], local_sem.at[n])
        local.start()
        locals_in.append(local)
    cot_copy = pltpu.make_async_copy(cot_hbm.at[pl.ds(pipe * IMGS, IMGS)], cot_ref, local_sem.at[7])
    cot_copy.start()
    greet([partner] + across + [place for axis in "yxz" for place in peers[axis]])
    for local in locals_in:
        local.wait()

    span = PACKED // 3
    width = span // 8

    def weight_piece(y, lo, size):
        start = pl.multiple_of(block_index(y, me["core"]) * 128, 128)
        return w_ref.at[pl.ds(start, 128), pl.ds(lo, size)]

    def quarter(chunk, part, index):
        return pl.multiple_of(chunk * span + part * (span // 2) + index * width, 128), width

    first_base = {}

    def set_off(chunk):
        first_base[chunk] = copies.count
        for k in (1, 2, 3):
            for part, axis in enumerate("xz"):
                piece = weight_piece(me["y"], *quarter(chunk, part, me[axis]))
                copies.start(piece, piece, moved(me, "y", k))

    to_partner = {}
    set_off(0)
    tiny_copies = [
        copies.start(tiny_ref, tiny_land.at[own], place) for place in [partner] + peers["y"] + across
    ]
    for chunk in range(3):
        piece = weight_piece(me["y"], chunk * span, span)
        to_partner["own", chunk] = copies.start(piece, piece, partner)
    tiny_land[own] = tiny_ref[...]

    for b in range(IMGS):
        picture = images_ref[slots_ref[pipe * IMGS + b]]
        x_ref[0, b * IMG_ROWS : (b + 1) * IMG_ROWS] = dot(order_ref[0], picture).astype(BF16)
    set_off(1)
    cot_copy.wait()
    for b in range(IMGS):
        dy_ref[b * IMG_ROWS : (b + 1) * IMG_ROWS] = dot(order_ref[1], cot_ref[b]).astype(BF16)

    steps = [2 - pipe, 1 + 2 * pipe, 3 - pipe]
    seconds = {}

    def pass_on(chunk, slots):
        for slot in slots:
            y = (me["y"] - steps[slot] + 4) % 4
            for part, axis in enumerate("xz"):
                piece = weight_piece(y, *quarter(chunk, part, me[axis]))
                index = first_base[chunk] + (steps[slot] - 1) * 2 + part
                pltpu.make_async_remote_copy(
                    src_ref=piece, dst_ref=piece, send_sem=send_sem.at[index],
                    recv_sem=recv_sem.at[index], device_id=device_at(partner), device_id_type=MESH,
                ).wait_recv()
                for j in (1, 3, 2):
                    seconds[chunk, slot, part, j] = copies.start(piece, piece, moved(me, axis, j))

    def hand_over(chunk, slots):
        for slot in slots:
            y = (me["y"] - steps[slot] + 4) % 4
            for part in range(2):
                for j in (1, 3, 2):
                    seconds[chunk, slot, part, j].wait_recv()
            piece = weight_piece(y, chunk * span, span)
            to_partner[slot, chunk] = copies.start(piece, piece, partner)

    def arrived(chunk, slots):
        for slot in slots:
            to_partner[slot, chunk].wait_recv()

    pass_on(0, (0, 1))
    set_off(2)
    for copy in tiny_copies:
        copy.wait_recv()
    qbias_ref[...] = jnp.zeros_like(qbias_ref)
    for layer in range(2):
        for shard in range(4):
            rows = tiny_land[layer * 4 + shard]
            small_ref[layer, :, shard * 128 : (shard + 1) * 128] = rows[0:8, 0:128]
            for j in range(4):
                at = shard * 512 + j * 128
                hbias_ref[layer, :, at : at + 128] = rows[8 + j : 9 + j, 0:128]
                head = layer * 16 + shard * 4 + j
                tables_ref[head : head + 1] = rows[16 + j : 17 + j]
        qbias_ref[layer, :, 0:D] = small_ref[layer, 4:5]
        qbias_ref[layer, :, 2 * D : 3 * D] = small_ref[layer, 5:6]
    table_rows_of(tables_ref, places_ref, rel_ref)
    hand_over(0, (0, 1))
    pass_on(1, (0, 1))
    arrived(0, ("own", 0, 1))

    def params(layer):
        return (
            w_ref.at[pl.ds(layer * D, D)], small_ref.at[layer], qbias_ref.at[layer], hbias_ref.at[layer],
            rel_ref.at[pl.ds(layer * 16, 16)], mask_ref.at[layer],
        )

    def saved(layer):
        return tuple(ref.at[layer] for ref in (qkv_ref, o_ref, r_ref, act_ref, slope_ref))

    def in_token_order(layer, value, out, turned):
        for b in range(IMGS):
            own_rows = value[b * IMG_ROWS : (b + 1) * IMG_ROWS]
            out[b] = dot(back_ref[layer], own_rows).astype(BF16)
            if turned is not None:
                turned[b * IMG_ROWS : (b + 1) * IMG_ROWS] = dot(turn_ref[layer], own_rows).astype(BF16)

    def before_mlp0():
        hand_over(2, (0, 1))
        for chunk in range(3):
            pass_on(chunk, (2,))
        arrived(1, ("own", 0, 1))
        arrived(2, ("own", 0, 1))

    def after_qkv1():
        hand_over(1, (2,))
        hand_over(2, (2,))

    def before_mlp1():
        arrived(1, (2,))
        arrived(2, (2,))

    y0 = forward_body(
        params(0), saved(0), x_ref.at[0], low_ref, du_ref, after_qkv=lambda: pass_on(2, (0, 1)),
        after_attend=lambda: hand_over(1, (0, 1)), before_mlp=before_mlp0,
    )
    hand_over(0, (2,))
    in_token_order(0, y0, y_ref.at[0], x_ref.at[1])
    arrived(0, (2,))
    y1 = forward_body(
        params(1), saved(1), x_ref.at[1], low_ref, du_ref, after_qkv=after_qkv1, before_mlp=before_mlp1
    )
    in_token_order(1, y1, y_ref.at[1], None)
    neighbour = {**me, "y": me["y"] + 1 - 2 * pipe}
    y_copy = copies.start(y_ref.at[1 - pipe], y_land, neighbour)
    keep_out = pltpu.make_async_copy(y_ref.at[pipe], y_hbm.at[pl.ds(pipe * IMGS, IMGS)], local_sem.at[0])
    keep_out.start()

    core_copies, sent, regions = {}, {}, {}

    def send_core(layer, streams):
        for t in streams:
            lo, hi, _ = STREAMS[t]
            core_copies[layer, t] = copies.start(
                g_ref.at[layer, :, 1 - me["core"], :, lo:hi], core_ref.at[:, :, lo:hi], partner
            )

    def add_core(layer, streams):
        for t in streams:
            lo, hi, _ = STREAMS[t]
            core_copies[layer, t].wait_recv()

            def one(n, _, lo=lo, hi=hi):
                half, rows = n // 4, pl.ds(pl.multiple_of((n % 4) * 32, 32), 32)
                mine = (layer, half, me["core"], rows, slice(lo, hi))
                total = g_ref[mine].astype(F32) + core_ref[half, rows, lo:hi].astype(F32)
                g_ref[mine] = total.astype(BF16)
                return 0

            lax.fori_loop(0, 8, one, 0)
            regions[layer, t] = ((0, 128), (lo, hi - lo))

    def send(layer, streams, stage):
        for t in streams:
            axis = STREAMS[t][2][stage]
            land = (land_a, land_b)[stage][t]
            region = regions[layer, t]
            sent[layer, t] = [
                copies.start(
                    g_ref.at[(layer, slice(None), me["core"]) + piece_of(cut(region, axis, (me[axis] + k) % 4))],
                    land.at[layer, k - 1], moved(me, axis, k),
                )
                for k in (1, 3, 2)
            ]
            regions[layer, t] = cut(region, axis, me[axis])

    def add(layer, streams, stage):
        for t in streams:
            for copy in sent[layer, t]:
                copy.wait_recv()
            land = (land_a, land_b)[stage][t]
            (r0, nr), cols = regions[layer, t]
            steps_of = nr // 32

            def one(n, _, land=land, r0=r0, cols=cols, steps_of=steps_of):
                half, row = n // steps_of, pl.multiple_of((n % steps_of) * 32, 32)
                at = (layer, half, me["core"], pl.ds(pl.multiple_of(r0 + row, 32), 32), pl.ds(*cols))
                total = g_ref[at].astype(F32)
                for k in range(3):
                    total = total + land[layer, k, half, pl.ds(row, 32), :].astype(F32)
                g_ref[at] = total.astype(BF16)
                return 0

            lax.fori_loop(0, 2 * steps_of, one, 0)

    def send_y(streams):
        for t in streams:
            piece = piece_of(regions[0, t])
            sent["y", t] = []
            for k in (1, 3, 2):
                to = (me["y"] + k) % 4
                sent["y", t].append(
                    copies.start(
                        g_ref.at[(to % 2, to // 2, me["core"]) + piece], land_y[t].at[k - 1], moved(me, "y", k)
                    )
                )

    def add_y(streams):
        for t in streams:
            for copy in sent["y", t]:
                copy.wait_recv()
            piece = piece_of(regions[0, t])
            total = g_ref[(pipe, me["y"] // 2, me["core"]) + piece].astype(F32)
            for k in range(3):
                total = total + land_y[t][k].astype(F32)
            fin_ref[piece] = total.astype(BF16)

    def spread(streams, level):
        for t in streams:
            if level == 1:
                for copy in sent["fin", t]:
                    copy.wait_recv()
            lo, hi, order = STREAMS[t]
            part = (hi - lo) // 4
            rows = pl.ds(pl.multiple_of(me["z"] * 32, 32), 32)
            cols = pl.ds(pl.multiple_of(lo + me["x"] * part, 128), part)
            if level == 1:
                if order[0] == "x":
                    cols = pl.ds(lo, hi - lo)
                else:
                    rows = pl.ds(0, 128)
            piece = fin_ref.at[rows, cols]
            sent["fin", t] = [copies.start(piece, piece, moved(me, order[level], k)) for k in (1, 3, 2)]

    late = LATE
    early = tuple(t for t in range(len(STREAMS)) if t not in late)

    def results(layer):
        return (g_ref.at[layer], gsmall_ref.at[layer], ghidden_ref.at[layer], gbias_ref.at[layer])

    scratch = (low_ref, turned_ref, du_ref, dqkv_ref, do_ref)

    def before_attend1():
        for t in (1, 0):
            add_core(1, (t,))
            send(1, (t,), 0)

    dx1 = backward_body(
        params(1), saved(1), x_ref.at[1], dy_ref, results(1), scratch,
        after_mlp=lambda: send_core(1, (1,)), after_proj=lambda: send_core(1, (0,)),
        before_attend=before_attend1, after_weights=lambda: send_core(1, late),
    )
    in_token_order(1, dx1, dx_ref.at[1], dy_ref)
    add_core(1, late)
    pl.semaphore_signal(free_sem, inc=1, device_id=device_at(partner), device_id_type=MESH)
    send(1, late, 0)

    def in_mlp0():
        add(1, (1, 0), 0)
        send(1, (1, 0), 1)

    def after_mlp0():
        pl.semaphore_wait(free_sem, 1)
        send_core(0, (1,))
        add(1, late, 0)
        send(1, late, 1)

    def before_attend0():
        for t in (1, 0):
            add_core(0, (t,))
            send(0, (t,), 0)

    def after_attend0():
        add(1, early, 1)
        add(1, late, 1)

    def after_weights0():
        send_core(0, late)
        add(0, (1,), 0)
        send(0, (1,), 1)

    dx0 = backward_body(
        params(0), saved(0), x_ref.at[0], dy_ref, results(0), scratch,
        in_mlp=in_mlp0, after_mlp=after_mlp0, after_proj=lambda: send_core(0, (0,)),
        before_attend=before_attend0, after_attend=after_attend0, after_weights=after_weights0,
    )
    add_core(0, late)
    send(0, late, 0)
    in_token_order(0, dx0, dx_ref.at[0], None)
    dx_copy = copies.start(dx_ref.at[1 - pipe], dx_land, neighbour)
    dx_keep = pltpu.make_async_copy(dx_ref.at[pipe], dx_hbm.at[pl.ds(pipe * IMGS, IMGS)], local_sem.at[1])
    dx_keep.start()
    add(0, (0,), 0)
    send(0, (0,), 1)

    for layer in range(2):
        gtable = table_sums(gbias_ref.at[layer], places_ref)
        for shard in range(4):
            half, core = shard // 2, shard % 2
            y = half * 2 + layer
            sums_in[core, y] = jnp.zeros((SMALL_ROWS, RELS_PAD), F32)
            sums_in[core, y, 0:8, 0:128] = gsmall_ref[layer, :, shard * 128 : (shard + 1) * 128]
            for j in range(4):
                at = shard * 512 + j * 128
                sums_in[core, y, 8 + j : 9 + j, 0:128] = ghidden_ref[layer, :, at : at + 128]
            sums_in[core, y, 16:20] = gtable[shard * 4 : shard * 4 + 4]
    small_copy = copies.start(sums_in.at[1 - me["core"]], sums_core, partner)
    add(0, early, 1)
    send_y(early)
    add(0, late, 0)
    send(0, late, 1)
    small_copy.wait_recv()
    sums_own[0] = sums_in[me["core"]] + sums_core[...]
    small_sent = [
        copies.start(sums_own.at[0, (me["y"] + k) % 4], sums_land.at[0, k - 1], moved(me, "y", k))
        for k in (1, 3, 2)
    ]

    def add_small(stage):
        for copy in small_sent:
            copy.wait_recv()
        start = sums_own[0, me["y"]] if stage == 0 else sums_own[stage, 0]
        return start + sums_land[stage, 0] + sums_land[stage, 1] + sums_land[stage, 2]

    add_y(early)
    spread(early, 0)
    add(0, late, 1)
    send_y(late)
    for stage, axis in enumerate("xz", 1):
        sums_own[stage, 0] = add_small(stage - 1)
        small_sent = [
            copies.start(sums_own.at[stage, 0], sums_land.at[stage, k - 1], moved(me, axis, k))
            for k in (1, 3, 2)
        ]
        if stage == 1:
            spread(early, 1)
            add_y(late)
            spread(late, 0)
    spread(late, 1)
    sums_ref[...] = add_small(2)
    outs = []
    y_copy.wait_recv()
    dx_copy.wait_recv()
    for n, (src, dst) in enumerate(((y_land, y_hbm), (dx_land, dx_hbm)), 2):
        out = pltpu.make_async_copy(src, dst.at[pl.ds((1 - pipe) * IMGS, IMGS)], local_sem.at[n])
        out.start()
        outs.append(out)
    for t in early + late:
        for copy in sent["fin", t]:
            copy.wait_recv()
    grad_out = pltpu.make_async_copy(fin_ref, grad_hbm, local_sem.at[4])
    grad_out.start()
    for copy in [keep_out, dx_keep, grad_out] + outs:
        copy.wait()
    copies.finish()


def land_shapes(stage):
    shapes = []
    for lo, hi, order in STREAMS:
        done = order[: stage + 1]
        shape = (2, 3, 2, 32 if "z" in done else 128, (hi - lo) // (4 if "x" in done else 1))
        shapes.append(pltpu.VMEM(shape, BF16))
    return tuple(shapes)


def train(slots, images, cotangent, qkv, proj, up, down, tiny, places, mask, order, back, turn):
    anywhere = pl.BlockSpec(memory_space=pl.ANY)
    vmem = pl.BlockSpec(memory_space=pltpu.VMEM)
    tokens = (2 * IMGS, OUT_ROWS, D)
    half = (IMGS, OUT_ROWS, D)
    piece = (SMALL_ROWS, RELS_PAD)
    low = pltpu.VMEM((ROWS, D), BF16)
    return pl.pallas_call(
        train_kernel,
        out_shape=[
            jax.ShapeDtypeStruct(tokens, BF16), jax.ShapeDtypeStruct(tokens, BF16),
            jax.ShapeDtypeStruct((128, PACKED), BF16), jax.ShapeDtypeStruct(piece, F32),
        ],
        in_specs=[pl.BlockSpec(memory_space=pltpu.SMEM), vmem] + [anywhere] * 5 + [vmem] * 6,
        out_specs=[anywhere] * 3 + [vmem],
        scratch_shapes=[
            pltpu.VMEM((2 * D, PACKED), BF16),
            pltpu.VMEM((2, ROWS, D), BF16),
            pltpu.VMEM((2, KROWS, 3 * D), BF16),
            pltpu.VMEM((2, ROWS, D), BF16),
            pltpu.VMEM((2, ROWS, D), F32),
            pltpu.VMEM((2, ROWS, FF), BF16),
            pltpu.VMEM((2, ROWS, FF), BF16),
            pltpu.VMEM((2, 2, 2, 128, PACKED), BF16),
            pltpu.VMEM((2, 128, PACKED), BF16),
            land_shapes(0), land_shapes(1),
            tuple(pltpu.VMEM((3, 32, (hi - lo) // 4), BF16) for lo, hi, _ in STREAMS),
            pltpu.VMEM((128, PACKED), BF16),
            pltpu.VMEM((32, PAIR, KEYS), F32),
            pltpu.VMEM((2, 16, PAIR, KEYS), F32),
            low,
            pltpu.VMEM((D, ROWS), BF16),
            pltpu.VMEM((ROWS, D), F32),
            pltpu.VMEM((ROWS, 3 * D), BF16),
            low,
            low,
            pltpu.VMEM((IMGS, TOK, D), BF16),
            pltpu.VMEM((2,) + half, BF16),
            pltpu.VMEM(half, BF16),
            pltpu.VMEM((2,) + half, BF16),
            pltpu.VMEM(half, BF16),
            pltpu.VMEM((8, TINY_ROWS, RELS_PAD), F32),
            pltpu.VMEM((32, RELS_PAD), F32),
            pltpu.VMEM((2, 8, D), F32),
            pltpu.VMEM((2, 1, 3 * D), F32),
            pltpu.VMEM((2, 1, FF), F32),
            pltpu.VMEM((2, 8, D), F32),
            pltpu.VMEM((2, 1, FF), F32),
            pltpu.VMEM((2, 4) + piece, F32),
            pltpu.VMEM((4,) + piece, F32),
            pltpu.VMEM((3, 4) + piece, F32),
            pltpu.VMEM((3, 3) + piece, F32),
            pltpu.SemaphoreType.DMA((COPIES,)),
            pltpu.SemaphoreType.DMA((COPIES,)),
            pltpu.SemaphoreType.DMA((8,)),
            pltpu.SemaphoreType.REGULAR,
        ],
        compiler_params=pltpu.CompilerParams(
            collective_id=1, has_side_effects=True, vmem_limit_bytes=VMEM_LIMIT
        ),
        cost_estimate=pl.CostEstimate(
            flops=12 * ROWS * D * PACKED, bytes_accessed=16 << 20, transcendentals=6 * ROWS * FF
        ),
        name="train_layers",
    )(slots, images, cotangent, qkv, proj, up, down, tiny, places, mask, order, back, turn)


def block_pair(blocks, fill):
    lead = blocks.shape[:-3]
    none = [(0, 0)] * len(lead)
    pad_rows = [(0, WPAD - WTOK)]
    first = jnp.pad(blocks[..., 0, :, :], none + pad_rows + [(0, KEYS - WTOK)], constant_values=fill)
    second = jnp.pad(
        blocks[..., 1, :, :], none + pad_rows + [(WPAD, KEYS - WTOK - WPAD)], constant_values=fill
    )
    return jnp.concatenate([first, second], axis=-2)


def inside_blocks():
    rows, cols = np.arange(PAIR)[:, None] // WPAD, np.arange(KEYS)[None, :]
    return (cols // WPAD == rows) & (cols % WPAD < WTOK) & (cols < PAIR)


def on_device(
    images, cotangent, micro_order, region_ids, rel_index, qkv_weight, proj_weight, up_weight,
    down_weight, bias_table, norm_gains, offsets, hidden_bias,
):
    first_section = lax.axis_index("pipe") == 0
    table_rows = bias_table.shape[1]

    def lanes(block, rows):
        return jnp.pad(
            block.astype(F32), ((0, rows - block.shape[0]), (0, RELS_PAD - block.shape[1]))
        )

    tiny = jnp.concatenate(
        [
            lanes(jnp.concatenate([norm_gains[0], offsets[0]]), 8),
            lanes(hidden_bias[0].reshape(4, 128), 8),
            lanes(bias_table[0].T, 8),
        ]
    )
    places = jnp.pad(rel_index, ((0, WPAD - WTOK), (0, KEYS - WTOK)), constant_values=-1)
    regions = region_ids.reshape(2, WIN, 2, WIN).transpose(0, 2, 1, 3).reshape(2, 2, WTOK)
    regions = jnp.pad(regions, ((0, 0), (0, 0), (0, WPAD - WTOK))).reshape(2, PAIR)
    queries = regions[:, :, None]
    keys = jnp.pad(regions, ((0, 0), (0, KEYS - PAIR)))[:, None, :]
    inside = inside_blocks()
    mask0 = np.broadcast_to(np.where(inside, 0.0, BLOCKED), (2, PAIR, KEYS)).astype(np.float32)
    mask1 = jnp.where(inside[None], jnp.where(queries == keys, 0.0, -1e9), BLOCKED).astype(F32)
    mask = jnp.stack([jnp.asarray(mask0), mask1])
    order = jnp.asarray(np.stack([order_matrix(0), order_matrix(SHIFT)]), BF16)
    back = jnp.asarray(np.stack([back_matrix(0), back_matrix(SHIFT)]), BF16)
    turn = jnp.asarray(np.stack([turn_matrix(0, SHIFT), turn_matrix(SHIFT, 0)]), BF16)
    slot_order = micro_order[0]

    layer_out, dx_slots, share, sums = train(
        slot_order, images, cotangent, qkv_weight, proj_weight, up_weight, down_weight, tiny, places,
        mask, order, back, turn,
    )
    slots = jnp.arange(2 * IMGS, dtype=jnp.int32)
    inverse = jnp.sum(jnp.where(slot_order[:, None] == slots[None, :], slots[:, None], 0), axis=0)
    picks = jnp.where(first_section, inverse, slots)
    input_grad = jnp.take(dx_slots[:, :TOK], picks, axis=0).astype(F32)
    down = jnp.concatenate(
        [share[:, DOWN0 + k * D : DOWN0 + (k + 1) * D] for k in range(4)], axis=0
    )
    return (
        layer_out[None, :, :TOK],
        input_grad[None],
        share[None, :, QKV0:PROJ0].astype(F32),
        share[None, :, PROJ0:UP0].astype(F32),
        share[None, :, UP0:DOWN0].astype(F32),
        down[None].astype(F32),
        sums[16:20, :table_rows].T[None],
        sums[None, 0:2, 0:128],
        sums[None, 2:8, 0:128],
        sums[8:12, 0:128].reshape(1, D),
    )


def solution(mesh):
    rows = P(("shard", "rep"), None, None)
    split = P("pipe", "shard", None)
    lanes = P("pipe", None, "shard")
    return jax.shard_map(
        on_device,
        mesh=mesh,
        in_specs=(
            rows, rows, P(("shard", "rep"), None), P(), P(),
            split, split, split, split, lanes, lanes, lanes, P("pipe", "shard"),
        ),
        out_specs=(
            P("pipe", ("shard", "rep"), None, None), P("pipe", ("shard", "rep"), None, None),
            split, split, split, split, lanes, lanes, lanes, P("pipe", "shard"),
        ),
        check_vma=False,
    )
```

```python
import functools
import math

import jax
import jax.numpy as jnp
import numpy as np
from jax import lax
from jax.experimental import pallas as pl
from jax.experimental.pallas import tpu as pltpu
from jax.sharding import PartitionSpec as P

SIDE = 14
WIN = 7
SHIFT = 3
D = 512
FF = 2048
HEAD = 32
TOK = SIDE * SIDE
WTOK = WIN * WIN
WPAD = 56
PAIR = 2 * WPAD
IMG_ROWS = 4 * WPAD
IMGS = 2
ROWS = IMGS * IMG_ROWS
PAIRS = ROWS // PAIR
KEYS = 128
KROWS = ROWS + KEYS - PAIR
OUT_ROWS = 208
RELS_PAD = 256
QKV0, PROJ0, UP0, DOWN0, PACKED = 0, 1536, 2048, 4096, 6144
CHUNK = 256
SCALE = HEAD ** (-0.5)
BLOCKED = -1e30
VMEM_LIMIT = 64 * 1024 * 1024 - 1024
BF16 = jnp.bfloat16
F32 = jnp.float32


def window_places(shift):
    place = np.zeros((TOK,), np.int64)
    for wr in range(2):
        for wc in range(2):
            for i in range(WIN):
                for j in range(WIN):
                    a = (wr * WIN + i + shift) % SIDE
                    b = (wc * WIN + j + shift) % SIDE
                    place[a * SIDE + b] = (wr * 2 + wc) * WPAD + i * WIN + j
    return place


def order_matrix(shift):
    matrix = np.zeros((IMG_ROWS, TOK), np.float32)
    matrix[window_places(shift), np.arange(TOK)] = 1.0
    return matrix


def back_matrix(shift):
    matrix = np.zeros((OUT_ROWS, IMG_ROWS), np.float32)
    matrix[:TOK] = order_matrix(shift).T
    return matrix


def turn_matrix(from_shift, to_shift):
    return order_matrix(to_shift) @ order_matrix(from_shift).T


def dot(a, b, dims=((1,), (0,))):
    return lax.dot_general(a, b, (dims, ((), ())), preferred_element_type=F32)


def normalised(x):
    mean = jnp.mean(x, -1, keepdims=True)
    centred = x - mean
    rstd = lax.rsqrt(jnp.mean(centred * centred, -1, keepdims=True) + 1e-5)
    return centred * rstd, rstd


def head_masks(rows):
    lane = lax.broadcasted_iota(jnp.int32, (rows, 128), 1) // HEAD
    return [lane == h for h in range(4)]


def spread_heads(block, masks):
    zero = jnp.zeros_like(block)
    return jnp.concatenate([jnp.where(m, block, zero) for m in masks], axis=0)


def join_heads(stacked, masks):
    total = None
    for h, m in enumerate(masks):
        part = jnp.where(m, stacked[h * PAIR : (h + 1) * PAIR], 0.0)
        total = part if total is None else total + part
    return total


def probabilities(q4, k, rel_ref, mask_ref, i, g):
    s = dot(q4, k, ((1,), (1,))) * SCALE
    bias = rel_ref[pl.ds(g * 4, 4)].astype(F32) + mask_ref[lax.rem(i, 2)][None]
    s = s + bias.reshape(4 * PAIR, KEYS)
    e = jnp.exp(s - jnp.max(s, -1, keepdims=True))
    return e * (1.0 / jnp.sum(e, -1, keepdims=True))


def down_chunk(w_ref, c):
    row = pl.multiple_of((c // 2) * 128, 128)
    col = pl.multiple_of(DOWN0 + (c % 2) * 1024, 128)
    first = w_ref[pl.ds(row, 128), pl.ds(col, D)]
    second = w_ref[pl.ds(row, 128), pl.ds(col + D, D)]
    return jnp.concatenate([first, second], axis=0)


MESH = pl.DeviceIdType.MESH
STREAMS = ((1536, 4096, "xz"), (4096, 6144, "zx"), (0, 512, "xz"), (512, 1536, "zx"))
LATE = (2, 3)
TINY_ROWS = 24
SMALL_ROWS = 24


def here():
    pipe, shard, rep = lax.axis_index("pipe"), lax.axis_index("shard"), lax.axis_index("rep")
    return {"y": (shard // 2) * 2 + pipe, "core": shard % 2, "z": rep // 4, "x": rep % 4}


def device_at(place):
    return {
        "pipe": place["y"] % 2,
        "shard": (place["y"] // 2) * 2 + place["core"],
        "rep": place["z"] * 4 + place["x"],
    }


def moved(place, axis, steps):
    size = 2 if axis == "core" else 4
    return {**place, axis: (place[axis] + steps) % size}


def block_index(y, core):
    return (y % 2) * 4 + (y // 2) * 2 + core


class Copies:
    def __init__(self, send_sem, recv_sem):
        self.send_sem, self.recv_sem, self.count, self.started = send_sem, recv_sem, 0, []

    def start(self, src, dst, place):
        copy = pltpu.make_async_remote_copy(
            src_ref=src, dst_ref=dst, send_sem=self.send_sem.at[self.count],
            recv_sem=self.recv_sem.at[self.count], device_id=device_at(place), device_id_type=MESH,
        )
        copy.start()
        self.count += 1
        self.started.append(copy)
        return copy

    def finish(self):
        for copy in self.started:
            copy.wait_send()


def greet(places, meanwhile):
    barrier = pltpu.get_barrier_semaphore()
    for place in places:
        pl.semaphore_signal(barrier, inc=1, device_id=device_at(place), device_id_type=MESH)
    meanwhile()
    pl.semaphore_wait(barrier, len(places))


def nothing():
    pass


def forward_body(
    params, saved, x_ref, low_ref, acc_ref, after_qkv=nothing, after_attend=nothing, before_mlp=nothing
):
    w_ref, small_ref, qbias_ref, hbias_ref, rel_ref, mask_ref = params
    qkv_ref, o_ref, r_ref, act_ref, slope_ref = saved
    n1, _ = normalised(x_ref[...].astype(F32))
    low_ref[...] = (n1 * small_ref[0:1] + small_ref[2:3]).astype(BF16)
    qkv_ref[ROWS:, :] = jnp.zeros((KROWS - ROWS, 3 * D), BF16)

    def qkv_step(n, _):
        cols = pl.ds(pl.multiple_of(n * CHUNK, CHUNK), CHUNK)
        part = dot(low_ref[...], w_ref[:, cols]) + qbias_ref[:, cols]
        qkv_ref[0:ROWS, cols] = part.astype(BF16)
        return 0

    lax.fori_loop(0, 3 * D // CHUNK, qkv_step, 0)
    after_qkv()
    masks = head_masks(PAIR)

    def attend(i, _):
        rows = pl.ds(pl.multiple_of(i * PAIR, 16), PAIR)
        keys = pl.ds(pl.multiple_of(i * PAIR, 16), KEYS)
        for g in range(4):
            q = qkv_ref[rows, g * 128 : (g + 1) * 128]
            k = qkv_ref[keys, D + g * 128 : D + (g + 1) * 128]
            v = qkv_ref[keys, 2 * D + g * 128 : 2 * D + (g + 1) * 128]
            p = probabilities(spread_heads(q, masks), k, rel_ref, mask_ref, i, g)
            o4 = dot(p.astype(BF16), v)
            o_ref[rows, g * 128 : (g + 1) * 128] = join_heads(o4, masks).astype(BF16)
        return 0

    lax.fori_loop(0, PAIRS, attend, 0)
    after_attend()
    for n in range(D // CHUNK):
        cols = slice(n * CHUNK, (n + 1) * CHUNK)
        part = dot(o_ref[...], w_ref[:, PROJ0 + n * CHUNK : PROJ0 + (n + 1) * CHUNK])
        r_ref[:, cols] = x_ref[:, cols].astype(F32) + part + small_ref[6:7, cols]
    r = r_ref[...]
    n2, _ = normalised(r)
    low_ref[...] = (n2 * small_ref[1:2] + small_ref[3:4]).astype(BF16)
    acc_ref[...] = r + small_ref[7:8]
    before_mlp()

    def mlp(c, _):
        cols = pl.ds(pl.multiple_of(c * CHUNK, CHUNK), CHUNK)
        up = w_ref[:, pl.ds(pl.multiple_of(UP0 + c * CHUNK, CHUNK), CHUNK)]
        hid = dot(low_ref[...], up) + hbias_ref[:, cols]
        cdf = 0.5 * (1.0 + lax.erf(hid * math.sqrt(0.5)))
        act = (hid * cdf).astype(BF16)
        act_ref[:, cols] = act
        density = jnp.exp(-0.5 * hid * hid) * (1.0 / math.sqrt(2.0 * math.pi))
        slope_ref[:, cols] = (cdf + hid * density).astype(BF16)
        acc_ref[...] += dot(act, down_chunk(w_ref, c))
        return 0

    lax.fori_loop(0, FF // CHUNK, mlp, 0)
    return acc_ref[...].astype(BF16)


def backward_body(
    params, saved, x_ref, dy_ref, results, scratch,
    in_mlp=nothing, after_mlp=nothing, after_proj=nothing, before_attend=nothing, after_attend=nothing,
    after_weights=nothing,
):
    w_ref, small_ref, _, _, rel_ref, mask_ref = params
    qkv_ref, o_ref, r_ref, act_ref, slope_ref = saved
    g_ref, gsmall_ref, ghidden_ref, gbias_ref = results
    low_ref, turned_ref, du_ref, dqkv_ref, do_ref = scratch

    def put(cols, value):
        for b in range(4):
            g_ref[b // 2, b % 2, :, cols] = value[b * 128 : (b + 1) * 128]

    n2, rstd2 = normalised(r_ref[...])
    turned_ref[...] = (n2 * small_ref[1:2] + small_ref[3:4]).T.astype(BF16)
    du_ref[...] = jnp.zeros_like(du_ref)

    def mlp(c, _):
        cols = pl.ds(pl.multiple_of(c * CHUNK, CHUNK), CHUNK)
        up_cols = pl.ds(pl.multiple_of(UP0 + c * CHUNK, CHUNK), CHUNK)
        dy = dy_ref[...]
        dact = dot(dy, down_chunk(w_ref, c), ((1,), (1,)))
        dhid = (dact * slope_ref[:, cols].astype(F32)).astype(BF16)
        ghidden_ref[:, cols] = jnp.sum(dhid.astype(F32), 0, keepdims=True)
        down = dot(act_ref[:, cols], dy, ((0,), (0,))).astype(BF16)
        block = c // 2
        col = pl.multiple_of(DOWN0 + (c % 2) * 1024, 128)
        g_ref[block // 2, block % 2, :, pl.ds(col, D)] = down[:128]
        g_ref[block // 2, block % 2, :, pl.ds(col + D, D)] = down[128:]
        put(up_cols, dot(turned_ref[...], dhid).astype(BF16))
        du_ref[...] += dot(dhid, w_ref[:, up_cols], ((1,), (1,)))
        return 0

    lax.fori_loop(0, FF // CHUNK // 2, mlp, 0)
    in_mlp()
    lax.fori_loop(FF // CHUNK // 2, FF // CHUNK, mlp, 0)
    after_mlp()
    dy = dy_ref[...].astype(F32)
    du2 = du_ref[...]
    n2, rstd2 = normalised(r_ref[...])
    z = du2 * small_ref[1:2]
    zm = jnp.mean(z, -1, keepdims=True)
    zn = jnp.mean(z * n2, -1, keepdims=True)
    dr = dy + rstd2 * (z - zm - n2 * zn)
    db = dr.astype(BF16)
    low_ref[...] = db
    gsmall_ref[1:2] = jnp.sum(du2 * n2, 0, keepdims=True)
    gsmall_ref[3:4] = jnp.sum(du2, 0, keepdims=True)
    gsmall_ref[6:7] = jnp.sum(db.astype(F32), 0, keepdims=True)
    gsmall_ref[7:8] = jnp.sum(dy, 0, keepdims=True)
    du_ref[...] = dr
    turned_ref[...] = o_ref[...].astype(F32).T.astype(BF16)
    for n in range(D // CHUNK):
        cols = slice(n * CHUNK, (n + 1) * CHUNK)
        put(
            slice(PROJ0 + n * CHUNK, PROJ0 + (n + 1) * CHUNK),
            dot(turned_ref[...], low_ref[:, cols]).astype(BF16),
        )
    after_proj()
    for n in range(D // CHUNK):
        cols = slice(n * CHUNK, (n + 1) * CHUNK)
        rows_of = w_ref[n * CHUNK : (n + 1) * CHUNK, PROJ0 : PROJ0 + D]
        do_ref[:, cols] = dot(low_ref[...], rows_of, ((1,), (1,))).astype(BF16)
    before_attend()
    gbias_ref[...] = jnp.zeros_like(gbias_ref)
    masks = head_masks(PAIR)

    def attend(i, _):
        rows = pl.ds(pl.multiple_of(i * PAIR, 16), PAIR)
        keys = pl.ds(pl.multiple_of(i * PAIR, 16), KEYS)
        for g in range(4):
            here = slice(g * 128, (g + 1) * 128)
            k = qkv_ref[keys, D + g * 128 : D + (g + 1) * 128]
            v = qkv_ref[keys, 2 * D + g * 128 : 2 * D + (g + 1) * 128]
            q4 = spread_heads(qkv_ref[rows, here], masks)
            do4 = spread_heads(do_ref[rows, here], masks)
            p = probabilities(q4, k, rel_ref, mask_ref, i, g)
            dp = dot(do4, v, ((1,), (1,)))
            ds = (p * (dp - jnp.sum(dp * p, -1, keepdims=True))).astype(BF16)
            gbias_ref[g * 4 : (g + 1) * 4] += ds.astype(F32).reshape(4, PAIR, KEYS)
            dq = join_heads(dot(ds, k), masks) * SCALE
            dk = dot(ds, q4, ((0,), (0,))) * SCALE
            dv = dot(p.astype(BF16), do4, ((0,), (0,)))
            dqkv_ref[rows, here] = dq.astype(BF16)
            dqkv_ref[rows, D + g * 128 : D + (g + 1) * 128] = dk[:PAIR].astype(BF16)
            dqkv_ref[rows, 2 * D + g * 128 : 2 * D + (g + 1) * 128] = dv[:PAIR].astype(BF16)
        return 0

    lax.fori_loop(0, PAIRS, attend, 0)
    after_attend()
    n1, rstd1 = normalised(x_ref[...].astype(F32))
    turned_ref[...] = (n1 * small_ref[0:1] + small_ref[2:3]).T.astype(BF16)

    def qkv_step(n, _):
        cols = pl.ds(pl.multiple_of(n * CHUNK, CHUNK), CHUNK)
        put(cols, dot(turned_ref[...], dqkv_ref[:, cols]).astype(BF16))
        return 0

    lax.fori_loop(0, 3 * D // CHUNK, qkv_step, 0)
    after_weights()
    gsmall_ref[4:5] = jnp.sum(dqkv_ref[:, 0:D].astype(F32), 0, keepdims=True)
    gsmall_ref[5:6] = jnp.sum(dqkv_ref[:, 2 * D : 3 * D].astype(F32), 0, keepdims=True)
    du = dot(dqkv_ref[...], w_ref[:, QKV0 : QKV0 + 3 * D], ((1,), (1,)))
    n1, rstd1 = normalised(x_ref[...].astype(F32))
    gsmall_ref[0:1] = jnp.sum(du * n1, 0, keepdims=True)
    gsmall_ref[2:3] = jnp.sum(du, 0, keepdims=True)
    z = du * small_ref[0:1]
    zm = jnp.mean(z, -1, keepdims=True)
    zn = jnp.mean(z * n1, -1, keepdims=True)
    return (du_ref[...] + rstd1 * (z - zm - n1 * zn)).astype(BF16)


def table_rows_of(tables_ref, places_ref, rel_ref):
    rel_ref[...] = jnp.zeros_like(rel_ref)
    entry = lax.broadcasted_iota(jnp.int32, (RELS_PAD, KEYS), 0)
    tables = tables_ref[...].astype(BF16)

    def rows(n, _):
        for step in range(WIN):
            i = n * WIN + step
            hot = jnp.where(entry == places_ref[pl.ds(i, 1), :], 1.0, 0.0).astype(BF16)
            values = dot(tables, hot)
            rel_ref[:, i, :] = values
            rel_ref[:, i + WPAD, :] = pltpu.roll(values, WPAD, 1)
        return 0

    lax.fori_loop(0, WIN, rows, 0)


def table_sums(gbias_ref, places_ref):
    second = gbias_ref[:, WPAD:PAIR].reshape(32 * WPAD, KEYS)
    gbias_ref[:, 0:WPAD] += pltpu.roll(second, KEYS - WPAD, 1).reshape(32, WPAD, KEYS)
    entry = lax.broadcasted_iota(jnp.int32, (RELS_PAD, KEYS), 0)

    def rows(n, total):
        parts = []
        for step in range(WIN):
            i = n * WIN + step
            values = gbias_ref[:, i, :]
            high = values.astype(BF16)
            low = (values - high.astype(F32)).astype(BF16)
            hot = jnp.where(entry == places_ref[pl.ds(i, 1), :], 1.0, 0.0).astype(BF16)
            parts.append(dot(jnp.concatenate([high, low], axis=0), hot, ((1,), (1,))))
        return total + sum(parts)

    total = lax.fori_loop(0, WIN, rows, jnp.zeros((64, RELS_PAD), F32))
    return total[0:32] + total[32:64]


COPIES = 224


def piece_of(region):
    rows, cols = region
    return (pl.ds(rows[0], rows[1]), pl.ds(cols[0], cols[1]))


def cut(region, axis, index):
    rows, cols = region
    if axis == "z":
        return ((pl.multiple_of(index * 32, 32), 32), cols)
    width = cols[1] // 4
    return (rows, (pl.multiple_of(cols[0] + index * width, 128), width))


def train_kernel(
    slots_ref, images_ref, cot_hbm, qkv_hbm, proj_hbm, up_hbm, down_hbm, tiny_ref, places_ref, mask_ref,
    order_ref, back_ref, turn_ref,
    y_hbm, dx_hbm, grad_hbm, sums_ref,
    w_ref, x_ref, qkv_ref, o_ref, r_ref, act_ref, slope_ref, g_ref, core_ref, land_a, land_b, land_y, fin_ref,
    rel_ref, gbias_ref, low_ref, turned_ref, du_ref, dqkv_ref, do_ref, dy_ref, cot_ref,
    y_ref, y_land, dx_ref, dx_land, tiny_land, tables_ref, small_ref, qbias_ref, hbias_ref,
    gsmall_ref, ghidden_ref, sums_in, sums_core, sums_own, sums_land,
    send_sem, recv_sem, local_sem, free_sem,
):
    me = here()
    pipe = me["y"] % 2
    copies = Copies(send_sem, recv_sem)
    partner = moved(me, "core", 1)
    peers = {axis: [moved(me, axis, k) for k in (1, 2, 3)] for axis in "yxz"}
    across = [moved(partner, "y", k) for k in (1, 2, 3)]

    def block_at(y):
        return pl.ds(pl.multiple_of(block_index(y, me["core"]) * 128, 128), 128)

    own = block_index(me["y"], me["core"])
    own_rows = block_at(me["y"])
    parts = [
        (qkv_hbm.at[0], QKV0, 3 * D), (proj_hbm.at[0], PROJ0, D), (up_hbm.at[0], UP0, FF),
    ] + [(down_hbm.at[0, k * 128 : (k + 1) * 128], DOWN0 + k * D, D) for k in range(4)]
    locals_in = []
    for n, (src, lo, width) in enumerate(parts):
        local = pltpu.make_async_copy(src, w_ref.at[own_rows, lo : lo + width], local_sem.at[n])
        local.start()
        locals_in.append(local)
    cot_copy = pltpu.make_async_copy(cot_hbm.at[pl.ds(pipe * IMGS, IMGS)], cot_ref, local_sem.at[7])
    cot_copy.start()

    def order_tokens():
        for b in range(IMGS):
            picture = images_ref[slots_ref[pipe * IMGS + b]]
            x_ref[0, b * IMG_ROWS : (b + 1) * IMG_ROWS] = dot(order_ref[0], picture).astype(BF16)
        cot_copy.wait()
        for b in range(IMGS):
            dy_ref[b * IMG_ROWS : (b + 1) * IMG_ROWS] = dot(order_ref[1], cot_ref[b]).astype(BF16)
        for local in locals_in:
            local.wait()

    greet([partner] + across + [place for axis in "yxz" for place in peers[axis]], order_tokens)

    span = PACKED // 3
    width = span // 8

    def weight_piece(y, lo, size):
        start = pl.multiple_of(block_index(y, me["core"]) * 128, 128)
        return w_ref.at[pl.ds(start, 128), pl.ds(lo, size)]

    def quarter(chunk, part, index):
        return pl.multiple_of(chunk * span + part * (span // 2) + index * width, 128), width

    first_base = {}

    def set_off(chunk):
        first_base[chunk] = copies.count
        for k in (1, 2, 3):
            for part, axis in enumerate("xz"):
                piece = weight_piece(me["y"], *quarter(chunk, part, me[axis]))
                copies.start(piece, piece, moved(me, "y", k))

    to_partner = {}
    set_off(0)
    tiny_copies = [
        copies.start(tiny_ref, tiny_land.at[own], place) for place in [partner] + peers["y"] + across
    ]
    for chunk in range(3):
        piece = weight_piece(me["y"], chunk * span, span)
        to_partner["own", chunk] = copies.start(piece, piece, partner)
    tiny_land[own] = tiny_ref[...]

    steps = [2 - pipe, 1 + 2 * pipe, 3 - pipe]
    seconds = {}

    def pass_on(chunk, slots):
        for slot in slots:
            y = (me["y"] - steps[slot] + 4) % 4
            for part, axis in enumerate("xz"):
                piece = weight_piece(y, *quarter(chunk, part, me[axis]))
                index = first_base[chunk] + (steps[slot] - 1) * 2 + part
                pltpu.make_async_remote_copy(
                    src_ref=piece, dst_ref=piece, send_sem=send_sem.at[index],
                    recv_sem=recv_sem.at[index], device_id=device_at(partner), device_id_type=MESH,
                ).wait_recv()
                for j in (1, 3, 2):
                    seconds[chunk, slot, part, j] = copies.start(piece, piece, moved(me, axis, j))

    def hand_over(chunk, slots):
        for slot in slots:
            y = (me["y"] - steps[slot] + 4) % 4
            for part in range(2):
                for j in (1, 3, 2):
                    seconds[chunk, slot, part, j].wait_recv()
            piece = weight_piece(y, chunk * span, span)
            to_partner[slot, chunk] = copies.start(piece, piece, partner)

    def arrived(chunk, slots):
        for slot in slots:
            to_partner[slot, chunk].wait_recv()

    set_off(1)
    pass_on(0, (0, 1))
    set_off(2)
    for copy in tiny_copies:
        copy.wait_recv()
    qbias_ref[...] = jnp.zeros_like(qbias_ref)
    for layer in range(2):
        for shard in range(4):
            rows = tiny_land[layer * 4 + shard]
            small_ref[layer, :, shard * 128 : (shard + 1) * 128] = rows[0:8, 0:128]
            for j in range(4):
                at = shard * 512 + j * 128
                hbias_ref[layer, :, at : at + 128] = rows[8 + j : 9 + j, 0:128]
                head = layer * 16 + shard * 4 + j
                tables_ref[head : head + 1] = rows[16 + j : 17 + j]
        qbias_ref[layer, :, 0:D] = small_ref[layer, 4:5]
        qbias_ref[layer, :, 2 * D : 3 * D] = small_ref[layer, 5:6]
    table_rows_of(tables_ref, places_ref, rel_ref)
    pass_on(1, (0, 1))
    hand_over(0, (0, 1))
    pass_on(2, (0, 1))
    arrived(0, ("own", 0, 1))

    def params(layer):
        return (
            w_ref.at[pl.ds(layer * D, D)], small_ref.at[layer], qbias_ref.at[layer], hbias_ref.at[layer],
            rel_ref.at[pl.ds(layer * 16, 16)], mask_ref.at[layer],
        )

    def saved(layer):
        return tuple(ref.at[layer] for ref in (qkv_ref, o_ref, r_ref, act_ref, slope_ref))

    def in_token_order(layer, value, out, turned):
        for b in range(IMGS):
            own_rows = value[b * IMG_ROWS : (b + 1) * IMG_ROWS]
            out[b] = dot(back_ref[layer], own_rows).astype(BF16)
            if turned is not None:
                turned[b * IMG_ROWS : (b + 1) * IMG_ROWS] = dot(turn_ref[layer], own_rows).astype(BF16)

    def after_attend0():
        hand_over(2, (0, 1))
        for chunk in range(3):
            pass_on(chunk, (2,))

    def before_mlp0():
        arrived(1, ("own", 0, 1))
        arrived(2, ("own", 0, 1))

    def after_qkv1():
        hand_over(1, (2,))
        hand_over(2, (2,))

    def before_mlp1():
        arrived(1, (2,))
        arrived(2, (2,))

    y0 = forward_body(
        params(0), saved(0), x_ref.at[0], low_ref, du_ref, after_qkv=lambda: hand_over(1, (0, 1)),
        after_attend=after_attend0, before_mlp=before_mlp0,
    )
    hand_over(0, (2,))
    in_token_order(0, y0, y_ref.at[0], x_ref.at[1])
    arrived(0, (2,))
    y1 = forward_body(
        params(1), saved(1), x_ref.at[1], low_ref, du_ref, after_qkv=after_qkv1, before_mlp=before_mlp1
    )
    in_token_order(1, y1, y_ref.at[1], None)
    neighbour = {**me, "y": me["y"] + 1 - 2 * pipe}
    y_copy = copies.start(y_ref.at[1 - pipe], y_land, neighbour)
    keep_out = pltpu.make_async_copy(y_ref.at[pipe], y_hbm.at[pl.ds(pipe * IMGS, IMGS)], local_sem.at[0])
    keep_out.start()

    core_copies, sent, regions = {}, {}, {}

    def send_core(layer, streams, begin=0, end=PACKED):
        for t in streams:
            lo, hi = max(STREAMS[t][0], begin), min(STREAMS[t][1], end)
            core_copies.setdefault((layer, t), []).append(
                copies.start(g_ref.at[layer, :, 1 - me["core"], :, lo:hi], core_ref.at[:, :, lo:hi], partner)
            )

    def add_core(layer, streams):
        for t in streams:
            lo, hi, _ = STREAMS[t]
            for copy in core_copies[layer, t]:
                copy.wait_recv()

            def one(n, _, lo=lo, hi=hi):
                half, rows = n // 4, pl.ds(pl.multiple_of((n % 4) * 32, 32), 32)
                mine = (layer, half, me["core"], rows, slice(lo, hi))
                total = g_ref[mine].astype(F32) + core_ref[half, rows, lo:hi].astype(F32)
                g_ref[mine] = total.astype(BF16)
                return 0

            lax.fori_loop(0, 8, one, 0)
            regions[layer, t] = ((0, 128), (lo, hi - lo))

    def send(layer, streams, stage):
        for t in streams:
            axis = STREAMS[t][2][stage]
            land = (land_a, land_b)[stage][t]
            region = regions[layer, t]
            sent[layer, t] = [
                copies.start(
                    g_ref.at[(layer, slice(None), me["core"]) + piece_of(cut(region, axis, (me[axis] + k) % 4))],
                    land.at[layer, k - 1], moved(me, axis, k),
                )
                for k in (1, 3, 2)
            ]
            regions[layer, t] = cut(region, axis, me[axis])

    def add(layer, streams, stage):
        for t in streams:
            for copy in sent[layer, t]:
                copy.wait_recv()
            land = (land_a, land_b)[stage][t]
            (r0, nr), cols = regions[layer, t]
            steps_of = nr // 32

            def one(n, _, land=land, r0=r0, cols=cols, steps_of=steps_of):
                half, row = n // steps_of, pl.multiple_of((n % steps_of) * 32, 32)
                at = (layer, half, me["core"], pl.ds(pl.multiple_of(r0 + row, 32), 32), pl.ds(*cols))
                total = g_ref[at].astype(F32)
                for k in range(3):
                    total = total + land[layer, k, half, pl.ds(row, 32), :].astype(F32)
                g_ref[at] = total.astype(BF16)
                return 0

            lax.fori_loop(0, 2 * steps_of, one, 0)

    def send_y(streams):
        for t in streams:
            piece = piece_of(regions[0, t])
            sent["y", t] = []
            for k in (1, 3, 2):
                to = (me["y"] + k) % 4
                sent["y", t].append(
                    copies.start(
                        g_ref.at[(to % 2, to // 2, me["core"]) + piece], land_y[t].at[k - 1], moved(me, "y", k)
                    )
                )

    def add_y(streams):
        for t in streams:
            for copy in sent["y", t]:
                copy.wait_recv()
            piece = piece_of(regions[0, t])
            total = g_ref[(pipe, me["y"] // 2, me["core"]) + piece].astype(F32)
            for k in range(3):
                total = total + land_y[t][k].astype(F32)
            fin_ref[piece] = total.astype(BF16)

    def spread(streams, level):
        for t in streams:
            if level == 1:
                for copy in sent["fin", t]:
                    copy.wait_recv()
            lo, hi, order = STREAMS[t]
            part = (hi - lo) // 4
            rows = pl.ds(pl.multiple_of(me["z"] * 32, 32), 32)
            cols = pl.ds(pl.multiple_of(lo + me["x"] * part, 128), part)
            if level == 1:
                if order[0] == "x":
                    cols = pl.ds(lo, hi - lo)
                else:
                    rows = pl.ds(0, 128)
            piece = fin_ref.at[rows, cols]
            sent["fin", t] = [copies.start(piece, piece, moved(me, order[level], k)) for k in (1, 3, 2)]

    late = LATE
    early = tuple(t for t in range(len(STREAMS)) if t not in late)

    def results(layer):
        return (g_ref.at[layer], gsmall_ref.at[layer], ghidden_ref.at[layer], gbias_ref.at[pl.ds(layer * 16, 16)])

    scratch = (low_ref, turned_ref, du_ref, dqkv_ref, do_ref)

    def after_mlp1():
        send_core(1, (1,))
        send_core(1, (0,), begin=UP0)

    def after_proj1():
        send_core(1, (0,), end=UP0)
        add_core(1, (1,))
        send(1, (1,), 0)

    def before_attend1():
        add_core(1, (0,))
        send(1, (0,), 0)

    dx1 = backward_body(
        params(1), saved(1), x_ref.at[1], dy_ref, results(1), scratch,
        after_mlp=after_mlp1, after_proj=after_proj1,
        before_attend=before_attend1, after_weights=lambda: send_core(1, late),
    )
    in_token_order(1, dx1, dx_ref.at[1], dy_ref)
    add_core(1, late)
    pl.semaphore_signal(free_sem, inc=1, device_id=device_at(partner), device_id_type=MESH)
    send(1, late, 0)

    def in_mlp0():
        add(1, (1, 0), 0)
        send(1, (1, 0), 1)

    def after_mlp0():
        pl.semaphore_wait(free_sem, 1)
        send_core(0, (1,))
        send_core(0, (0,), begin=UP0)

    def after_proj0():
        send_core(0, (0,), end=UP0)
        add_core(0, (1,))
        send(0, (1,), 0)

    def before_attend0():
        add_core(0, (0,))
        send(0, (0,), 0)

    def after_attend0():
        add(1, early, 1)
        add(1, late, 0)
        send(1, late, 1)

    def after_weights0():
        send_core(0, late)
        add(0, (1,), 0)
        send(0, (1,), 1)

    dx0 = backward_body(
        params(0), saved(0), x_ref.at[0], dy_ref, results(0), scratch,
        in_mlp=in_mlp0, after_mlp=after_mlp0, after_proj=after_proj0,
        before_attend=before_attend0, after_attend=after_attend0, after_weights=after_weights0,
    )
    add_core(0, late)
    send(0, late, 0)
    in_token_order(0, dx0, dx_ref.at[0], None)
    dx_copy = copies.start(dx_ref.at[1 - pipe], dx_land, neighbour)
    dx_keep = pltpu.make_async_copy(dx_ref.at[pipe], dx_hbm.at[pl.ds(pipe * IMGS, IMGS)], local_sem.at[1])
    dx_keep.start()
    add(0, (0,), 0)
    send(0, (0,), 1)

    add(0, (1,), 1)
    send_y((1,))
    gtable = table_sums(gbias_ref, places_ref)
    for layer in range(2):
        for shard in range(4):
            half, core = shard // 2, shard % 2
            y = half * 2 + layer
            sums_in[core, y] = jnp.zeros((SMALL_ROWS, RELS_PAD), F32)
            sums_in[core, y, 0:8, 0:128] = gsmall_ref[layer, :, shard * 128 : (shard + 1) * 128]
            for j in range(4):
                at = shard * 512 + j * 128
                sums_in[core, y, 8 + j : 9 + j, 0:128] = ghidden_ref[layer, :, at : at + 128]
            sums_in[core, y, 16:20] = gtable[layer * 16 + shard * 4 : layer * 16 + shard * 4 + 4]
    small_copy = copies.start(sums_in.at[1 - me["core"]], sums_core, partner)
    add(0, late, 0)
    send(0, late, 1)
    add(0, (0,), 1)
    send_y((0,))
    add(1, late, 1)
    add_y((1,))
    spread((1,), 0)
    small_copy.wait_recv()
    sums_own[0] = sums_in[me["core"]] + sums_core[...]
    small_sent = [
        copies.start(sums_own.at[0, (me["y"] + k) % 4], sums_land.at[0, k - 1], moved(me, "y", k))
        for k in (1, 3, 2)
    ]

    def add_small(stage):
        for copy in small_sent:
            copy.wait_recv()
        start = sums_own[0, me["y"]] if stage == 0 else sums_own[stage, 0]
        return start + sums_land[stage, 0] + sums_land[stage, 1] + sums_land[stage, 2]

    add_y((0,))
    spread((0,), 0)
    add(0, late, 1)
    send_y(late)
    for stage, axis in enumerate("xz", 1):
        sums_own[stage, 0] = add_small(stage - 1)
        small_sent = [
            copies.start(sums_own.at[stage, 0], sums_land.at[stage, k - 1], moved(me, axis, k))
            for k in (1, 3, 2)
        ]
        if stage == 1:
            spread(early, 1)
            add_y(late)
            spread(late, 0)
    spread(late, 1)
    sums_ref[...] = add_small(2)
    outs = []
    y_copy.wait_recv()
    dx_copy.wait_recv()
    for n, (src, dst) in enumerate(((y_land, y_hbm), (dx_land, dx_hbm)), 2):
        out = pltpu.make_async_copy(src, dst.at[pl.ds((1 - pipe) * IMGS, IMGS)], local_sem.at[n])
        out.start()
        outs.append(out)
    for t in early + late:
        for copy in sent["fin", t]:
            copy.wait_recv()
    grad_out = pltpu.make_async_copy(fin_ref, grad_hbm, local_sem.at[4])
    grad_out.start()
    for copy in [keep_out, dx_keep, grad_out] + outs:
        copy.wait()
    copies.finish()


def land_shapes(stage):
    shapes = []
    for lo, hi, order in STREAMS:
        done = order[: stage + 1]
        shape = (2, 3, 2, 32 if "z" in done else 128, (hi - lo) // (4 if "x" in done else 1))
        shapes.append(pltpu.VMEM(shape, BF16))
    return tuple(shapes)


def train(slots, images, cotangent, qkv, proj, up, down, tiny, places, mask, order, back, turn):
    anywhere = pl.BlockSpec(memory_space=pl.ANY)
    vmem = pl.BlockSpec(memory_space=pltpu.VMEM)
    tokens = (2 * IMGS, OUT_ROWS, D)
    half = (IMGS, OUT_ROWS, D)
    piece = (SMALL_ROWS, RELS_PAD)
    low = pltpu.VMEM((ROWS, D), BF16)
    return pl.pallas_call(
        train_kernel,
        out_shape=[
            jax.ShapeDtypeStruct(tokens, BF16), jax.ShapeDtypeStruct(tokens, BF16),
            jax.ShapeDtypeStruct((128, PACKED), BF16), jax.ShapeDtypeStruct(piece, F32),
        ],
        in_specs=[pl.BlockSpec(memory_space=pltpu.SMEM), vmem] + [anywhere] * 5 + [vmem] * 6,
        out_specs=[anywhere] * 3 + [vmem],
        scratch_shapes=[
            pltpu.VMEM((2 * D, PACKED), BF16),
            pltpu.VMEM((2, ROWS, D), BF16),
            pltpu.VMEM((2, KROWS, 3 * D), BF16),
            pltpu.VMEM((2, ROWS, D), BF16),
            pltpu.VMEM((2, ROWS, D), F32),
            pltpu.VMEM((2, ROWS, FF), BF16),
            pltpu.VMEM((2, ROWS, FF), BF16),
            pltpu.VMEM((2, 2, 2, 128, PACKED), BF16),
            pltpu.VMEM((2, 128, PACKED), BF16),
            land_shapes(0), land_shapes(1),
            tuple(pltpu.VMEM((3, 32, (hi - lo) // 4), BF16) for lo, hi, _ in STREAMS),
            pltpu.VMEM((128, PACKED), BF16),
            pltpu.VMEM((32, PAIR, KEYS), F32),
            pltpu.VMEM((32, PAIR, KEYS), F32),
            low,
            pltpu.VMEM((D, ROWS), BF16),
            pltpu.VMEM((ROWS, D), F32),
            pltpu.VMEM((ROWS, 3 * D), BF16),
            low,
            low,
            pltpu.VMEM((IMGS, TOK, D), BF16),
            pltpu.VMEM((2,) + half, BF16),
            pltpu.VMEM(half, BF16),
            pltpu.VMEM((2,) + half, BF16),
            pltpu.VMEM(half, BF16),
            pltpu.VMEM((8, TINY_ROWS, RELS_PAD), F32),
            pltpu.VMEM((32, RELS_PAD), F32),
            pltpu.VMEM((2, 8, D), F32),
            pltpu.VMEM((2, 1, 3 * D), F32),
            pltpu.VMEM((2, 1, FF), F32),
            pltpu.VMEM((2, 8, D), F32),
            pltpu.VMEM((2, 1, FF), F32),
            pltpu.VMEM((2, 4) + piece, F32),
            pltpu.VMEM((4,) + piece, F32),
            pltpu.VMEM((3, 4) + piece, F32),
            pltpu.VMEM((3, 3) + piece, F32),
            pltpu.SemaphoreType.DMA((COPIES,)),
            pltpu.SemaphoreType.DMA((COPIES,)),
            pltpu.SemaphoreType.DMA((8,)),
            pltpu.SemaphoreType.REGULAR,
        ],
        compiler_params=pltpu.CompilerParams(
            collective_id=1, has_side_effects=True, vmem_limit_bytes=VMEM_LIMIT
        ),
        cost_estimate=pl.CostEstimate(
            flops=12 * ROWS * D * PACKED, bytes_accessed=16 << 20, transcendentals=6 * ROWS * FF
        ),
        name="train_layers",
    )(slots, images, cotangent, qkv, proj, up, down, tiny, places, mask, order, back, turn)


def block_pair(blocks, fill):
    lead = blocks.shape[:-3]
    none = [(0, 0)] * len(lead)
    pad_rows = [(0, WPAD - WTOK)]
    first = jnp.pad(blocks[..., 0, :, :], none + pad_rows + [(0, KEYS - WTOK)], constant_values=fill)
    second = jnp.pad(
        blocks[..., 1, :, :], none + pad_rows + [(WPAD, KEYS - WTOK - WPAD)], constant_values=fill
    )
    return jnp.concatenate([first, second], axis=-2)


def inside_blocks():
    rows, cols = np.arange(PAIR)[:, None] // WPAD, np.arange(KEYS)[None, :]
    return (cols // WPAD == rows) & (cols % WPAD < WTOK) & (cols < PAIR)


def on_device(
    images, cotangent, micro_order, region_ids, rel_index, qkv_weight, proj_weight, up_weight,
    down_weight, bias_table, norm_gains, offsets, hidden_bias,
):
    first_section = lax.axis_index("pipe") == 0
    table_rows = bias_table.shape[1]

    def lanes(block, rows):
        return jnp.pad(
            block.astype(F32), ((0, rows - block.shape[0]), (0, RELS_PAD - block.shape[1]))
        )

    tiny = jnp.concatenate(
        [
            lanes(jnp.concatenate([norm_gains[0], offsets[0]]), 8),
            lanes(hidden_bias[0].reshape(4, 128), 8),
            lanes(bias_table[0].T, 8),
        ]
    )
    places = jnp.pad(rel_index, ((0, WPAD - WTOK), (0, KEYS - WTOK)), constant_values=-1)
    regions = region_ids.reshape(2, WIN, 2, WIN).transpose(0, 2, 1, 3).reshape(2, 2, WTOK)
    regions = jnp.pad(regions, ((0, 0), (0, 0), (0, WPAD - WTOK))).reshape(2, PAIR)
    queries = regions[:, :, None]
    keys = jnp.pad(regions, ((0, 0), (0, KEYS - PAIR)))[:, None, :]
    inside = inside_blocks()
    mask0 = np.broadcast_to(np.where(inside, 0.0, BLOCKED), (2, PAIR, KEYS)).astype(np.float32)
    mask1 = jnp.where(inside[None], jnp.where(queries == keys, 0.0, -1e9), BLOCKED).astype(F32)
    mask = jnp.stack([jnp.asarray(mask0), mask1])
    order = jnp.asarray(np.stack([order_matrix(0), order_matrix(SHIFT)]), BF16)
    back = jnp.asarray(np.stack([back_matrix(0), back_matrix(SHIFT)]), BF16)
    turn = jnp.asarray(np.stack([turn_matrix(0, SHIFT), turn_matrix(SHIFT, 0)]), BF16)
    slot_order = micro_order[0]

    layer_out, dx_slots, share, sums = train(
        slot_order, images, cotangent, qkv_weight, proj_weight, up_weight, down_weight, tiny, places,
        mask, order, back, turn,
    )
    slots = jnp.arange(2 * IMGS, dtype=jnp.int32)
    inverse = jnp.sum(jnp.where(slot_order[:, None] == slots[None, :], slots[:, None], 0), axis=0)
    picks = jnp.where(first_section, inverse, slots)
    input_grad = jnp.take(dx_slots[:, :TOK], picks, axis=0, mode="clip").astype(F32)
    down = jnp.concatenate(
        [share[:, DOWN0 + k * D : DOWN0 + (k + 1) * D] for k in range(4)], axis=0
    )
    return (
        layer_out[None, :, :TOK],
        input_grad[None],
        share[None, :, QKV0:PROJ0].astype(F32),
        share[None, :, PROJ0:UP0].astype(F32),
        share[None, :, UP0:DOWN0].astype(F32),
        down[None].astype(F32),
        sums[16:20, :table_rows].T[None],
        sums[None, 0:2, 0:128],
        sums[None, 2:8, 0:128],
        sums[8:12, 0:128].reshape(1, D),
    )


def solution(mesh):
    rows = P(("shard", "rep"), None, None)
    split = P("pipe", "shard", None)
    lanes = P("pipe", None, "shard")
    return jax.shard_map(
        on_device,
        mesh=mesh,
        in_specs=(
            rows, rows, P(("shard", "rep"), None), P(), P(),
            split, split, split, split, lanes, lanes, lanes, P("pipe", "shard"),
        ),
        out_specs=(
            P("pipe", ("shard", "rep"), None, None), P("pipe", ("shard", "rep"), None, None),
            split, split, split, split, lanes, lanes, lanes, P("pipe", "shard"),
        ),
        check_vma=False,
    )
```

```python
import functools
import math

import jax
import jax.numpy as jnp
import numpy as np
from jax import lax
from jax.experimental import pallas as pl
from jax.experimental.pallas import tpu as pltpu
from jax.sharding import PartitionSpec as P

SIDE = 14
WIN = 7
SHIFT = 3
D = 512
FF = 2048
HEAD = 32
TOK = SIDE * SIDE
WTOK = WIN * WIN
WPAD = 56
PAIR = 2 * WPAD
IMG_ROWS = 4 * WPAD
IMGS = 2
ROWS = IMGS * IMG_ROWS
PAIRS = ROWS // PAIR
KEYS = 128
KROWS = ROWS + KEYS - PAIR
OUT_ROWS = 208
RELS_PAD = 256
QKV0, PROJ0, UP0, DOWN0, PACKED = 0, 1536, 2048, 4096, 6144
CHUNK = 256
SCALE = HEAD ** (-0.5)
BLOCKED = -1e30
VMEM_LIMIT = 64 * 1024 * 1024 - 1024
BF16 = jnp.bfloat16
F32 = jnp.float32


def window_places(shift):
    place = np.zeros((TOK,), np.int64)
    for wr in range(2):
        for wc in range(2):
            for i in range(WIN):
                for j in range(WIN):
                    a = (wr * WIN + i + shift) % SIDE
                    b = (wc * WIN + j + shift) % SIDE
                    place[a * SIDE + b] = (wr * 2 + wc) * WPAD + i * WIN + j
    return place


def order_matrix(shift):
    matrix = np.zeros((IMG_ROWS, TOK), np.float32)
    matrix[window_places(shift), np.arange(TOK)] = 1.0
    return matrix


def back_matrix(shift):
    matrix = np.zeros((OUT_ROWS, IMG_ROWS), np.float32)
    matrix[:TOK] = order_matrix(shift).T
    return matrix


def turn_matrix(from_shift, to_shift):
    return order_matrix(to_shift) @ order_matrix(from_shift).T


def dot(a, b, dims=((1,), (0,))):
    return lax.dot_general(a, b, (dims, ((), ())), preferred_element_type=F32)


def normalised(x):
    mean = jnp.mean(x, -1, keepdims=True)
    centred = x - mean
    rstd = lax.rsqrt(jnp.mean(centred * centred, -1, keepdims=True) + 1e-5)
    return centred * rstd, rstd


def head_masks(rows):
    lane = lax.broadcasted_iota(jnp.int32, (rows, 128), 1) // HEAD
    return [lane == h for h in range(4)]


def spread_heads(block, masks):
    zero = jnp.zeros_like(block)
    return jnp.concatenate([jnp.where(m, block, zero) for m in masks], axis=0)


def join_heads(stacked, masks):
    total = None
    for h, m in enumerate(masks):
        part = jnp.where(m, stacked[h * PAIR : (h + 1) * PAIR], 0.0)
        total = part if total is None else total + part
    return total


def probabilities(q4, k, rel_ref, mask_ref, i, g):
    s = dot(q4, k, ((1,), (1,))) * SCALE
    bias = rel_ref[pl.ds(g * 4, 4)].astype(F32) + mask_ref[lax.rem(i, 2)][None]
    s = s + bias.reshape(4 * PAIR, KEYS)
    e = jnp.exp(s - jnp.max(s, -1, keepdims=True))
    return e * (1.0 / jnp.sum(e, -1, keepdims=True))


def down_chunk(w_ref, c):
    row = pl.multiple_of((c // 2) * 128, 128)
    col = pl.multiple_of(DOWN0 + (c % 2) * 1024, 128)
    first = w_ref[pl.ds(row, 128), pl.ds(col, D)]
    second = w_ref[pl.ds(row, 128), pl.ds(col + D, D)]
    return jnp.concatenate([first, second], axis=0)


MESH = pl.DeviceIdType.MESH
STREAMS = ((1536, 4096, "xz"), (4096, 6144, "zx"), (0, 512, "xz"), (512, 1536, "zx"))
LATE = (2, 3)
TINY_ROWS = 24
SMALL_ROWS = 24


def here():
    pipe, shard, rep = lax.axis_index("pipe"), lax.axis_index("shard"), lax.axis_index("rep")
    return {"y": (shard // 2) * 2 + pipe, "core": shard % 2, "z": rep // 4, "x": rep % 4}


def device_at(place):
    return {
        "pipe": place["y"] % 2,
        "shard": (place["y"] // 2) * 2 + place["core"],
        "rep": place["z"] * 4 + place["x"],
    }


def moved(place, axis, steps):
    size = 2 if axis == "core" else 4
    return {**place, axis: (place[axis] + steps) % size}


def block_index(y, core):
    return (y % 2) * 4 + (y // 2) * 2 + core


class Copies:
    def __init__(self, send_sem, recv_sem):
        self.send_sem, self.recv_sem, self.count, self.started = send_sem, recv_sem, 0, []

    def start(self, src, dst, place):
        copy = pltpu.make_async_remote_copy(
            src_ref=src, dst_ref=dst, send_sem=self.send_sem.at[self.count],
            recv_sem=self.recv_sem.at[self.count], device_id=device_at(place), device_id_type=MESH,
        )
        copy.start()
        self.count += 1
        self.started.append(copy)
        return copy

    def finish(self):
        for copy in self.started:
            copy.wait_send()


def greet(places, meanwhile):
    barrier = pltpu.get_barrier_semaphore()
    for place in places:
        pl.semaphore_signal(barrier, inc=1, device_id=device_at(place), device_id_type=MESH)
    meanwhile()
    pl.semaphore_wait(barrier, len(places))


def nothing():
    pass


def forward_body(
    params, saved, x_ref, low_ref, acc_ref, after_qkv=nothing, after_attend=nothing, before_mlp=nothing
):
    w_ref, small_ref, qbias_ref, hbias_ref, rel_ref, mask_ref = params
    qkv_ref, o_ref, r_ref, act_ref, slope_ref = saved
    n1, _ = normalised(x_ref[...].astype(F32))
    low_ref[...] = (n1 * small_ref[0:1] + small_ref[2:3]).astype(BF16)
    qkv_ref[ROWS:, :] = jnp.zeros((KROWS - ROWS, 3 * D), BF16)

    def qkv_step(n, _):
        cols = pl.ds(pl.multiple_of(n * CHUNK, CHUNK), CHUNK)
        part = dot(low_ref[...], w_ref[:, cols]) + qbias_ref[:, cols]
        qkv_ref[0:ROWS, cols] = part.astype(BF16)
        return 0

    lax.fori_loop(0, 3 * D // CHUNK, qkv_step, 0)
    after_qkv()
    masks = head_masks(PAIR)

    def attend(i, _):
        rows = pl.ds(pl.multiple_of(i * PAIR, 16), PAIR)
        keys = pl.ds(pl.multiple_of(i * PAIR, 16), KEYS)
        for g in range(4):
            q = qkv_ref[rows, g * 128 : (g + 1) * 128]
            k = qkv_ref[keys, D + g * 128 : D + (g + 1) * 128]
            v = qkv_ref[keys, 2 * D + g * 128 : 2 * D + (g + 1) * 128]
            p = probabilities(spread_heads(q, masks), k, rel_ref, mask_ref, i, g)
            o4 = dot(p.astype(BF16), v)
            o_ref[rows, g * 128 : (g + 1) * 128] = join_heads(o4, masks).astype(BF16)
        return 0

    lax.fori_loop(0, PAIRS, attend, 0)
    after_attend()
    for n in range(D // CHUNK):
        cols = slice(n * CHUNK, (n + 1) * CHUNK)
        part = dot(o_ref[...], w_ref[:, PROJ0 + n * CHUNK : PROJ0 + (n + 1) * CHUNK])
        r_ref[:, cols] = x_ref[:, cols].astype(F32) + part + small_ref[6:7, cols]
    r = r_ref[...]
    n2, _ = normalised(r)
    low_ref[...] = (n2 * small_ref[1:2] + small_ref[3:4]).astype(BF16)
    acc_ref[...] = r + small_ref[7:8]
    before_mlp()

    def mlp(c, _):
        cols = pl.ds(pl.multiple_of(c * CHUNK, CHUNK), CHUNK)
        up = w_ref[:, pl.ds(pl.multiple_of(UP0 + c * CHUNK, CHUNK), CHUNK)]
        hid = dot(low_ref[...], up) + hbias_ref[:, cols]
        cdf = 0.5 * (1.0 + lax.erf(hid * math.sqrt(0.5)))
        act = (hid * cdf).astype(BF16)
        act_ref[:, cols] = act
        density = jnp.exp(-0.5 * hid * hid) * (1.0 / math.sqrt(2.0 * math.pi))
        slope_ref[:, cols] = (cdf + hid * density).astype(BF16)
        acc_ref[...] += dot(act, down_chunk(w_ref, c))
        return 0

    lax.fori_loop(0, FF // CHUNK, mlp, 0)
    return acc_ref[...].astype(BF16)


def backward_body(
    params, saved, x_ref, dy_ref, results, scratch,
    in_mlp=nothing, after_mlp=nothing, after_proj=nothing, before_attend=nothing, after_attend=nothing,
    after_weights=nothing,
):
    w_ref, small_ref, _, _, rel_ref, mask_ref = params
    qkv_ref, o_ref, r_ref, act_ref, slope_ref = saved
    g_ref, gsmall_ref, ghidden_ref, gbias_ref = results
    low_ref, turned_ref, du_ref, dqkv_ref, do_ref = scratch

    def put(cols, value):
        for b in range(4):
            g_ref[b // 2, b % 2, :, cols] = value[b * 128 : (b + 1) * 128]

    n2, rstd2 = normalised(r_ref[...])
    turned_ref[...] = (n2 * small_ref[1:2] + small_ref[3:4]).T.astype(BF16)
    du_ref[...] = jnp.zeros_like(du_ref)

    def mlp(c, _):
        cols = pl.ds(pl.multiple_of(c * CHUNK, CHUNK), CHUNK)
        up_cols = pl.ds(pl.multiple_of(UP0 + c * CHUNK, CHUNK), CHUNK)
        dy = dy_ref[...]
        dact = dot(dy, down_chunk(w_ref, c), ((1,), (1,)))
        dhid = (dact * slope_ref[:, cols].astype(F32)).astype(BF16)
        ghidden_ref[:, cols] = jnp.sum(dhid.astype(F32), 0, keepdims=True)
        down = dot(act_ref[:, cols], dy, ((0,), (0,))).astype(BF16)
        block = c // 2
        col = pl.multiple_of(DOWN0 + (c % 2) * 1024, 128)
        g_ref[block // 2, block % 2, :, pl.ds(col, D)] = down[:128]
        g_ref[block // 2, block % 2, :, pl.ds(col + D, D)] = down[128:]
        put(up_cols, dot(turned_ref[...], dhid).astype(BF16))
        du_ref[...] += dot(dhid, w_ref[:, up_cols], ((1,), (1,)))
        return 0

    lax.fori_loop(0, FF // CHUNK // 2, mlp, 0)
    in_mlp()
    lax.fori_loop(FF // CHUNK // 2, FF // CHUNK, mlp, 0)
    after_mlp()
    dy = dy_ref[...].astype(F32)
    du2 = du_ref[...]
    n2, rstd2 = normalised(r_ref[...])
    z = du2 * small_ref[1:2]
    zm = jnp.mean(z, -1, keepdims=True)
    zn = jnp.mean(z * n2, -1, keepdims=True)
    dr = dy + rstd2 * (z - zm - n2 * zn)
    db = dr.astype(BF16)
    low_ref[...] = db
    gsmall_ref[1:2] = jnp.sum(du2 * n2, 0, keepdims=True)
    gsmall_ref[3:4] = jnp.sum(du2, 0, keepdims=True)
    gsmall_ref[6:7] = jnp.sum(db.astype(F32), 0, keepdims=True)
    gsmall_ref[7:8] = jnp.sum(dy, 0, keepdims=True)
    du_ref[...] = dr
    turned_ref[...] = o_ref[...].astype(F32).T.astype(BF16)
    for n in range(D // CHUNK):
        cols = slice(n * CHUNK, (n + 1) * CHUNK)
        put(
            slice(PROJ0 + n * CHUNK, PROJ0 + (n + 1) * CHUNK),
            dot(turned_ref[...], low_ref[:, cols]).astype(BF16),
        )
    after_proj()
    for n in range(D // CHUNK):
        cols = slice(n * CHUNK, (n + 1) * CHUNK)
        rows_of = w_ref[n * CHUNK : (n + 1) * CHUNK, PROJ0 : PROJ0 + D]
        do_ref[:, cols] = dot(low_ref[...], rows_of, ((1,), (1,))).astype(BF16)
    before_attend()
    gbias_ref[...] = jnp.zeros_like(gbias_ref)
    masks = head_masks(PAIR)

    def attend(i, _):
        rows = pl.ds(pl.multiple_of(i * PAIR, 16), PAIR)
        keys = pl.ds(pl.multiple_of(i * PAIR, 16), KEYS)
        for g in range(4):
            here = slice(g * 128, (g + 1) * 128)
            k = qkv_ref[keys, D + g * 128 : D + (g + 1) * 128]
            v = qkv_ref[keys, 2 * D + g * 128 : 2 * D + (g + 1) * 128]
            q4 = spread_heads(qkv_ref[rows, here], masks)
            do4 = spread_heads(do_ref[rows, here], masks)
            p = probabilities(q4, k, rel_ref, mask_ref, i, g)
            dp = dot(do4, v, ((1,), (1,)))
            ds = (p * (dp - jnp.sum(dp * p, -1, keepdims=True))).astype(BF16)
            gbias_ref[g * 4 : (g + 1) * 4] += ds.astype(F32).reshape(4, PAIR, KEYS)
            dq = join_heads(dot(ds, k), masks) * SCALE
            dk = dot(ds, q4, ((0,), (0,))) * SCALE
            dv = dot(p.astype(BF16), do4, ((0,), (0,)))
            dqkv_ref[rows, here] = dq.astype(BF16)
            dqkv_ref[rows, D + g * 128 : D + (g + 1) * 128] = dk[:PAIR].astype(BF16)
            dqkv_ref[rows, 2 * D + g * 128 : 2 * D + (g + 1) * 128] = dv[:PAIR].astype(BF16)
        return 0

    lax.fori_loop(0, PAIRS, attend, 0)
    after_attend()
    n1, rstd1 = normalised(x_ref[...].astype(F32))
    turned_ref[...] = (n1 * small_ref[0:1] + small_ref[2:3]).T.astype(BF16)

    def qkv_step(n, _):
        cols = pl.ds(pl.multiple_of(n * CHUNK, CHUNK), CHUNK)
        put(cols, dot(turned_ref[...], dqkv_ref[:, cols]).astype(BF16))
        return 0

    lax.fori_loop(0, 3 * D // CHUNK, qkv_step, 0)
    after_weights()
    gsmall_ref[4:5] = jnp.sum(dqkv_ref[:, 0:D].astype(F32), 0, keepdims=True)
    gsmall_ref[5:6] = jnp.sum(dqkv_ref[:, 2 * D : 3 * D].astype(F32), 0, keepdims=True)
    du = dot(dqkv_ref[...], w_ref[:, QKV0 : QKV0 + 3 * D], ((1,), (1,)))
    n1, rstd1 = normalised(x_ref[...].astype(F32))
    gsmall_ref[0:1] = jnp.sum(du * n1, 0, keepdims=True)
    gsmall_ref[2:3] = jnp.sum(du, 0, keepdims=True)
    z = du * small_ref[0:1]
    zm = jnp.mean(z, -1, keepdims=True)
    zn = jnp.mean(z * n1, -1, keepdims=True)
    return (du_ref[...] + rstd1 * (z - zm - n1 * zn)).astype(BF16)


def table_rows_of(tables_ref, places_ref, rel_ref):
    rel_ref[...] = jnp.zeros_like(rel_ref)
    entry = lax.broadcasted_iota(jnp.int32, (RELS_PAD, KEYS), 0)
    tables = tables_ref[...].astype(BF16)

    def rows(n, _):
        for step in range(WIN):
            i = n * WIN + step
            hot = jnp.where(entry == places_ref[pl.ds(i, 1), :], 1.0, 0.0).astype(BF16)
            values = dot(tables, hot)
            rel_ref[:, i, :] = values
            rel_ref[:, i + WPAD, :] = pltpu.roll(values, WPAD, 1)
        return 0

    lax.fori_loop(0, WIN, rows, 0)


def table_sums(gbias_ref, places_ref):
    second = gbias_ref[:, WPAD:PAIR].reshape(32 * WPAD, KEYS)
    gbias_ref[:, 0:WPAD] += pltpu.roll(second, KEYS - WPAD, 1).reshape(32, WPAD, KEYS)
    entry = lax.broadcasted_iota(jnp.int32, (RELS_PAD, KEYS), 0)

    def rows(n, total):
        parts = []
        for step in range(WIN):
            i = n * WIN + step
            values = gbias_ref[:, i, :]
            high = values.astype(BF16)
            low = (values - high.astype(F32)).astype(BF16)
            hot = jnp.where(entry == places_ref[pl.ds(i, 1), :], 1.0, 0.0).astype(BF16)
            parts.append(dot(jnp.concatenate([high, low], axis=0), hot, ((1,), (1,))))
        return total + sum(parts)

    total = lax.fori_loop(0, WIN, rows, jnp.zeros((64, RELS_PAD), F32))
    return total[0:32] + total[32:64]


COPIES = 224


def piece_of(region):
    rows, cols = region
    return (pl.ds(rows[0], rows[1]), pl.ds(cols[0], cols[1]))


def cut(region, axis, index):
    rows, cols = region
    if axis == "z":
        return ((pl.multiple_of(index * 32, 32), 32), cols)
    width = cols[1] // 4
    return (rows, (pl.multiple_of(cols[0] + index * width, 128), width))


def train_kernel(
    slots_ref, images_ref, cot_hbm, qkv_hbm, proj_hbm, up_hbm, down_hbm, tiny_ref, places_ref, mask_ref,
    order_ref, back_ref, turn_ref,
    y_hbm, dx_hbm, grad_hbm, sums_ref,
    w_ref, x_ref, qkv_ref, o_ref, r_ref, act_ref, slope_ref, g_ref, core_ref, land_a, land_b, land_y, fin_ref,
    rel_ref, gbias_ref, low_ref, turned_ref, du_ref, dqkv_ref, do_ref, dy_ref, cot_ref,
    y_ref, y_land, dx_ref, dx_land, tiny_land, tables_ref, small_ref, qbias_ref, hbias_ref,
    gsmall_ref, ghidden_ref, sums_in, sums_core, sums_own, sums_land,
    send_sem, recv_sem, local_sem, free_sem,
):
    me = here()
    pipe = me["y"] % 2
    copies = Copies(send_sem, recv_sem)
    partner = moved(me, "core", 1)
    peers = {axis: [moved(me, axis, k) for k in (1, 2, 3)] for axis in "yxz"}
    across = [moved(partner, "y", k) for k in (1, 2, 3)]

    def block_at(y):
        return pl.ds(pl.multiple_of(block_index(y, me["core"]) * 128, 128), 128)

    own = block_index(me["y"], me["core"])
    own_rows = block_at(me["y"])
    parts = [
        (qkv_hbm.at[0], QKV0, 3 * D), (proj_hbm.at[0], PROJ0, D), (up_hbm.at[0], UP0, FF),
    ] + [(down_hbm.at[0, k * 128 : (k + 1) * 128], DOWN0 + k * D, D) for k in range(4)]
    locals_in = []
    for n, (src, lo, width) in enumerate(parts):
        local = pltpu.make_async_copy(src, w_ref.at[own_rows, lo : lo + width], local_sem.at[n])
        local.start()
        locals_in.append(local)
    cot_copy = pltpu.make_async_copy(cot_hbm.at[pl.ds(pipe * IMGS, IMGS)], cot_ref, local_sem.at[7])
    cot_copy.start()

    def order_tokens():
        for b in range(IMGS):
            picture = images_ref[slots_ref[pipe * IMGS + b]]
            x_ref[0, b * IMG_ROWS : (b + 1) * IMG_ROWS] = dot(order_ref[0], picture).astype(BF16)
        cot_copy.wait()
        for b in range(IMGS):
            dy_ref[b * IMG_ROWS : (b + 1) * IMG_ROWS] = dot(order_ref[1], cot_ref[b]).astype(BF16)
        for local in locals_in:
            local.wait()

    greet([partner] + across + [place for axis in "yxz" for place in peers[axis]], order_tokens)

    span = PACKED // 3
    width = span // 8

    def weight_piece(y, lo, size):
        start = pl.multiple_of(block_index(y, me["core"]) * 128, 128)
        return w_ref.at[pl.ds(start, 128), pl.ds(lo, size)]

    def quarter(chunk, part, index):
        return pl.multiple_of(chunk * span + part * (span // 2) + index * width, 128), width

    first_base = {}

    def set_off(chunk):
        first_base[chunk] = copies.count
        for k in (1, 2, 3):
            for part, axis in enumerate("xz"):
                piece = weight_piece(me["y"], *quarter(chunk, part, me[axis]))
                copies.start(piece, piece, moved(me, "y", k))

    to_partner = {}
    set_off(0)
    tiny_copies = [
        copies.start(tiny_ref, tiny_land.at[own], place) for place in [partner] + peers["y"] + across
    ]
    for chunk in range(3):
        piece = weight_piece(me["y"], chunk * span, span)
        to_partner["own", chunk] = copies.start(piece, piece, partner)
    tiny_land[own] = tiny_ref[...]

    steps = [2 - pipe, 1 + 2 * pipe, 3 - pipe]
    seconds = {}

    def pass_on(chunk, slots):
        for slot in slots:
            y = (me["y"] - steps[slot] + 4) % 4
            for part, axis in enumerate("xz"):
                piece = weight_piece(y, *quarter(chunk, part, me[axis]))
                index = first_base[chunk] + (steps[slot] - 1) * 2 + part
                pltpu.make_async_remote_copy(
                    src_ref=piece, dst_ref=piece, send_sem=send_sem.at[index],
                    recv_sem=recv_sem.at[index], device_id=device_at(partner), device_id_type=MESH,
                ).wait_recv()
                for j in (1, 3, 2):
                    seconds[chunk, slot, part, j] = copies.start(piece, piece, moved(me, axis, j))

    def hand_over(chunk, slots):
        for slot in slots:
            y = (me["y"] - steps[slot] + 4) % 4
            for part in range(2):
                for j in (1, 3, 2):
                    seconds[chunk, slot, part, j].wait_recv()
            piece = weight_piece(y, chunk * span, span)
            to_partner[slot, chunk] = copies.start(piece, piece, partner)

    def arrived(chunk, slots):
        for slot in slots:
            to_partner[slot, chunk].wait_recv()

    set_off(1)
    pass_on(0, (0, 1))
    set_off(2)
    for copy in tiny_copies:
        copy.wait_recv()
    qbias_ref[...] = jnp.zeros_like(qbias_ref)
    for layer in range(2):
        for shard in range(4):
            rows = tiny_land[layer * 4 + shard]
            small_ref[layer, :, shard * 128 : (shard + 1) * 128] = rows[0:8, 0:128]
            for j in range(4):
                at = shard * 512 + j * 128
                hbias_ref[layer, :, at : at + 128] = rows[8 + j : 9 + j, 0:128]
                head = layer * 16 + shard * 4 + j
                tables_ref[head : head + 1] = rows[16 + j : 17 + j]
        qbias_ref[layer, :, 0:D] = small_ref[layer, 4:5]
        qbias_ref[layer, :, 2 * D : 3 * D] = small_ref[layer, 5:6]
    table_rows_of(tables_ref, places_ref, rel_ref)
    pass_on(1, (0, 1))
    hand_over(0, (0, 1))
    pass_on(2, (0, 1))
    arrived(0, ("own", 0, 1))

    def params(layer):
        return (
            w_ref.at[pl.ds(layer * D, D)], small_ref.at[layer], qbias_ref.at[layer], hbias_ref.at[layer],
            rel_ref.at[pl.ds(layer * 16, 16)], mask_ref.at[layer],
        )

    def saved(layer):
        return tuple(ref.at[layer] for ref in (qkv_ref, o_ref, r_ref, act_ref, slope_ref))

    def in_token_order(layer, value, out, turned):
        for b in range(IMGS):
            own_rows = value[b * IMG_ROWS : (b + 1) * IMG_ROWS]
            out[b] = dot(back_ref[layer], own_rows).astype(BF16)
            if turned is not None:
                turned[b * IMG_ROWS : (b + 1) * IMG_ROWS] = dot(turn_ref[layer], own_rows).astype(BF16)

    def after_attend0():
        hand_over(2, (0, 1))
        for chunk in range(3):
            pass_on(chunk, (2,))

    def before_mlp0():
        arrived(1, ("own", 0, 1))
        arrived(2, ("own", 0, 1))

    def after_qkv1():
        hand_over(1, (2,))
        hand_over(2, (2,))

    def before_mlp1():
        arrived(1, (2,))
        arrived(2, (2,))

    y0 = forward_body(
        params(0), saved(0), x_ref.at[0], low_ref, du_ref, after_qkv=lambda: hand_over(1, (0, 1)),
        after_attend=after_attend0, before_mlp=before_mlp0,
    )
    hand_over(0, (2,))
    in_token_order(0, y0, y_ref.at[0], x_ref.at[1])
    arrived(0, (2,))
    y1 = forward_body(
        params(1), saved(1), x_ref.at[1], low_ref, du_ref, after_qkv=after_qkv1, before_mlp=before_mlp1
    )
    in_token_order(1, y1, y_ref.at[1], None)
    neighbour = {**me, "y": me["y"] + 1 - 2 * pipe}
    y_copy = copies.start(y_ref.at[1 - pipe], y_land, neighbour)
    keep_out = pltpu.make_async_copy(y_ref.at[pipe], y_hbm.at[pl.ds(pipe * IMGS, IMGS)], local_sem.at[0])
    keep_out.start()

    core_copies, sent, regions = {}, {}, {}

    def send_core(layer, streams, begin=0, end=PACKED):
        for t in streams:
            lo, hi = max(STREAMS[t][0], begin), min(STREAMS[t][1], end)
            core_copies.setdefault((layer, t), []).append(
                copies.start(g_ref.at[layer, :, 1 - me["core"], :, lo:hi], core_ref.at[:, :, lo:hi], partner)
            )

    def add_core(layer, streams):
        for t in streams:
            lo, hi, _ = STREAMS[t]
            for copy in core_copies[layer, t]:
                copy.wait_recv()

            def one(n, _, lo=lo, hi=hi):
                half, rows = n // 4, pl.ds(pl.multiple_of((n % 4) * 32, 32), 32)
                mine = (layer, half, me["core"], rows, slice(lo, hi))
                total = g_ref[mine].astype(F32) + core_ref[half, rows, lo:hi].astype(F32)
                g_ref[mine] = total.astype(BF16)
                return 0

            lax.fori_loop(0, 8, one, 0)
            regions[layer, t] = ((0, 128), (lo, hi - lo))

    def send(layer, streams, stage):
        for t in streams:
            axis = STREAMS[t][2][stage]
            land = (land_a, land_b)[stage][t]
            region = regions[layer, t]
            sent[layer, t] = [
                copies.start(
                    g_ref.at[(layer, slice(None), me["core"]) + piece_of(cut(region, axis, (me[axis] + k) % 4))],
                    land.at[layer, k - 1], moved(me, axis, k),
                )
                for k in (1, 3, 2)
            ]
            regions[layer, t] = cut(region, axis, me[axis])

    def add(layer, streams, stage):
        for t in streams:
            for copy in sent[layer, t]:
                copy.wait_recv()
            land = (land_a, land_b)[stage][t]
            (r0, nr), cols = regions[layer, t]
            steps_of = nr // 32

            def one(n, _, land=land, r0=r0, cols=cols, steps_of=steps_of):
                half, row = n // steps_of, pl.multiple_of((n % steps_of) * 32, 32)
                at = (layer, half, me["core"], pl.ds(pl.multiple_of(r0 + row, 32), 32), pl.ds(*cols))
                total = g_ref[at].astype(F32)
                for k in range(3):
                    total = total + land[layer, k, half, pl.ds(row, 32), :].astype(F32)
                g_ref[at] = total.astype(BF16)
                return 0

            lax.fori_loop(0, 2 * steps_of, one, 0)

    def send_y(streams):
        for t in streams:
            piece = piece_of(regions[0, t])
            sent["y", t] = []
            for k in (1, 3, 2):
                to = (me["y"] + k) % 4
                sent["y", t].append(
                    copies.start(
                        g_ref.at[(to % 2, to // 2, me["core"]) + piece], land_y[t].at[k - 1], moved(me, "y", k)
                    )
                )

    def add_y(streams):
        for t in streams:
            for copy in sent["y", t]:
                copy.wait_recv()
            piece = piece_of(regions[0, t])
            total = g_ref[(pipe, me["y"] // 2, me["core"]) + piece].astype(F32)
            for k in range(3):
                total = total + land_y[t][k].astype(F32)
            fin_ref[piece] = total.astype(BF16)

    def spread(streams, level):
        for t in streams:
            if level == 1:
                for copy in sent["fin", t]:
                    copy.wait_recv()
            lo, hi, order = STREAMS[t]
            part = (hi - lo) // 4
            rows = pl.ds(pl.multiple_of(me["z"] * 32, 32), 32)
            cols = pl.ds(pl.multiple_of(lo + me["x"] * part, 128), part)
            if level == 1:
                if order[0] == "x":
                    cols = pl.ds(lo, hi - lo)
                else:
                    rows = pl.ds(0, 128)
            piece = fin_ref.at[rows, cols]
            sent["fin", t] = [copies.start(piece, piece, moved(me, order[level], k)) for k in (1, 3, 2)]

    late = LATE
    early = tuple(t for t in range(len(STREAMS)) if t not in late)

    def results(layer):
        return (g_ref.at[layer], gsmall_ref.at[layer], ghidden_ref.at[layer], gbias_ref.at[pl.ds(layer * 16, 16)])

    scratch = (low_ref, turned_ref, du_ref, dqkv_ref, do_ref)

    def after_mlp1():
        send_core(1, (1,))
        send_core(1, (0,), begin=UP0)

    def after_proj1():
        send_core(1, (0,), end=UP0)
        add_core(1, (1,))
        send(1, (1,), 0)

    def before_attend1():
        add_core(1, (0,))
        send(1, (0,), 0)

    dx1 = backward_body(
        params(1), saved(1), x_ref.at[1], dy_ref, results(1), scratch,
        after_mlp=after_mlp1, after_proj=after_proj1,
        before_attend=before_attend1, after_weights=lambda: send_core(1, late),
    )
    in_token_order(1, dx1, dx_ref.at[1], dy_ref)
    add_core(1, late)
    pl.semaphore_signal(free_sem, inc=1, device_id=device_at(partner), device_id_type=MESH)
    send(1, late, 0)

    def in_mlp0():
        add(1, (1, 0), 0)
        send(1, (1, 0), 1)

    def after_mlp0():
        pl.semaphore_wait(free_sem, 1)
        send_core(0, (1,))
        send_core(0, (0,), begin=UP0)

    def after_proj0():
        send_core(0, (0,), end=UP0)
        add_core(0, (1,))
        send(0, (1,), 0)

    def before_attend0():
        add_core(0, (0,))
        send(0, (0,), 0)

    def after_attend0():
        add(1, early, 1)
        add(1, late, 0)
        send(1, late, 1)

    def after_weights0():
        send_core(0, late)
        add(0, (1,), 0)
        send(0, (1,), 1)

    dx0 = backward_body(
        params(0), saved(0), x_ref.at[0], dy_ref, results(0), scratch,
        in_mlp=in_mlp0, after_mlp=after_mlp0, after_proj=after_proj0,
        before_attend=before_attend0, after_attend=after_attend0, after_weights=after_weights0,
    )
    add(0, (0,), 0)
    send(0, (0,), 1)
    add_core(0, late)
    send(0, late, 0)
    in_token_order(0, dx0, dx_ref.at[0], None)
    dx_copy = copies.start(dx_ref.at[1 - pipe], dx_land, neighbour)
    dx_keep = pltpu.make_async_copy(dx_ref.at[pipe], dx_hbm.at[pl.ds(pipe * IMGS, IMGS)], local_sem.at[1])
    dx_keep.start()

    add(0, (1,), 1)
    send_y((1,))
    gtable = table_sums(gbias_ref, places_ref)
    for layer in range(2):
        for shard in range(4):
            half, core = shard // 2, shard % 2
            y = half * 2 + layer
            sums_in[core, y] = jnp.zeros((SMALL_ROWS, RELS_PAD), F32)
            sums_in[core, y, 0:8, 0:128] = gsmall_ref[layer, :, shard * 128 : (shard + 1) * 128]
            for j in range(4):
                at = shard * 512 + j * 128
                sums_in[core, y, 8 + j : 9 + j, 0:128] = ghidden_ref[layer, :, at : at + 128]
            sums_in[core, y, 16:20] = gtable[layer * 16 + shard * 4 : layer * 16 + shard * 4 + 4]
    small_copy = copies.start(sums_in.at[1 - me["core"]], sums_core, partner)
    add(0, late, 0)
    send(0, late, 1)
    add(0, (0,), 1)
    send_y((0,))
    add(1, late, 1)
    add_y((1,))
    spread((1,), 0)
    small_copy.wait_recv()
    sums_own[0] = sums_in[me["core"]] + sums_core[...]
    small_sent = [
        copies.start(sums_own.at[0, (me["y"] + k) % 4], sums_land.at[0, k - 1], moved(me, "y", k))
        for k in (1, 3, 2)
    ]

    def add_small(stage):
        for copy in small_sent:
            copy.wait_recv()
        start = sums_own[0, me["y"]] if stage == 0 else sums_own[stage, 0]
        return start + sums_land[stage, 0] + sums_land[stage, 1] + sums_land[stage, 2]

    add_y((0,))
    spread((0,), 0)
    add(0, late, 1)
    send_y(late)
    for stage, axis in enumerate("xz", 1):
        sums_own[stage, 0] = add_small(stage - 1)
        small_sent = [
            copies.start(sums_own.at[stage, 0], sums_land.at[stage, k - 1], moved(me, axis, k))
            for k in (1, 3, 2)
        ]
        if stage == 1:
            spread(early, 1)
            add_y(late)
            spread(late, 0)
    spread(late, 1)
    sums_ref[...] = add_small(2)
    outs = []
    y_copy.wait_recv()
    dx_copy.wait_recv()
    for n, (src, dst) in enumerate(((y_land, y_hbm), (dx_land, dx_hbm)), 2):
        out = pltpu.make_async_copy(src, dst.at[pl.ds((1 - pipe) * IMGS, IMGS)], local_sem.at[n])
        out.start()
        outs.append(out)
    for t in early + late:
        for copy in sent["fin", t]:
            copy.wait_recv()
    grad_out = pltpu.make_async_copy(fin_ref, grad_hbm, local_sem.at[4])
    grad_out.start()
    for copy in [keep_out, dx_keep, grad_out] + outs:
        copy.wait()
    copies.finish()


def land_shapes(stage):
    shapes = []
    for lo, hi, order in STREAMS:
        done = order[: stage + 1]
        shape = (2, 3, 2, 32 if "z" in done else 128, (hi - lo) // (4 if "x" in done else 1))
        shapes.append(pltpu.VMEM(shape, BF16))
    return tuple(shapes)


def train(slots, images, cotangent, qkv, proj, up, down, tiny, places, mask, order, back, turn):
    anywhere = pl.BlockSpec(memory_space=pl.ANY)
    vmem = pl.BlockSpec(memory_space=pltpu.VMEM)
    tokens = (2 * IMGS, OUT_ROWS, D)
    half = (IMGS, OUT_ROWS, D)
    piece = (SMALL_ROWS, RELS_PAD)
    low = pltpu.VMEM((ROWS, D), BF16)
    return pl.pallas_call(
        train_kernel,
        out_shape=[
            jax.ShapeDtypeStruct(tokens, BF16), jax.ShapeDtypeStruct(tokens, BF16),
            jax.ShapeDtypeStruct((128, PACKED), BF16), jax.ShapeDtypeStruct(piece, F32),
        ],
        in_specs=[pl.BlockSpec(memory_space=pltpu.SMEM), vmem] + [anywhere] * 5 + [vmem] * 6,
        out_specs=[anywhere] * 3 + [vmem],
        scratch_shapes=[
            pltpu.VMEM((2 * D, PACKED), BF16),
            pltpu.VMEM((2, ROWS, D), BF16),
            pltpu.VMEM((2, KROWS, 3 * D), BF16),
            pltpu.VMEM((2, ROWS, D), BF16),
            pltpu.VMEM((2, ROWS, D), F32),
            pltpu.VMEM((2, ROWS, FF), BF16),
            pltpu.VMEM((2, ROWS, FF), BF16),
            pltpu.VMEM((2, 2, 2, 128, PACKED), BF16),
            pltpu.VMEM((2, 128, PACKED), BF16),
            land_shapes(0), land_shapes(1),
            tuple(pltpu.VMEM((3, 32, (hi - lo) // 4), BF16) for lo, hi, _ in STREAMS),
            pltpu.VMEM((128, PACKED), BF16),
            pltpu.VMEM((32, PAIR, KEYS), F32),
            pltpu.VMEM((32, PAIR, KEYS), F32),
            low,
            pltpu.VMEM((D, ROWS), BF16),
            pltpu.VMEM((ROWS, D), F32),
            pltpu.VMEM((ROWS, 3 * D), BF16),
            low,
            low,
            pltpu.VMEM((IMGS, TOK, D), BF16),
            pltpu.VMEM((2,) + half, BF16),
            pltpu.VMEM(half, BF16),
            pltpu.VMEM((2,) + half, BF16),
            pltpu.VMEM(half, BF16),
            pltpu.VMEM((8, TINY_ROWS, RELS_PAD), F32),
            pltpu.VMEM((32, RELS_PAD), F32),
            pltpu.VMEM((2, 8, D), F32),
            pltpu.VMEM((2, 1, 3 * D), F32),
            pltpu.VMEM((2, 1, FF), F32),
            pltpu.VMEM((2, 8, D), F32),
            pltpu.VMEM((2, 1, FF), F32),
            pltpu.VMEM((2, 4) + piece, F32),
            pltpu.VMEM((4,) + piece, F32),
            pltpu.VMEM((3, 4) + piece, F32),
            pltpu.VMEM((3, 3) + piece, F32),
            pltpu.SemaphoreType.DMA((COPIES,)),
            pltpu.SemaphoreType.DMA((COPIES,)),
            pltpu.SemaphoreType.DMA((8,)),
            pltpu.SemaphoreType.REGULAR,
        ],
        compiler_params=pltpu.CompilerParams(
            collective_id=1, has_side_effects=True, vmem_limit_bytes=VMEM_LIMIT
        ),
        cost_estimate=pl.CostEstimate(
            flops=12 * ROWS * D * PACKED, bytes_accessed=16 << 20, transcendentals=6 * ROWS * FF
        ),
        name="train_layers",
    )(slots, images, cotangent, qkv, proj, up, down, tiny, places, mask, order, back, turn)


def block_pair(blocks, fill):
    lead = blocks.shape[:-3]
    none = [(0, 0)] * len(lead)
    pad_rows = [(0, WPAD - WTOK)]
    first = jnp.pad(blocks[..., 0, :, :], none + pad_rows + [(0, KEYS - WTOK)], constant_values=fill)
    second = jnp.pad(
        blocks[..., 1, :, :], none + pad_rows + [(WPAD, KEYS - WTOK - WPAD)], constant_values=fill
    )
    return jnp.concatenate([first, second], axis=-2)


def inside_blocks():
    rows, cols = np.arange(PAIR)[:, None] // WPAD, np.arange(KEYS)[None, :]
    return (cols // WPAD == rows) & (cols % WPAD < WTOK) & (cols < PAIR)


def on_device(
    images, cotangent, micro_order, region_ids, rel_index, qkv_weight, proj_weight, up_weight,
    down_weight, bias_table, norm_gains, offsets, hidden_bias,
):
    first_section = lax.axis_index("pipe") == 0
    table_rows = bias_table.shape[1]

    def lanes(block, rows):
        return jnp.pad(
            block.astype(F32), ((0, rows - block.shape[0]), (0, RELS_PAD - block.shape[1]))
        )

    tiny = jnp.concatenate(
        [
            lanes(jnp.concatenate([norm_gains[0], offsets[0]]), 8),
            lanes(hidden_bias[0].reshape(4, 128), 8),
            lanes(bias_table[0].T, 8),
        ]
    )
    places = jnp.pad(rel_index, ((0, WPAD - WTOK), (0, KEYS - WTOK)), constant_values=-1)
    regions = region_ids.reshape(2, WIN, 2, WIN).transpose(0, 2, 1, 3).reshape(2, 2, WTOK)
    regions = jnp.pad(regions, ((0, 0), (0, 0), (0, WPAD - WTOK))).reshape(2, PAIR)
    queries = regions[:, :, None]
    keys = jnp.pad(regions, ((0, 0), (0, KEYS - PAIR)))[:, None, :]
    inside = inside_blocks()
    mask0 = np.broadcast_to(np.where(inside, 0.0, BLOCKED), (2, PAIR, KEYS)).astype(np.float32)
    mask1 = jnp.where(inside[None], jnp.where(queries == keys, 0.0, -1e9), BLOCKED).astype(F32)
    mask = jnp.stack([jnp.asarray(mask0), mask1])
    order = jnp.asarray(np.stack([order_matrix(0), order_matrix(SHIFT)]), BF16)
    back = jnp.asarray(np.stack([back_matrix(0), back_matrix(SHIFT)]), BF16)
    turn = jnp.asarray(np.stack([turn_matrix(0, SHIFT), turn_matrix(SHIFT, 0)]), BF16)
    slot_order = micro_order[0]

    layer_out, dx_slots, share, sums = train(
        slot_order, images, cotangent, qkv_weight, proj_weight, up_weight, down_weight, tiny, places,
        mask, order, back, turn,
    )
    slots = jnp.arange(2 * IMGS, dtype=jnp.int32)
    inverse = jnp.sum(jnp.where(slot_order[:, None] == slots[None, :], slots[:, None], 0), axis=0)
    picks = jnp.where(first_section, inverse, slots)
    input_grad = jnp.take(dx_slots[:, :TOK], picks, axis=0, mode="clip").astype(F32)
    down = jnp.concatenate(
        [share[:, DOWN0 + k * D : DOWN0 + (k + 1) * D] for k in range(4)], axis=0
    )
    return (
        layer_out[None, :, :TOK],
        input_grad[None],
        share[None, :, QKV0:PROJ0].astype(F32),
        share[None, :, PROJ0:UP0].astype(F32),
        share[None, :, UP0:DOWN0].astype(F32),
        down[None].astype(F32),
        sums[16:20, :table_rows].T[None],
        sums[None, 0:2, 0:128],
        sums[None, 2:8, 0:128],
        sums[8:12, 0:128].reshape(1, D),
    )


def solution(mesh):
    rows = P(("shard", "rep"), None, None)
    split = P("pipe", "shard", None)
    lanes = P("pipe", None, "shard")
    return jax.shard_map(
        on_device,
        mesh=mesh,
        in_specs=(
            rows, rows, P(("shard", "rep"), None), P(), P(),
            split, split, split, split, lanes, lanes, lanes, P("pipe", "shard"),
        ),
        out_specs=(
            P("pipe", ("shard", "rep"), None, None), P("pipe", ("shard", "rep"), None, None),
            split, split, split, split, lanes, lanes, lanes, P("pipe", "shard"),
        ),
        check_vma=False,
    )
```
